32 devices in a mesh: ctx: 16 (over z, x, core), fsdp: 2 (over y).
Axes of the slice: x: 2, y: 2, z: 4, core: 2. Of those that a mesh axis runs over, the one named last changes fastest.
Arguments:
- tokens: bfloat16 [8192, 1536], P(('ctx', 'fsdp')), may hold values from -6 to 6
- cotangent: bfloat16 [8192, 1536], P(('ctx', 'fsdp')), may hold values from -6 to 6
- lengths: int32 [2, 4], P('fsdp'), may hold values from 1 to 2048, 4096 in all within a row
- block_of: int32 [2, 16], P('fsdp'), may hold values from 0 to 15, each once within a row
- gain_attn: bfloat16 [1536], P('fsdp'), may hold values from 0.5 to 1.5
- w_query: bfloat16 [1536, 1536], P('fsdp'), may hold values from -0.3125 to 0.3125
- w_keyval: bfloat16 [1536, 256], P('fsdp'), may hold values from -0.15625 to 0.15625
- w_out: bfloat16 [1536, 1536], P('fsdp'), may hold values from -1.25 to 1.25
- gain_mlp: bfloat16 [1536], P('fsdp'), may hold values from 0.5 to 1.5
- w_gateup: bfloat16 [1536, 9216], P('fsdp'), may hold values from -0.15625 to 0.15625
- w_down: bfloat16 [4608, 1536], P('fsdp'), may hold values from -0.1875 to 0.1875
Outputs:
- block_output: bfloat16 [8192, 1536], P(('ctx', 'fsdp'))
- grad_tokens: float32 [8192, 1536], P(('ctx', 'fsdp'))
- grad_gain_attn: float32 [1536], P('fsdp')
- grad_query: float32 [1536, 1536], P('fsdp')
- grad_keyval: float32 [1536, 256], P('fsdp')
- grad_out: float32 [1536, 1536], P('fsdp')
- grad_gain_mlp: float32 [1536], P('fsdp')
- grad_gateup: float32 [1536, 9216], P('fsdp')
- grad_down: float32 [4608, 1536], P('fsdp')
The draws below stay inside these ranges and needn't reach their ends.
Inputs may be any that keep to these rules, and one draw needn't show every extreme that they name: Each row holds the 4 lengths of one group, summing to 4096. `block_of`: each row is a permutation of the 16 pack blocks of one group.
All inputs are finite; a program needn't handle non-finite values.
Results may differ from the reference program's by a relative error of at most 0.024.
Values may be sent and summed in bfloat16 or wider, within the bound.
No kernel may reach another device: no remote copies, remote signals or barrier semaphores. Data moves between devices by JAX's collectives and lax.ppermute only.
A program may use at most 320 MiB of HBM per device.

```python
import math
import jax
import jax.numpy as jnp
import numpy as np
from jax import lax

D = 1536
H = 12
HD = 128
FF = 4608
WINDOW = 1024
TOK_DEV = 256
SEQS = 4
GROUP = 4096
TOKENS = 8192
N_CTX = 16
N_FSDP = 2


def shard_levels(rng, extent, pieces, low, high):
    loudness, own = 1.0, jax.random.fold_in(rng, 6)
    for dim, parts in pieces:
        draws = jnp.exp(jax.random.uniform(jax.random.fold_in(own, dim), (parts,), jnp.float32, low / len(pieces), high / len(pieces)))
        loudness = loudness * jnp.repeat(draws, extent[dim] // parts).reshape([-1 if axis == dim else 1 for axis in range(len(extent))])
    return loudness


def split_up(amount, total, bound, lean):
    loads = [(1 << 20) // math.isqrt(standing ** lean) + 1 for standing in range(2, amount + 1)]
    surplus, holding = total - bound - (amount - 1), [1] * (amount - 1)
    while surplus > 0:
        candidates = [i for i in range(amount - 1) if holding[i] < bound]
        whole, budget = sum([loads[i] for i in candidates]), surplus
        for i in candidates:
            addition = min(bound - holding[i], max(1, budget * loads[i] // whole), surplus)
            holding[i] = holding[i] + addition
            surplus = surplus - addition
    return np.array([bound] + holding)


def uneven_parts(rng, number_of, total, most, skew):
    if number_of == 2:
        one = jax.random.randint(rng, (), max(1, total - most), min(most, total - 1) + 1)
        return jnp.stack([one, total - one])
    sizes = jnp.asarray(split_up(number_of, total, most, skew), jnp.int32)
    twos = (number_of - 1) // 2
    donor, receiver = sizes[1:1 + 2 * twos:2], sizes[2:2 + 2 * twos:2]
    room = jnp.minimum(donor - 1, most - receiver)
    moved = jax.random.randint(jax.random.fold_in(rng, 1), (twos,), 0, 1 << 20) % (room + 1)
    sizes = sizes.at[1:1 + 2 * twos:2].set(donor - moved).at[2:2 + 2 * twos:2].set(receiver + moved)
    return sizes[jax.random.permutation(jax.random.fold_in(rng, 2), number_of)]


def gaussian(stream_key, extent, scale, bound, cuts=(), kind=jnp.bfloat16):
    entries = jax.random.normal(stream_key, extent, jnp.float32) * scale
    if len(cuts) > 0:
        entries = shard_levels(stream_key, extent, cuts, -0.22, 0.18) * entries
    return jnp.clip(entries, min=-bound, max=bound).astype(kind)


def setup_inputs(seed: int = 0) -> dict:
    key_list = jax.random.split(jax.random.key(seed), 12)
    tokens = gaussian(key_list[0], (TOKENS, D), 1.0, 6.0, ((0, 32),))
    cotangent = gaussian(key_list[1], (TOKENS, D), 1.0, 6.0, ((0, 32),))
    lengths = jax.vmap(lambda own: uneven_parts(own, SEQS, GROUP, GROUP // 2, 2))(jax.random.split(key_list[2], N_FSDP)).reshape((N_FSDP, SEQS)).astype(jnp.int32)
    block_of = jax.vmap(lambda own: jax.random.permutation(own, N_CTX))(jax.random.split(key_list[3], N_FSDP)).reshape((N_FSDP, N_CTX)).astype(jnp.int32)
    gain_attn = jnp.clip(1.0 + 0.1 * jax.random.normal(key_list[4], (D,), jnp.float32), 0.5, 1.5).astype(jnp.bfloat16)
    w_query = gaussian(key_list[5], (D, H * HD), (D // 4) ** -0.5, 0.3125, ((0, 2),))
    w_keyval = gaussian(key_list[6], (D, 2 * HD), D ** -0.5, 0.15625, ((0, 2),))
    w_out = gaussian(key_list[7], (H * HD, D), (H * HD // 64) ** -0.5, 1.25, ((0, 2),))
    gain_mlp = jnp.clip(1.0 + 0.1 * jax.random.normal(key_list[8], (D,), jnp.float32), 0.5, 1.5).astype(jnp.bfloat16)
    w_gateup = gaussian(key_list[9], (D, 2 * FF), D ** -0.5, 0.15625, ((0, 2),))
    w_down = gaussian(key_list[10], (FF, D), (FF // 4) ** -0.5, 0.1875, ((0, 2),))
    return {"tokens": tokens, "cotangent": cotangent, "lengths": lengths, "block_of": block_of, "gain_attn": gain_attn, "w_query": w_query, "w_keyval": w_keyval, "w_out": w_out, "gain_mlp": gain_mlp, "w_gateup": w_gateup, "w_down": w_down}


@jax.custom_vjp
def low(v):
    return lax.optimization_barrier(v.astype(jnp.bfloat16)).astype(jnp.float32)

@jax.custom_vjp
def low_back(v):
    return v

def low_keep(v):
    return (low(v), None)

def low_pass(kept, grad):
    return (grad,)

def back_keep(v):
    return (v, None)

def back_low(kept, grad):
    return (low(grad),)
low.defvjp(low_keep, low_pass)
low_back.defvjp(back_keep, back_low)
EPSILON = 1e-06
PRECISE = lax.Precision.HIGHEST

def tables(places, width):
    half_width = width // 2
    frequency = jnp.exp(jnp.arange(half_width, dtype=jnp.float32) * (-2.0 * math.log(10000.0) / width))
    angles = places.astype(jnp.float32)[:, None] * frequency[None, :]
    return (jnp.cos(angles), jnp.sin(angles))

def rotate(values, cosine, sine_table):
    half_width = values.shape[-1] // 2
    former = values[..., :half_width]
    latter = values[..., half_width:]
    return jnp.concatenate([former * cosine - latter * sine_table, latter * cosine + former * sine_table], axis=-1)

def rms_norm(values, gain):
    factor = lax.rsqrt(lax.optimization_barrier(jnp.mean(values * values, axis=-1, keepdims=True)) + EPSILON)
    return values * factor * gain

def segment_info(places, seq_lengths):
    seq_ends = jnp.cumsum(seq_lengths).astype(jnp.int32)
    passed = places[:, None] >= seq_ends[None, :]
    segment = lax.optimization_barrier(jnp.sum(passed.astype(jnp.int32), axis=1)).astype(jnp.int32)
    seq_start = lax.optimization_barrier(jnp.sum(jnp.where(passed, seq_lengths[None, :], 0), axis=1)).astype(jnp.int32)
    return (segment, (places - seq_start).astype(jnp.int32))

def block_layer(inputs, gain_attn, w_query, w_keyval, w_out, gain_mlp, w_gateup, w_down, segment, position):
    normed = low(rms_norm(inputs, gain_attn))
    cosine, sine_table = tables(position, HD)
    queries = jnp.dot(normed, w_query, precision=PRECISE).reshape(GROUP, H, HD)
    queries = low(rotate(low_back(queries), cosine[:, None, :], sine_table[:, None, :]) * HD ** (-0.5))
    keyval = low_back(jnp.dot(normed, w_keyval, precision=PRECISE))
    keyval = low(jnp.concatenate([rotate(keyval[:, :HD], cosine, sine_table), keyval[:, HD:]], axis=1))
    padded_kv = jnp.concatenate([jnp.zeros((WINDOW, 2 * HD), jnp.float32), keyval], axis=0)
    padded_seg = jnp.concatenate([jnp.full((WINDOW,), -1, jnp.int32), segment], axis=0)
    distance = jnp.arange(TOK_DEV, dtype=jnp.int32)[:, None] + WINDOW - jnp.arange(WINDOW + TOK_DEV, dtype=jnp.int32)[None, :]

    def attend(block_index):
        start_row = (block_index * TOK_DEV).astype(jnp.int32)
        query_blk = lax.dynamic_slice_in_dim(queries, start_row, TOK_DEV, 0)
        window_kv = lax.dynamic_slice_in_dim(padded_kv, start_row, WINDOW + TOK_DEV, 0)
        query_seg = lax.dynamic_slice_in_dim(segment, start_row, TOK_DEV, 0)
        key_seg = lax.dynamic_slice_in_dim(padded_seg, start_row, WINDOW + TOK_DEV, 0)
        allowed = (query_seg[:, None] == key_seg[None, :]) & (distance >= 0) & (distance < WINDOW)
        scores = low_back(jnp.einsum('qhd,kd->qhk', query_blk, window_kv[:, :HD], precision=PRECISE))
        scores = jnp.where(allowed[:, None, :], scores, -1e+30)
        row_max = lax.optimization_barrier(jnp.max(scores, axis=-1, keepdims=True))
        weights = jnp.exp(scores - row_max)
        weights = weights / lax.optimization_barrier(jnp.sum(weights, axis=-1, keepdims=True))
        return jnp.einsum('qhk,kd->qhd', low(weights), window_kv[:, HD:], precision=PRECISE)
    attended = lax.map(jax.checkpoint(attend), jnp.arange(GROUP // TOK_DEV, dtype=jnp.int32))
    attended = low(low_back(attended.reshape(GROUP, H * HD)))
    hidden = inputs + low_back(jnp.dot(attended, w_out, precision=PRECISE))
    normed2 = low(rms_norm(hidden, gain_mlp))
    both_parts = low_back(jnp.dot(normed2, w_gateup, precision=PRECISE))
    inner_act = low(jax.nn.gelu(both_parts[:, :FF], approximate=True) * both_parts[:, FF:])
    return hidden + low_back(jnp.dot(inner_act, w_down, precision=PRECISE))

def reference(tokens, cotangent, lengths, block_of, gain_attn, w_query, w_keyval, w_out, gain_mlp, w_gateup, w_down):
    params = (gain_attn.astype(jnp.float32), w_query.astype(jnp.float32), w_keyval.astype(jnp.float32), w_out.astype(jnp.float32), gain_mlp.astype(jnp.float32), w_gateup.astype(jnp.float32), w_down.astype(jnp.float32))
    inputs = jnp.transpose(tokens.astype(jnp.float32).reshape(N_CTX, N_FSDP, TOK_DEV, D), (1, 0, 2, 3))
    upstream = jnp.transpose(cotangent.astype(jnp.float32).reshape(N_CTX, N_FSDP, TOK_DEV, D), (1, 0, 2, 3))
    places = jnp.arange(GROUP, dtype=jnp.int32)

    def one_group(summed, packet):
        local_in, local_ct, seq_lengths, order = packet
        packed_in = jnp.zeros_like(local_in).at[order].set(local_in).reshape(GROUP, D)
        packed_ct = jnp.zeros_like(local_ct).at[order].set(local_ct).reshape(GROUP, D)
        segment, position = segment_info(places, seq_lengths)

        def apply_layer(values, *weights):
            return block_layer(values, *weights, segment, position)
        output, pullback = jax.vjp(apply_layer, packed_in, *params)
        grads = pullback(packed_ct)
        output = output.reshape(N_CTX, TOK_DEV, D)[order]
        back_in = grads[0].reshape(N_CTX, TOK_DEV, D)[order]
        summed = jax.tree.map(jnp.add, summed, tuple(grads[1:]))
        return (summed, (output, back_in))
    initial = tuple((jnp.zeros_like(param) for param in params))
    summed, stacked = lax.scan(one_group, initial, (inputs, upstream, lengths, block_of))
    outputs = jnp.transpose(stacked[0], (1, 0, 2, 3)).reshape(TOKENS, D)
    back_all = jnp.transpose(stacked[1], (1, 0, 2, 3)).reshape(TOKENS, D)
    return (outputs.astype(jnp.bfloat16), back_all, summed[0], summed[1], summed[2], summed[3], summed[4], summed[5], summed[6])
```

```python
import math

import jax
import jax.numpy as jnp
from jax import lax
from jax.sharding import Mesh
from jax.sharding import PartitionSpec as P

H = 12
HD = 128
FF = 4608
WINDOW = 1024
EPSILON = 1e-06
BF = jnp.bfloat16
F32 = jnp.float32


def tables(places, width):
    half_width = width // 2
    frequency = jnp.exp(
        jnp.arange(half_width, dtype=jnp.float32) * (-2.0 * math.log(10000.0) / width)
    )
    angles = places.astype(jnp.float32)[:, None] * frequency[None, :]
    return (jnp.cos(angles), jnp.sin(angles))


def rotate(values, cosine, sine_table):
    half_width = values.shape[-1] // 2
    former = values[..., :half_width]
    latter = values[..., half_width:]
    return jnp.concatenate(
        [former * cosine - latter * sine_table, latter * cosine + former * sine_table], axis=-1
    )


def rms_factor(values):
    return lax.rsqrt(jnp.mean(values * values, axis=-1, keepdims=True) + EPSILON)


def norm_back(grad_normed, values, factor, gain):
    scaled = grad_normed * gain
    return factor * scaled - values * factor**3 * jnp.mean(scaled * values, axis=-1, keepdims=True)


def segment_info(places, seq_lengths):
    seq_ends = jnp.cumsum(seq_lengths)
    passed = places[:, None] >= seq_ends[None, :]
    segment = jnp.sum(passed.astype(jnp.int32), axis=1)
    seq_start = jnp.sum(jnp.where(passed, seq_lengths[None, :], 0), axis=1)
    return (segment, places - seq_start)


def masked_scores(heads_first, keys, allowed):
    scores = jnp.einsum("hqd,kd->hqk", heads_first, keys, preferred_element_type=jnp.float32)
    return jnp.where(allowed[None, :, :], scores, -1e30)


def dot(a, b):
    return jnp.dot(a, b, preferred_element_type=F32)


def dot_t(a, b):
    return lax.dot_general(a, b, (((1,), (1,)), ((), ())), preferred_element_type=F32)


def t_dot(a, b):
    return lax.dot_general(a, b, (((0,), (0,)), ((), ())), preferred_element_type=F32)


def bits_of(axis):
    count = lax.axis_size(axis).bit_length() - 1
    return [(axis, k) for k in reversed(range(count))]


def own_bit(bit):
    return (lax.axis_index(bit[0]) >> bit[1]) & 1


def flip(array, bit):
    axis, k = bit
    return lax.ppermute(array, axis, [(i, i ^ (1 << k)) for i in range(lax.axis_size(axis))])


def pick(array, index, dim):
    return lax.dynamic_index_in_dim(array, index, dim, keepdims=False)


def gather_rel(array, bits):
    held = array[None]
    for bit in bits:
        held = jnp.concatenate([held, flip(held, bit)], axis=0)
    return held


def scatter_rel(array, bits):
    for bit in reversed(bits):
        half = array.shape[0] // 2
        array = (array[:half].astype(F32) + flip(array[half:].astype(BF), bit).astype(F32)).astype(BF)
    return array[0]


def join(own, other, bit, dim):
    low = jnp.concatenate([own, other], axis=dim)
    high = jnp.concatenate([other, own], axis=dim)
    return jnp.where(own_bit(bit) == 0, low, high)


def gather_abs(array, bits, dim):
    for bit in bits:
        array = join(array, flip(array, bit), bit, dim)
    return array


def scatter_abs(array, bits, dim=0):
    rows = array.shape[dim]
    lead = array.shape[:dim]
    tail = array.shape[dim + 1 :]
    count = len(bits)
    array = array.reshape(lead + (2,) * count + (rows >> count,) + tail)
    for place in reversed(range(count)):
        bit = bits[place]
        mine = own_bit(bit)
        sent = pick(array, 1 - mine, dim + place)
        kept = pick(array, mine, dim + place)
        array = (kept.astype(F32) + flip(sent, bit).astype(F32)).astype(BF)
    return array


def body(
    tokens,
    cotangent,
    lengths,
    block_of,
    gain_attn,
    w_query,
    w_keyval,
    w_out,
    gain_mlp,
    w_gateup,
    w_down,
):
    tok_rows, width = tokens.shape
    y_count, z_count = lax.axis_size("y"), lax.axis_size("z")
    ctx_count = 4 * z_count
    x_bit, c_bit = ("x", 0), ("c", 0)
    y_bits, z_bits = bits_of("y"), bits_of("z")
    up_z = list(reversed(z_bits))
    x_at, c_at, y_at = lax.axis_index("x"), lax.axis_index("c"), lax.axis_index("y")
    own_index = (lax.axis_index("z") * 2 + x_at) * 2 + c_at

    def whole_weight(shard, share):
        piece = shard
        rows = shard.shape[0]
        if share:
            for bit in share:
                rows = rows // 2
                piece = lax.dynamic_slice_in_dim(piece, own_bit(bit) * rows, rows, 0)
        others = gather_rel(piece, y_bits)
        parts = []
        for r in range(1, y_count):
            part = others[r]
            for bit in reversed(share):
                part = join(part, flip(part, bit), bit, 0)
            parts.append(part)
        if y_count == 2:
            return join(shard, parts[0], y_bits[0], 0)
        rel = jnp.stack([shard] + parts)
        order = jnp.arange(y_count, dtype=jnp.int32) ^ y_at
        return jnp.take(rel, order, axis=0).reshape((y_count * shard.shape[0],) + shard.shape[1:])

    gains = whole_weight(jnp.stack([gain_attn, gain_mlp], axis=1), [])
    gain_one = gains[:, 0].astype(F32)
    gain_two = gains[:, 1].astype(F32)
    w_kv = whole_weight(w_keyval, [c_bit])
    w_q = whole_weight(w_query, [c_bit, x_bit])
    w_o = whole_weight(w_out, [c_bit, x_bit])

    units = FF // (2 * y_count)
    gu = w_gateup.reshape(w_gateup.shape[0], 2, y_count, 2, units)
    wide = gu.shape[0]

    def unit_columns(rows, part, y_index):
        return lax.dynamic_slice_in_dim(
            rows, part * FF + (y_index * 2 + x_at) * units, units, 1
        )

    rows_half = wide // 2
    half_rows = lax.dynamic_slice_in_dim(w_gateup, c_at * rows_half, rows_half, 0)
    gu_parts = {}
    for r in range(1, y_count):
        piece = jnp.concatenate([unit_columns(half_rows, part, y_at ^ r) for part in (0, 1)], axis=1)
        piece = lax.ppermute(piece, "y", [(i, i ^ r) for i in range(y_count)])
        gu_parts[r] = join(piece, flip(piece, c_bit), c_bit, 0)
    gu_parts[0] = jnp.concatenate([unit_columns(w_gateup, part, y_at) for part in (0, 1)], axis=1)
    if y_count == 2:
        w_gu = join(gu_parts[0], gu_parts[1], y_bits[0], 0)
    else:
        order = jnp.arange(y_count, dtype=jnp.int32) ^ y_at
        w_gu = jnp.take(jnp.stack([gu_parts[r] for r in range(y_count)]), order, axis=0)
        w_gu = w_gu.reshape(width, 2 * units)
    w_dn = lax.dynamic_slice_in_dim(w_down, x_at * units, units, 0)

    half_tok = tok_rows // 2
    group = 2 * y_count
    order_a = y_bits + [x_bit]
    order_b = [x_bit] + y_bits

    def group_gather(array):
        first = gather_rel(array[:half_tok], order_a).reshape(group * half_tok, -1)
        second = gather_rel(array[half_tok:], order_b).reshape(group * half_tok, -1)
        return jnp.concatenate([first, second], axis=0)

    def group_scatter(array):
        array = array.astype(BF).reshape(2, group, half_tok, -1)
        return jnp.concatenate(
            [scatter_rel(array[0], order_a), scatter_rel(array[1], order_b)], axis=0
        ).astype(F32)

    cot_all = group_gather(cotangent)

    device_ids = jnp.arange(ctx_count, dtype=jnp.int32)
    block_row = block_of[0]
    own_block = jnp.sum(jnp.where(device_ids == own_index, block_row, 0))
    own_start = own_block * tok_rows
    owners = jnp.sum(
        jnp.where(block_row[None, :] == device_ids[:, None], device_ids[None, :], 0), axis=1
    )
    seq_lengths = lengths[0]
    query_places = own_start + jnp.arange(tok_rows, dtype=jnp.int32)
    key_places = own_start - WINDOW + jnp.arange(WINDOW + tok_rows, dtype=jnp.int32)
    query_segment, query_position = segment_info(query_places, seq_lengths)
    key_segment = segment_info(key_places, seq_lengths)[0]
    distance = query_places[:, None] - key_places[None, :]
    allowed = (
        (query_segment[:, None] == key_segment[None, :])
        & (key_places >= 0)[None, :]
        & (distance >= 0)
        & (distance < WINDOW)
    )
    cosine, sine_table = tables(query_position, HD)

    inputs = tokens.astype(F32)
    scale_attn = rms_factor(inputs)
    normed = (inputs * scale_attn * gain_one).astype(BF)
    kv_raw = dot(normed, w_kv)
    keyval = jnp.concatenate(
        [rotate(kv_raw[:, :HD], cosine, sine_table), kv_raw[:, HD:]], axis=1
    ).astype(BF)
    kv_bits = [x_bit] + z_bits + [c_bit]
    all_kv = gather_rel(keyval, kv_bits)

    def rel_place(ctx_index):
        differ = ctx_index ^ own_index
        place = (differ >> 1) & 1
        for n, (_, k) in enumerate(z_bits):
            place = place | (((differ >> (2 + k)) & 1) << (1 + n))
        return place | ((differ & 1) << (1 + len(z_bits)))

    query_raw = dot(normed, w_q).reshape(tok_rows, H, HD)
    queries = (rotate(query_raw, cosine[:, None, :], sine_table[:, None, :]) * HD ** (-0.5)).astype(BF)
    heads_first = jnp.swapaxes(queries, 0, 1)

    spans = WINDOW // tok_rows
    window_blocks = own_block - spans + jnp.arange(spans + 1, dtype=jnp.int32)
    window_places = rel_place(jnp.take(owners, jnp.clip(window_blocks, 0, ctx_count - 1)))
    window_kv = jnp.take(all_kv, window_places, axis=0).reshape(WINDOW + tok_rows, 2 * HD)
    keys = window_kv[:, :HD]
    values = window_kv[:, HD:]
    scores = masked_scores(heads_first, keys, allowed)
    row_max = jnp.max(scores, axis=-1, keepdims=True)
    log_total = row_max + jnp.log(jnp.sum(jnp.exp(scores - row_max), axis=-1, keepdims=True))
    softmax_w = jnp.exp(scores - log_total).astype(BF)
    attended = jnp.einsum("hqk,kd->qhd", softmax_w, values, preferred_element_type=F32)
    attended = attended.reshape(tok_rows, H * HD).astype(BF)
    hidden = inputs + dot(attended, w_o)

    scale_mlp = rms_factor(hidden)
    normed2 = group_gather((hidden * scale_mlp * gain_two).astype(BF))
    both_parts = dot(normed2, w_gu)
    gate_part = both_parts[:, :units]
    up_part = both_parts[:, units:]

    def gelu_tanh(values_in):
        return jax.nn.gelu(values_in, approximate=True)

    activated, gelu_back = jax.vjp(gelu_tanh, gate_part)
    inner_act = (activated * up_part).astype(BF)
    d_inner = dot_t(cot_all, w_dn)
    d_gate = gelu_back(d_inner * up_part)[0].astype(BF)
    d_up = (d_inner * activated).astype(BF)
    d_normed2 = group_scatter(dot_t(jnp.concatenate([d_gate, d_up], axis=1), w_gu))

    def core_sum(left, kept, sent):
        mine, theirs = t_dot(left, kept).astype(BF), t_dot(left, sent).astype(BF)
        return (mine.astype(F32) + flip(theirs, c_bit).astype(F32)).astype(BF)

    low_cot, high_cot = cot_all[:, : width // 2], cot_all[:, width // 2 :]
    down_sum = core_sum(
        inner_act,
        jnp.where(c_at == 0, low_cot, high_cot),
        jnp.where(c_at == 0, high_cot, low_cot),
    )
    down_sum = scatter_abs(down_sum, z_bits)
    down_half = gather_abs(down_sum, up_z[::-1] if False else z_bits, 0) if False else None
    up_sum = core_sum(
        normed2, jnp.where(c_at == 0, d_gate, d_up), jnp.where(c_at == 0, d_up, d_gate)
    )
    up_sum = scatter_abs(up_sum.reshape(y_count, width // y_count, units), z_bits, 1)

    def spread_z(array, dim):
        return gather_z(array, dim)

    def gather_z(array, dim):
        held = array[None]
        for bit in z_bits:
            held = jnp.concatenate([held, flip(held, bit)], axis=0)
        z_at = lax.axis_index("z")
        count = len(z_bits)
        order = []
        for place in range(z_count):
            differ = place ^ z_at
            rel = 0
            for n, (_, k) in enumerate(z_bits):
                rel = rel | (((differ >> k) & 1) << n)
            order.append(rel)
        del count
        return jnp.concatenate([pick(held, rel, 0) for rel in order], axis=dim)

    down_half = gather_z(down_sum, 0)
    down_half = gather_abs(down_half, [x_bit], 0)
    grad_down = gather_abs(down_half, [c_bit], 1).astype(F32)

    pieces = [pick(up_sum, y_at, 0)]
    for r in range(1, y_count):
        pieces.append(
            lax.ppermute(
                pick(up_sum, y_at ^ r, 0), "y", [(i, i ^ r) for i in range(y_count)]
            )
        )
    if y_count == 2:
        up_rows = join(pieces[0][:, None], pieces[1][:, None], y_bits[0], 1)
    else:
        order = jnp.arange(y_count, dtype=jnp.int32) ^ y_at
        up_rows = jnp.take(jnp.stack(pieces, axis=1), order, axis=1)
    up_rows = gather_z(up_rows, 0)
    up_rows = gather_abs(up_rows[:, :, None], [x_bit], 2)
    up_rows = up_rows.reshape(up_rows.shape[0], FF)
    grad_gateup = gather_abs(up_rows, [c_bit], 1).astype(F32)

    block_output = (hidden + group_scatter(dot(inner_act, w_dn))).astype(BF)

    d_gain_mlp = jnp.sum(d_normed2 * hidden * scale_mlp, axis=0)
    d_hidden = cotangent.astype(F32) + norm_back(d_normed2, hidden, scale_mlp, gain_two)

    def attn_grad(left, right):
        half = right.shape[1] // 2
        low_part, high_part = right[:, :half], right[:, half:]
        total = core_sum(
            left,
            jnp.where(c_at == 0, low_part, high_part),
            jnp.where(c_at == 0, high_part, low_part),
        )
        total = scatter_abs(total, z_y_x)
        return total

    z_y_x = y_bits
    def attn_finish(total):
        total = scatter_abs(total, z_bits + [x_bit])
        total = gather_z_x(total)
        return gather_abs(total, [c_bit], 1).astype(F32)

    def gather_z_x(total):
        rows, cols = total.shape
        total = gather_z(total[None], 0)
        total = gather_abs(total[:, None], [x_bit], 1)
        return total.reshape(z_count * 2 * rows, cols)

    d_attn = d_hidden.astype(BF)
    grad_out = attn_finish(attn_grad(attended, d_attn))
    d_attended = dot_t(d_attn, w_o)
    d_attended = jnp.swapaxes(d_attended.astype(BF).reshape(tok_rows, H, HD), 0, 1)
    soft_again = jnp.exp(masked_scores(heads_first, keys, allowed) - log_total)
    d_soft = jnp.einsum("hqd,kd->hqk", d_attended, values, preferred_element_type=F32)
    delta = jnp.sum(soft_again * d_soft, axis=-1, keepdims=True)
    d_scores = (soft_again * (d_soft - delta)).astype(BF)
    soft_low = soft_again.astype(BF)
    d_key = jnp.einsum("hqk,hqd->kd", d_scores, heads_first, preferred_element_type=F32)
    d_value = jnp.einsum("hqk,hqd->kd", soft_low, d_attended, preferred_element_type=F32)
    d_window = jnp.concatenate([d_key, d_value], axis=1).astype(BF)
    d_window = d_window.reshape(spans + 1, tok_rows, 2 * HD)
    d_window = jnp.concatenate([d_window, jnp.zeros_like(d_window[:1])], axis=0)
    rel_ids = jnp.zeros((ctx_count,), jnp.int32)
    rel_r = jnp.arange(ctx_count, dtype=jnp.int32)
    for n, (_, k) in enumerate(kv_bits):
        axis = kv_bits[n][0]
        shift = {"c": 0, "x": 1, "z": 2 + k}[axis]
        rel_ids = rel_ids | (((rel_r >> n) & 1) << shift)
    rel_ids = rel_ids ^ own_index
    entry = jnp.take(block_row, rel_ids) - (own_block - spans)
    entry = jnp.where((entry >= 0) & (entry <= spans), entry, spans + 1)
    d_rel = jnp.take(d_window, entry, axis=0)
    d_kv_own = scatter_rel(d_rel, kv_bits).astype(F32)

    d_query = jnp.einsum("hqk,kd->qhd", d_scores, keys, preferred_element_type=F32)
    d_query_raw = rotate(d_query * HD ** (-0.5), cosine[:, None, :], -sine_table[:, None, :])
    d_query_raw = d_query_raw.reshape(tok_rows, H * HD).astype(BF)
    grad_query = attn_finish(attn_grad(normed, d_query_raw))
    d_normed = dot_t(d_query_raw, w_q)
    d_kv_raw = jnp.concatenate(
        [rotate(d_kv_own[:, :HD], cosine, -sine_table), d_kv_own[:, HD:]], axis=1
    ).astype(BF)
    grad_keyval = attn_finish(attn_grad(normed, d_kv_raw))
    d_normed = d_normed + dot_t(d_kv_raw, w_kv)
    d_gain_attn = jnp.sum(d_normed * inputs * scale_attn, axis=0)
    grad_tokens = d_hidden + norm_back(d_normed, inputs, scale_attn, gain_one)

    d_gains = lax.psum(jnp.stack([d_gain_attn, d_gain_mlp]), ("z", "x", "c", "y"))
    d_gains = lax.dynamic_slice_in_dim(d_gains, y_at * gain_attn.shape[0], gain_attn.shape[0], 1)
    return (
        block_output,
        grad_tokens,
        d_gains[0],
        grad_query,
        grad_keyval,
        grad_out,
        d_gains[1],
        grad_gateup,
        grad_down,
    )


def solution(mesh):
    ctx_count, y_count = mesh.shape["ctx"], mesh.shape["fsdp"]
    fine = Mesh(mesh.devices.reshape(ctx_count // 4, 2, 2, y_count), ("z", "x", "c", "y"))
    rows, shard = P(("z", "x", "c", "y"), None), P("y", None)
    in_specs = (rows, rows, shard, shard, P("y"), shard, shard, shard, P("y"), shard, shard)
    out_specs = (rows, rows, P("y"), shard, shard, shard, P("y"), shard, shard)
    return jax.shard_map(body, mesh=fine, in_specs=in_specs, out_specs=out_specs, check_vma=False)
```

```python
import functools
import math

import jax
import jax.numpy as jnp
from jax import lax
from jax.experimental import pallas as pl
from jax.experimental.pallas import tpu as pltpu
from jax.sharding import Mesh
from jax.sharding import PartitionSpec as P

H = 12
HD = 128
FF = 4608
WINDOW = 1024
EPSILON = 1e-06
BF = jnp.bfloat16
F32 = jnp.float32
VMEM_LIMIT = 48 * 1024 * 1024


def tables(places, width):
    half_width = width // 2
    frequency = jnp.exp(
        jnp.arange(half_width, dtype=jnp.float32) * (-2.0 * math.log(10000.0) / width)
    )
    angles = places.astype(jnp.float32)[:, None] * frequency[None, :]
    return (jnp.cos(angles), jnp.sin(angles))


def rotate(values, cosine, sine):
    turned = jnp.concatenate([values[:, HD // 2 :], values[:, : HD // 2]], axis=1)
    return values * cosine + turned * sine


def rms_factor(values):
    return lax.rsqrt(jnp.mean(values * values, axis=-1, keepdims=True) + EPSILON)


def norm_back(grad_normed, values, factor, gain):
    scaled = grad_normed * gain
    return factor * scaled - values * factor**3 * jnp.mean(scaled * values, axis=-1, keepdims=True)


def segment_info(places, seq_lengths):
    seq_ends = jnp.cumsum(seq_lengths)
    passed = places[:, None] >= seq_ends[None, :]
    segment = jnp.sum(passed.astype(jnp.int32), axis=1)
    seq_start = jnp.sum(jnp.where(passed, seq_lengths[None, :], 0), axis=1)
    return (segment, places - seq_start)


def dot(a, b):
    return jnp.dot(a, b, preferred_element_type=F32)


def dot_t(a, b):
    return lax.dot_general(a, b, (((1,), (1,)), ((), ())), preferred_element_type=F32)


def t_dot(a, b):
    return lax.dot_general(a, b, (((0,), (0,)), ((), ())), preferred_element_type=F32)


def after(value, *earlier):
    return lax.optimization_barrier((value,) + earlier)[0]


def shift(array, axis, mask):
    return lax.ppermute(array, axis, [(i, i ^ mask) for i in range(lax.axis_size(axis))])


def bit(axis, k=0):
    return (lax.axis_index(axis) >> k) & 1


def pick(array, index, dim):
    return lax.dynamic_index_in_dim(array, index, dim, keepdims=False)


def add(a, b):
    return (a.astype(F32) + b.astype(F32)).astype(BF)


def by_place(entries, axis_name):
    if len(entries) == 2:
        low, high = jnp.stack(entries), jnp.stack(entries[::-1])
        return jnp.where(lax.axis_index(axis_name) == 0, low, high)
    order = jnp.arange(len(entries), dtype=jnp.int32) ^ lax.axis_index(axis_name)
    return jnp.take(jnp.stack(entries), order, axis=0)


def kernel_call(function, **options):
    return pl.pallas_call(
        function,
        compiler_params=pltpu.CompilerParams(vmem_limit_bytes=VMEM_LIMIT),
        cost_estimate=pl.CostEstimate(flops=1000, bytes_accessed=1000, transcendentals=0),
        **options,
    )


def whole_spec(array):
    zeros = (0,) * array.ndim
    return pl.BlockSpec(array.shape, lambda *_: zeros)


ANY = pl.BlockSpec(memory_space=pl.ANY)


def load_rows(target, pieces, rows, sem):
    copies = []
    for n, piece in enumerate(pieces):
        start = pl.multiple_of(rows[n], 16)
        copies.append(
            pltpu.make_async_copy(piece, target.at[pl.ds(start, piece.shape[0])], sem.at[n])
        )
    for copy in copies:
        copy.start()
    return copies


def copy_kernel(blocks, spots, *refs):
    parts, out, sem = refs[:-2], refs[-2], refs[-1]
    copies = []
    for n, (part, rows, columns) in enumerate(blocks):
        at = [pl.multiple_of(spots[n, 0], 16), pl.multiple_of(spots[n, 1], 128)]
        to = [pl.multiple_of(spots[n, 2], 16), pl.multiple_of(spots[n, 3], 128)]
        copies.append(
            pltpu.make_async_copy(
                parts[part].at[pl.ds(at[0], rows), pl.ds(at[1], columns)],
                out.at[pl.ds(to[0], rows), pl.ds(to[1], columns)],
                sem.at[n],
            )
        )
    for copy in copies:
        copy.start()
    for copy in copies:
        copy.wait()


def lay_out(shape, parts, moves):
    aligned = all(size[0] % 16 == 0 and size[1] % 128 == 0 for _, size, _, _ in moves)
    if not aligned:
        out = jnp.zeros(shape, parts[0].dtype)
        for part, size, at, to in moves:
            out = lax.dynamic_update_slice(out, lax.dynamic_slice(parts[part], at, size), to)
        return out
    spots = jnp.stack(
        [jnp.stack([jnp.asarray(v, jnp.int32) for v in at + to]) for _, _, at, to in moves]
    )
    blocks = tuple((part,) + size for part, size, _, _ in moves)
    return kernel_call(
        functools.partial(copy_kernel, blocks),
        out_shape=jax.ShapeDtypeStruct(shape, parts[0].dtype),
        in_specs=[pl.BlockSpec(memory_space=pltpu.SMEM)] + [ANY] * len(parts),
        out_specs=pl.BlockSpec(memory_space=pltpu.VMEM),
        scratch_shapes=[pltpu.SemaphoreType.DMA((len(moves),))],
    )(spots, *parts)


def widen_kernel(maps, *refs):
    parts, out = refs[:4], refs[-1]
    source = pl.program_id(1) ^ maps[0]
    for n in range(4):

        @pl.when(source == n)
        def _(n=n):
            out[...] = parts[n][...].reshape(out.shape).astype(F32)


def widen(parts, z_places, out_shape, spot, so_far=None):
    z_count, rows, columns = parts[0].shape
    x_at, c_at = lax.axis_index("x"), lax.axis_index("c")
    if columns % 128 or rows % 16:
        out = jnp.zeros(out_shape, F32) if so_far is None else so_far
        ordered = jnp.stack(parts)
        for z in range(z_count):
            for c in range(2):
                for x in range(2):
                    block = ordered[(c * 2 + x) ^ (c_at * 2 + x_at), z_places[z]]
                    at = spot(z, c, x)
                    out = lax.dynamic_update_slice(
                        out, block.astype(F32), (at[0] * rows, at[1] * columns)
                    )
        return out
    maps = jnp.concatenate(
        [jnp.stack([c_at * 2 + x_at, lax.axis_index("y")]).astype(jnp.int32), z_places]
    )
    specs = [pl.BlockSpec((1, rows, columns), lambda z, k, maps: (maps[2 + z], 0, 0))] * 4
    operands = list(parts)
    aliases = {}
    if so_far is not None:
        specs.append(ANY)
        operands.append(so_far)
        aliases = {5: 0}
    return kernel_call(
        widen_kernel,
        grid_spec=pltpu.PrefetchScalarGridSpec(
            num_scalar_prefetch=1,
            grid=(z_count, 4),
            in_specs=specs,
            out_specs=pl.BlockSpec(
                (rows, columns), lambda z, k, maps: spot(z, k // 2, k % 2, maps[1])
            ),
        ),
        out_shape=jax.ShapeDtypeStruct(out_shape, F32),
        input_output_aliases=aliases,
    )(maps, *operands)


def attend_kernel(n_q, n_o, spans, maps, *refs):
    normed, tokens, gain, bias, cosine, sine = refs[:6]
    blocks = refs[6 : 6 + spans]
    at = 6 + spans
    q_pieces, o_pieces = refs[at : at + n_q], refs[at + n_q : at + n_q + n_o]
    queries, attended, hidden, own_norm, factor = refs[at + n_q + n_o : at + n_q + n_o + 5]
    w_q, w_o, keys, values, total, q_sem, o_sem = refs[at + n_q + n_o + 5 :]
    step = pl.program_id(0)
    rows = normed.shape[0]

    @pl.when(step == 0)
    def _():
        first = load_rows(w_q, q_pieces, [maps[spans + n] for n in range(n_q)], q_sem)
        second = load_rows(w_o, o_pieces, [maps[spans + n_q + n] for n in range(n_o)], o_sem)
        for n in range(spans):
            keys[n * rows : (n + 1) * rows, :] = blocks[n][0, :, :HD]
            values[n * rows : (n + 1) * rows, :] = blocks[n][0, :, HD:]
        total[...] = tokens[...].astype(F32)
        for copy in first + second:
            copy.wait()

    columns = pl.ds(pl.multiple_of(step * 2 * HD, 2 * HD), 2 * HD)
    raw = dot(normed[...], w_q[:, columns])
    done = []
    for n in range(2):
        turned = rotate(raw[:, n * HD : (n + 1) * HD], cosine[...], sine[...])
        query = (turned * HD ** (-0.5)).astype(BF)
        queries[:, n * HD : (n + 1) * HD] = query
        scores = dot_t(query, keys[...]) + bias[...]
        weights = jnp.exp(scores - jnp.max(scores, axis=-1, keepdims=True))
        share = 1.0 / jnp.sum(weights, axis=-1, keepdims=True)
        done.append(dot((weights * share).astype(BF), values[...]).astype(BF))
    both = jnp.concatenate(done, axis=1)
    attended[...] = both
    total[...] += dot(both, w_o[columns, :])

    @pl.when(step == pl.num_programs(0) - 1)
    def _():
        out = total[...]
        hidden[...] = out
        scale = rms_factor(out)
        factor[...] = jnp.broadcast_to(scale, factor.shape)
        own_norm[...] = (out * scale * gain[...]).astype(BF)


def attend_back_kernel(n_o, spans, entry_count, maps, *refs):
    d_attn, queries, bias, cosine, sine = refs[:5]
    blocks = refs[5 : 5 + spans]
    pieces = refs[5 + spans : 5 + spans + n_o]
    d_raw, kept, sent = refs[5 + spans + n_o : 8 + spans + n_o]
    w_o, keys, values, d_keys, d_values, d_window, sem = refs[8 + spans + n_o :]
    step = pl.program_id(0)
    rows = d_attn.shape[0]

    @pl.when(step == 0)
    def _():
        base = spans + entry_count
        copies = load_rows(w_o, pieces, [maps[base + n] for n in range(n_o)], sem)
        for n in range(spans):
            keys[n * rows : (n + 1) * rows, :] = blocks[n][0, :, :HD]
            values[n * rows : (n + 1) * rows, :] = blocks[n][0, :, HD:]
        d_keys[...] = jnp.zeros_like(d_keys)
        d_values[...] = jnp.zeros_like(d_values)
        for copy in copies:
            copy.wait()

    w_rows = pl.ds(pl.multiple_of(step * 2 * HD, 2 * HD), 2 * HD)
    d_both = dot_t(d_attn[...], w_o[w_rows, :]).astype(BF)
    for n in range(2):
        query = queries[:, n * HD : (n + 1) * HD]
        d_out = d_both[:, n * HD : (n + 1) * HD]
        scores = dot_t(query, keys[...]) + bias[...]
        weights = jnp.exp(scores - jnp.max(scores, axis=-1, keepdims=True))
        soft = weights * (1.0 / jnp.sum(weights, axis=-1, keepdims=True))
        d_soft = dot_t(d_out, values[...])
        delta = jnp.sum(soft * d_soft, axis=-1, keepdims=True)
        d_scores = (soft * (d_soft - delta)).astype(BF)
        d_query = dot(d_scores, keys[...]) * HD ** (-0.5)
        d_raw[:, n * HD : (n + 1) * HD] = rotate(d_query, cosine[...], -sine[...]).astype(BF)
        d_keys[...] += t_dot(query, d_scores)
        d_values[...] += t_dot(d_out, soft.astype(BF))

    @pl.when(step == pl.num_programs(0) - 1)
    def _():
        d_window[: spans * rows, :HD] = d_keys[...].T.astype(BF)
        d_window[: spans * rows, HD:] = d_values[...].T.astype(BF)
        d_window[spans * rows :, :] = jnp.zeros((rows, 2 * HD), BF)
        for n in range(entry_count):
            out = kept if n < entry_count // 2 else sent
            start = pl.multiple_of(maps[spans + n] * rows, rows)
            out[n % (entry_count // 2)] = d_window[pl.ds(start, rows), :]


ROOT = math.sqrt(2.0 / math.pi)


def forward_kernel(maps, normed, cot, w_gate, w_up, w_down, inner, d_both):
    gate, up = dot(normed[...], w_gate[...]), dot(normed[...], w_up[...])
    d_inner = dot_t(cot[...], w_down[...])
    square = gate * gate
    bent = jnp.tanh(ROOT * (gate + 0.044715 * (square * gate)))
    half = 0.5 * (1.0 + bent)
    active = gate * half
    slope = half + 0.5 * gate * (1.0 - bent * bent) * (ROOT * (1.0 + 3 * 0.044715 * square))
    inner[...] = (active * up).astype(BF)
    d_both[0] = (d_inner * up * slope).astype(BF)
    d_both[1] = (d_inner * active).astype(BF)


def cut_rows(result, outs):
    at = 0
    for out in outs:
        out[...] = result[at : at + out.shape[0]].astype(BF)
        at += out.shape[0]


def back_kernel(d_both, w_gu, *outs):
    units = d_both.shape[2]
    result = dot_t(d_both[0], w_gu[:, :units]) + dot_t(d_both[1], w_gu[:, units:])
    cut_rows(result, outs)


def down_kernel(maps, inner, w_down, *outs):
    cut_rows(dot(inner[...], w_down[...]), outs)


def grad_kernel(groups, block_rows, added, maps, left, right, *refs):
    result = t_dot(left[...], right[...].reshape(right.shape[-2:]))
    if added:
        result = result + refs[0][...].astype(F32)
    outs = refs[1:] if added else refs
    if groups is None:
        outs[0][...] = result.astype(BF)
        return
    total = outs[-1]
    total[...] = result
    place = 0
    for n, count in enumerate(groups):
        for k in range(count):
            start = pl.multiple_of(maps[2 + place] * block_rows, 16)
            outs[n][k] = total[pl.ds(start, block_rows), :].astype(BF)
            place += 1


def grad(left, left_block, left_columns, right, half, added=None, groups=None, order=None):
    tokens = left.shape[0]
    if right.ndim == 3:
        columns = right.shape[2]
    else:
        columns = right.shape[1] // 2
    blocks = 0 if groups is None else sum(groups)
    block_rows = 0 if groups is None else left_columns // blocks
    if columns % 128 or left_columns % 128 or block_rows % 16:
        cut = lax.dynamic_slice_in_dim(left, left_block * left_columns, left_columns, 1)
        if right.ndim == 3:
            other = pick(right, half, 0)
        else:
            other = lax.dynamic_slice_in_dim(right, half * columns, columns, 1)
        result = t_dot(cut, other)
        if added is not None:
            result = result + added.astype(F32)
        result = result.astype(BF)
        if groups is None:
            return result
        result = jnp.take(result.reshape(blocks, block_rows, columns), order, axis=0)
        outs, at = [], 0
        for count in groups:
            outs.append(result[at : at + count])
            at += count
        return outs
    wide = 384 if columns % 384 == 0 else (256 if columns % 256 == 0 else 128)
    steps = columns // wide
    maps = jnp.stack([jnp.asarray(left_block, jnp.int32), jnp.asarray(half, jnp.int32)])
    if groups is not None:
        maps = jnp.concatenate([maps, order.astype(jnp.int32)])
    in_specs = [pl.BlockSpec((tokens, left_columns), lambda i, maps: (0, maps[0]))]
    if right.ndim == 3:
        in_specs.append(pl.BlockSpec((1, tokens, wide), lambda i, maps: (maps[1], 0, i)))
    else:
        in_specs.append(pl.BlockSpec((tokens, wide), lambda i, maps: (0, maps[1] * steps + i)))
    operands = [left, right]
    if added is not None:
        in_specs.append(pl.BlockSpec((left_columns, wide), lambda i, maps: (0, i)))
        operands.append(added)
    scratch = []
    if groups is None:
        shapes = [jax.ShapeDtypeStruct((left_columns, columns), BF)]
        out_specs = [pl.BlockSpec((left_columns, wide), lambda i, maps: (0, i))]
    else:
        shapes = [jax.ShapeDtypeStruct((count, block_rows, columns), BF) for count in groups]
        out_specs = [
            pl.BlockSpec((count, block_rows, wide), lambda i, maps: (0, 0, i)) for count in groups
        ]
        scratch = [pltpu.VMEM((left_columns, wide), F32)]
    outs = kernel_call(
        functools.partial(grad_kernel, groups, block_rows, added is not None),
        grid_spec=pltpu.PrefetchScalarGridSpec(
            num_scalar_prefetch=1,
            grid=(steps,),
            in_specs=in_specs,
            out_specs=out_specs,
            scratch_shapes=scratch,
        ),
        out_shape=shapes,
    )(maps, *operands)
    return outs[0] if groups is None else outs


class Clock:
    def __init__(self):
        self.marks = ()

    def tie(self, value):
        return after(value, *self.marks) if self.marks else value

    def mark(self, *values):
        self.marks = values


def body(
    tokens,
    cotangent,
    lengths,
    block_of,
    gain_attn,
    w_query,
    w_keyval,
    w_out,
    gain_mlp,
    w_gateup,
    w_down,
):
    tok_rows, width = tokens.shape
    y_count, z_count = lax.axis_size("y"), lax.axis_size("z")
    ctx_count = 4 * z_count
    z_levels = z_count.bit_length() - 1
    x_at, c_at, y_at, z_at = (lax.axis_index(name) for name in ("x", "c", "y", "z"))
    own_index = (z_at * 2 + x_at) * 2 + c_at
    deep = w_query.shape[0]
    quarter = deep // 4
    units = FF // (2 * y_count)
    half_tok = tok_rows // 2
    group = 2 * y_count
    others = range(1, y_count)
    clock = Clock()
    tie, mark = clock.tie, clock.mark

    gain_rows = -(-(-(-2 * deep // (2 * HD))) // 16) * 16
    gain_pack = jnp.concatenate([gain_attn, gain_mlp])
    gain_pack = jnp.pad(gain_pack, (0, gain_rows * 2 * HD - 2 * deep)).reshape(gain_rows, 2 * HD)
    pack = jnp.concatenate([w_keyval, gain_pack], axis=0)
    packs = [pack] + [shift(pack, "y", r) for r in others]
    place_cx = c_at * 2 + x_at
    place_cz = c_at * 2 + (z_at & 1)

    def rows_of(weight, place):
        return lax.dynamic_slice_in_dim(weight, place * quarter, quarter, 0)

    wq_piece = after(rows_of(w_query, place_cx), pack)
    wq_found = {r: [shift(wq_piece, "y", r)] for r in others}
    wo_piece = after(rows_of(w_out, place_cx), wq_piece)
    wo_found = {r: [shift(wo_piece, "y", r)] for r in others}
    cot_first = after(cotangent[:half_tok], wo_piece)
    cot_second = cotangent[half_tok:]
    cot_first = jnp.concatenate([cot_first] + [shift(cot_first, "y", r) for r in others], axis=0)
    cot_second = jnp.concatenate([cot_second, shift(cot_second, "x", 1)], axis=0)
    gu_found = {}
    for r in others:
        column = ((y_at ^ r) * 2 + x_at) * units
        moves = [
            (0, (quarter, units), (place_cz * quarter, part * FF + column), (0, part * units))
            for part in (0, 1)
        ]
        piece = lay_out((quarter, 2 * units), [after(w_gateup, wo_piece)], moves)
        gu_found[r] = [shift(piece, "y", r)]

    def with_sharer(found, axis):
        return {r: [pieces[0], shift(pieces[0], axis, 1)] for r, pieces in found.items()}

    def with_core(found):
        return {r: pair + [shift(p, "c", 1) for p in pair] for r, pair in found.items()}

    def listed(shard, found, place):
        pieces, rows = [shard], [y_at * deep]
        for r, quarters in found.items():
            for s, piece in enumerate(quarters):
                pieces.append(piece)
                rows.append((y_at ^ r) * deep + (place ^ s) * quarter)
        return pieces, rows

    device_ids = jnp.arange(ctx_count, dtype=jnp.int32)
    block_row = block_of[0]
    own_block = jnp.sum(jnp.where(device_ids == own_index, block_row, 0))
    own_start = own_block * tok_rows
    owners = jnp.sum(
        jnp.where(block_row[None, :] == device_ids[:, None], device_ids[None, :], 0), axis=1
    )
    seq_lengths = lengths[0]
    query_places = own_start + jnp.arange(tok_rows, dtype=jnp.int32)
    key_places = own_start - WINDOW + jnp.arange(WINDOW + tok_rows, dtype=jnp.int32)
    query_segment, query_position = segment_info(query_places, seq_lengths)
    key_segment = segment_info(key_places, seq_lengths)[0]
    distance = query_places[:, None] - key_places[None, :]
    allowed = (
        (query_segment[:, None] == key_segment[None, :])
        & (key_places >= 0)[None, :]
        & (distance >= 0)
        & (distance < WINDOW)
    )
    bias = jnp.where(allowed, 0.0, -1e30).astype(F32)
    cosine, sine = tables(query_position, HD)
    cosine = jnp.concatenate([cosine, cosine], axis=1)
    sine = jnp.concatenate([-sine, sine], axis=1)
    spans = WINDOW // tok_rows + 1
    first_block = own_block - (spans - 1)

    def entry_of(ctx_index):
        differ = ctx_index ^ own_index
        return (differ >> 2) | (((differ >> 1) & 1) << z_levels) | ((differ & 1) << (z_levels + 1))

    window = first_block + jnp.arange(spans, dtype=jnp.int32)
    window = entry_of(jnp.take(owners, jnp.clip(window, 0, ctx_count - 1)))
    entries = jnp.arange(ctx_count, dtype=jnp.int32)
    differ = (entries & (z_count - 1)) << 2
    differ = differ | (((entries >> z_levels) & 1) << 1) | (entries >> (z_levels + 1))
    entry_block = jnp.take(block_row, differ ^ own_index) - first_block
    entry_block = jnp.where((entry_block >= 0) & (entry_block < spans), entry_block, spans)

    inputs = tokens.astype(F32)
    scale_attn = rms_factor(inputs)
    w_kv = by_place([p[:deep] for p in packs], "y").reshape(width, 2 * HD)
    flat = [p[deep:].reshape(-1)[: 2 * deep].reshape(2, deep) for p in packs]
    gains = jnp.swapaxes(by_place(flat, "y"), 0, 1).reshape(2, width).astype(F32)
    gain_one, gain_two = gains[0], gains[1]
    normed = (inputs * scale_attn * gain_one).astype(BF)
    kv_raw = dot(normed, w_kv)
    keyval = jnp.concatenate(
        [rotate(kv_raw[:, :HD], cosine, sine), kv_raw[:, HD:]], axis=1
    ).astype(BF)
    all_kv = jnp.stack([keyval] + [shift(keyval, "z", d) for d in range(1, z_count)])
    all_kv = jnp.concatenate([all_kv, shift(all_kv, "x", 1)], axis=0)
    all_kv = jnp.concatenate([all_kv, shift(all_kv, "c", 1)], axis=0)

    q_pieces, q_rows = listed(w_query, with_core(with_sharer(wq_found, "x")), place_cx)
    o_pieces, o_rows = listed(w_out, with_core(with_sharer(wo_found, "x")), place_cx)
    n_q, n_o = len(q_pieces), len(o_pieces)
    pairs = H // 2
    kv_specs = [
        pl.BlockSpec((1, tok_rows, 2 * HD), lambda i, maps, n=n: (maps[n], 0, 0))
        for n in range(spans)
    ]
    pair_spec = pl.BlockSpec((tok_rows, 2 * HD), lambda i, maps: (0, i))
    token_spec = pl.BlockSpec((tok_rows, width), lambda i, maps: (0, 0))
    maps = jnp.concatenate([window, jnp.stack(q_rows + o_rows).astype(jnp.int32)])
    small = [gain_two[None], bias, cosine, sine]
    queries, attended, hidden, own_norm, factor = kernel_call(
        functools.partial(attend_kernel, n_q, n_o, spans),
        grid_spec=pltpu.PrefetchScalarGridSpec(
            num_scalar_prefetch=1,
            grid=(pairs,),
            in_specs=[token_spec, token_spec]
            + [whole_spec(a) for a in small]
            + kv_specs
            + [ANY] * (n_q + n_o),
            out_specs=[
                pair_spec,
                pair_spec,
                token_spec,
                token_spec,
                pl.BlockSpec((tok_rows, HD), lambda i, maps: (0, 0)),
            ],
            scratch_shapes=[
                pltpu.VMEM((width, H * HD), BF),
                pltpu.VMEM((H * HD, width), BF),
                pltpu.VMEM((spans * tok_rows, HD), BF),
                pltpu.VMEM((spans * tok_rows, HD), BF),
                pltpu.VMEM((tok_rows, width), F32),
                pltpu.SemaphoreType.DMA((n_q,)),
                pltpu.SemaphoreType.DMA((n_o,)),
            ],
        ),
        out_shape=[
            jax.ShapeDtypeStruct((tok_rows, H * HD), BF),
            jax.ShapeDtypeStruct((tok_rows, H * HD), BF),
            jax.ShapeDtypeStruct((tok_rows, width), F32),
            jax.ShapeDtypeStruct((tok_rows, width), BF),
            jax.ShapeDtypeStruct((tok_rows, HD), F32),
        ],
    )(maps, normed, tokens, *small, *([all_kv] * spans), *q_pieces, *o_pieces)
    scale_mlp = factor[:, :1]

    cot_first = jnp.concatenate([cot_first, shift(cot_first, "x", 1)], axis=0)
    cot_second = jnp.concatenate(
        [cot_second] + [shift(cot_second, "y", r) for r in others], axis=0
    )
    cot_all = jnp.concatenate([cot_first, cot_second], axis=0)
    gu_moves = [
        (0, (deep, units), (0, part * FF + (y_at * 2 + x_at) * units), (y_at * deep, part * units))
        for part in (0, 1)
    ]
    gu_pieces, gu_rows = listed(w_gateup, with_core(with_sharer(gu_found, "z")), place_cz)
    for n in range(1, len(gu_pieces)):
        gu_moves.append((n, (quarter, 2 * units), (0, 0), (gu_rows[n], 0)))
    w_gu = lay_out((width, 2 * units), gu_pieces, gu_moves)

    first, second = own_norm[:half_tok], own_norm[half_tok:]
    first = jnp.concatenate([first] + [shift(first, "y", r) for r in others], axis=0)
    second = jnp.concatenate([second, shift(second, "x", 1)], axis=0)
    first = jnp.concatenate([first, shift(first, "x", 1)], axis=0)
    second = jnp.concatenate([second] + [shift(second, "y", r) for r in others], axis=0)
    normed2 = jnp.concatenate([first, second], axis=0)
    many = group * tok_rows
    fits = units % 128 == 0
    cuts = [many // 4] * 2 + [many // 2 // y_count] * y_count
    cut_shapes = [jax.ShapeDtypeStruct((count, width), BF) for count in cuts]
    x_maps = jnp.stack([x_at]).astype(jnp.int32)

    def cut(result):
        outs, at = [], 0
        for count in cuts:
            outs.append(result[at : at + count].astype(BF))
            at += count
        return outs

    if fits:
        wide = 384 if units % 384 == 0 else 128
        steps = units // wide
        inner_act, d_both = kernel_call(
            forward_kernel,
            grid_spec=pltpu.PrefetchScalarGridSpec(
                num_scalar_prefetch=1,
                grid=(steps,),
                in_specs=[
                    pl.BlockSpec((many, width), lambda i, maps: (0, 0)),
                    pl.BlockSpec((many, width), lambda i, maps: (0, 0)),
                    pl.BlockSpec((width, wide), lambda i, maps: (0, i)),
                    pl.BlockSpec((width, wide), lambda i, maps: (0, steps + i)),
                    pl.BlockSpec((wide, width), lambda i, maps: (maps[0] * steps + i, 0)),
                ],
                out_specs=[
                    pl.BlockSpec((many, wide), lambda i, maps: (0, i)),
                    pl.BlockSpec((2, many, wide), lambda i, maps: (0, 0, i)),
                ],
            ),
            out_shape=[
                jax.ShapeDtypeStruct((many, units), BF),
                jax.ShapeDtypeStruct((2, many, units), BF),
            ],
        )(x_maps, normed2, cot_all, w_gu, w_gu, w_down)
        block = 512
        d_cut = kernel_call(
            back_kernel,
            grid=(width // block,),
            in_specs=[
                whole_spec(d_both),
                pl.BlockSpec((block, 2 * units), lambda i: (i, 0)),
            ],
            out_specs=[pl.BlockSpec((count, block), lambda i: (0, i)) for count in cuts],
            out_shape=cut_shapes,
        )(d_both, w_gu)

        def down_cut():
            return kernel_call(
                down_kernel,
                grid_spec=pltpu.PrefetchScalarGridSpec(
                    num_scalar_prefetch=1,
                    grid=(width // block,),
                    in_specs=[
                        pl.BlockSpec((many, units), lambda i, maps: (0, 0)),
                        pl.BlockSpec((units, block), lambda i, maps: (maps[0], i)),
                    ],
                    out_specs=[
                        pl.BlockSpec((count, block), lambda i, maps: (0, i)) for count in cuts
                    ],
                ),
                out_shape=cut_shapes,
            )(x_maps, tie(inner_act), w_down)

    else:
        w_dn = lax.dynamic_slice_in_dim(w_down, x_at * units, units, 0)
        d_inner = dot_t(cot_all, w_dn)
        both_parts = dot(normed2, w_gu)
        active, back = jax.vjp(
            lambda values: jax.nn.gelu(values, approximate=True), both_parts[:, :units]
        )
        up_part = both_parts[:, units:]
        inner_act = (active * up_part).astype(BF)
        d_both = jnp.stack([back(d_inner * up_part)[0], d_inner * active]).astype(BF)
        d_cut = cut(dot_t(d_both[0], w_gu[:, :units]) + dot_t(d_both[1], w_gu[:, units:]))

        def down_cut():
            return cut(dot(tie(inner_act), w_dn))

    mark(*d_cut)

    def group_back(cuts_in, result):
        keep_a, send_a, keep_b, send_b = cuts_in[0], cuts_in[1], cuts_in[2], cuts_in[3:]
        got_a = shift(send_a, "x", 1)
        got_b = [shift(part, "y", r) for r, part in zip(others, send_b, strict=True)]
        yield
        got_a, got_b = tie(got_a), [tie(part) for part in got_b]
        keep_a, got_a = (v.reshape(y_count, half_tok, width) for v in (keep_a, got_a))
        parts_b = [v.reshape(2, half_tok, width) for v in [keep_b] + got_b]
        left_a = [add(keep_a[r], got_a[r]) for r in range(y_count)]
        left_b = [sum(part[n].astype(F32) for part in parts_b).astype(BF) for n in range(2)]
        mark(*left_a[1:], left_b[1])
        got_a = [shift(left_a[r], "y", r) for r in others]
        got_b = shift(left_b[1], "x", 1)
        yield
        got_a, got_b = [tie(part) for part in got_a], tie(got_b)
        first = sum(v.astype(F32) for v in [left_a[0]] + got_a)
        second = left_b[0].astype(F32) + got_b.astype(F32)
        result.append(jnp.concatenate([first, second], axis=0))

    def scatter_z(kept, sent):
        for level in range(z_levels):
            got = shift(sent, "z", 1 << level)
            yield
            got = tie(got)
            half = kept.shape[0] // 2
            if half:
                sent = add(kept[half:], got[half:])
                kept = add(kept[:half], got[:half])
                mark(sent)
            else:
                kept = add(kept[0], got[0])
        return kept

    def spread(piece, finish):
        held = piece[None]
        for level in reversed(range(z_levels)):
            mark(held)
            got = shift(held, "z", 1 << level)
            yield
            held = jnp.concatenate([held, tie(got)], axis=0)
        mark(held)
        beside, across = shift(held, "x", 1), shift(held, "c", 1)
        yield
        beside = tie(beside)
        mark(beside)
        corner = shift(beside, "c", 1)
        yield
        mark(finish([held, beside, tie(across), tie(corner)]))

    z_places = jnp.zeros((z_count,), jnp.int32)
    z_differ = jnp.arange(z_count, dtype=jnp.int32) ^ z_at
    for n, level in enumerate(reversed(range(z_levels))):
        z_places = z_places | (((z_differ >> level) & 1) << n)
    z_order = jnp.zeros((z_count,), jnp.int32)
    for level in range(z_levels):
        z_order = z_order | (
            ((jnp.arange(z_count, dtype=jnp.int32) >> (z_levels - 1 - level)) & 1) << level
        )
    z_order = z_order ^ z_at
    z_groups = [z_count // 2, z_count // 2]

    found = {}

    def finish_down(parts):
        found["down"] = widen(
            parts, z_places, (w_down.shape[0], width), lambda z, c, x, y=None: (x * z_count + z, c)
        )
        return found["down"]

    def finish_up(r):
        def finish(parts):
            found["up"] = widen(
                parts,
                z_places,
                (deep, 2 * FF),
                lambda z, c, x, y=y_at: (z, (c * y_count + (y ^ r)) * 2 + x),
                found.get("up"),
            )
            return found["up"]

        return finish

    def finish_attn(name, columns):
        def finish(parts):
            found[name] = widen(
                parts, z_places, (deep, columns), lambda z, c, x, y=None: (z * 2 + x, c)
            )
            return found[name]

        return finish

    def ffn_chain(job, finish, r):
        left, left_block, left_columns, right = job
        theirs = grad(tie(left), left_block, left_columns, right, 1 - c_at)
        mark(theirs)
        got = shift(theirs, "c", 1)
        yield
        kept, sent = grad(
            tie(left), left_block, left_columns, right, c_at, got, z_groups, z_order
        )
        mark(sent)
        piece = yield from scatter_z(kept, sent)
        if r:
            mark(piece)
            piece = shift(piece, "y", r)
            yield
            piece = tie(piece)
        yield from spread(piece, finish)

    def attn_chain(left, right, finish, column=None):
        theirs = grad(tie(left), 0, width, right, 1 - c_at)
        if column is not None:
            lane = jnp.arange(HD) == 0
            own = jnp.where(c_at == 0, column[0], column[1])[:, None]
            other = jnp.where(c_at == 0, column[1], column[0])[:, None]
            theirs = jnp.concatenate([theirs, jnp.where(lane, other, 0).astype(BF)], axis=1)
        mark(theirs)
        got = shift(theirs, "c", 1)
        yield
        y_order = jnp.arange(y_count, dtype=jnp.int32) ^ y_at
        cols = right.shape[1] // 2
        parts = grad(
            tie(left), 0, width, right, c_at, got[:, :cols], [1] * y_count, y_order
        )
        parts = [part[0] for part in parts]
        if column is not None:
            extra = add(jnp.where(lane, own, 0), got[:, cols:]).reshape(y_count, deep, HD)
            parts = [
                jnp.concatenate([part, pick(extra, y_at ^ r, 0)], axis=1)
                for r, part in enumerate(parts)
            ]
        mark(*parts[1:])
        got = [shift(part, "y", r) for r, part in zip(others, parts[1:], strict=True)]
        yield
        got = [tie(part) for part in got]
        total = sum(v.astype(F32) for v in [parts[0]] + got).astype(BF)
        blocks = total.reshape(z_count, 2, deep // (2 * z_count), total.shape[1])
        kept = jnp.take(pick(blocks, x_at, 1), z_order, axis=0)
        sent = jnp.take(pick(blocks, 1 - x_at, 1), z_order, axis=0)
        mark(sent)
        got = shift(sent, "x", 1)
        yield
        got = tie(got)
        half = z_count // 2
        sent = add(kept[half:], got[half:])
        kept = add(kept[:half], got[:half])
        mark(sent)
        piece = yield from scatter_z(kept, sent)
        yield from spread(piece, finish)

    def step(chain):
        return next(chain, None)

    d_result, out_result = [], []
    d_chain = group_back(d_cut, d_result)
    step(d_chain)
    chain_down = ffn_chain((inner_act, 0, units, cot_all), finish_down, 0)
    chains_up = [
        ffn_chain((normed2, y_at ^ r, deep, d_both), finish_up(r), r)
        for r in list(others) + [0]
    ]
    ffn = chains_up[:-1] + [chain_down, chains_up[-1]]
    for chain in ffn:
        step(chain)
    for chain in ffn:
        step(chain)
    step(d_chain)
    out_cut = down_cut()
    mark(*out_cut)
    out_chain = group_back(out_cut, out_result)
    step(out_chain)
    step(ffn[0])
    step(d_chain)
    d_normed2 = d_result[0]
    d_gain_mlp = jnp.sum(d_normed2 * hidden * scale_mlp, axis=0)
    d_hidden = cotangent.astype(F32) + norm_back(d_normed2, hidden, scale_mlp, gain_two)
    d_attn = d_hidden.astype(BF)
    mark(d_attn)
    chain_out = attn_chain(attended, d_attn, finish_attn("out", width))
    step(chain_out)
    step(ffn[1])
    step(chain_out)

    maps = jnp.concatenate([window, entry_block, jnp.stack(o_rows).astype(jnp.int32)])
    entry_spec = pl.BlockSpec((ctx_count // 2, tok_rows, 2 * HD), lambda i, maps: (0, 0, 0))
    entry_shape = jax.ShapeDtypeStruct((ctx_count // 2, tok_rows, 2 * HD), BF)
    small = [bias, cosine, sine]
    d_query_raw, d_kept, d_sent = kernel_call(
        functools.partial(attend_back_kernel, n_o, spans, ctx_count),
        grid_spec=pltpu.PrefetchScalarGridSpec(
            num_scalar_prefetch=1,
            grid=(pairs,),
            in_specs=[token_spec, pair_spec]
            + [whole_spec(a) for a in small]
            + kv_specs
            + [ANY] * n_o,
            out_specs=[pair_spec, entry_spec, entry_spec],
            scratch_shapes=[
                pltpu.VMEM((H * HD, width), BF),
                pltpu.VMEM((spans * tok_rows, HD), BF),
                pltpu.VMEM((spans * tok_rows, HD), BF),
                pltpu.VMEM((HD, spans * tok_rows), F32),
                pltpu.VMEM((HD, spans * tok_rows), F32),
                pltpu.VMEM(((spans + 1) * tok_rows, 2 * HD), BF),
                pltpu.SemaphoreType.DMA((n_o,)),
            ],
        ),
        out_shape=[jax.ShapeDtypeStruct((tok_rows, H * HD), BF), entry_shape, entry_shape],
    )(maps, tie(d_attn), queries, *small, *([all_kv] * spans), *o_pieces)
    mark(d_sent)

    def kv_back(result):
        kept, sent = d_kept, d_sent
        for axis in ("c", "x"):
            got = shift(sent, axis, 1)
            yield
            got = tie(got)
            half = kept.shape[0] // 2
            if axis == "c":
                sent = add(kept[half:], got[half:])
                kept = add(kept[:half], got[:half])
                mark(sent)
            else:
                left = [add(kept[d], got[d]) for d in range(z_count)]
                mark(*left[1:])
        got = [shift(left[d], "z", d) for d in range(1, z_count)]
        yield
        got = [tie(part) for part in got]
        result.append(sum(v.astype(F32) for v in [left[0]] + got))

    kv_result = []
    kv_chain = kv_back(kv_result)
    step(kv_chain)
    step(ffn[2])
    step(kv_chain)
    chain_query = attn_chain(normed, d_query_raw, finish_attn("query", width))
    step(chain_query)
    step(ffn[0])
    step(ffn[1])
    step(kv_chain)
    step(chain_query)
    step(ffn[0])
    step(out_chain)
    step(kv_chain)
    d_kv_own = kv_result[0]
    d_kv_raw = jnp.concatenate(
        [rotate(d_kv_own[:, :HD], cosine, -sine), d_kv_own[:, HD:]], axis=1
    ).astype(BF)
    w_q = lay_out(
        (width, H * HD),
        q_pieces,
        [(n, p.shape, (0, 0), (q_rows[n], 0)) for n, p in enumerate(q_pieces)],
    )
    d_normed = dot_t(d_query_raw, w_q) + dot_t(d_kv_raw, w_kv)
    d_gain_attn = jnp.sum(d_normed * inputs * scale_attn, axis=0)
    grad_tokens = d_hidden + norm_back(d_normed, inputs, scale_attn, gain_one)
    mark(d_kv_raw, d_gain_attn)
    chain_kv = attn_chain(
        normed, d_kv_raw, finish_attn("keyval", 4 * HD), (d_gain_attn, d_gain_mlp)
    )
    step(chain_kv)
    step(out_chain)
    block_output = (hidden + out_result[0]).astype(BF)
    mark(block_output)

    waiting = [ffn[2], chain_out, ffn[1], chain_kv, ffn[0], chain_query] + ffn[3:]
    alive = list(waiting)
    while alive:
        for chain in list(alive):
            try:
                next(chain)
            except StopIteration:
                alive.remove(chain)
    last = found["keyval"]
    grad_keyval = jnp.concatenate([last[:, :HD], last[:, 2 * HD : 3 * HD]], axis=1)
    return (
        block_output,
        grad_tokens,
        last[:, HD],
        found["query"],
        grad_keyval,
        found["out"],
        last[:, 3 * HD],
        found["up"],
        found["down"],
    )


def solution(mesh):
    ctx_count, y_count = mesh.shape["ctx"], mesh.shape["fsdp"]
    fine = Mesh(mesh.devices.reshape(ctx_count // 4, 2, 2, y_count), ("z", "x", "c", "y"))
    rows, shard = P(("z", "x", "c", "y"), None), P("y", None)
    in_specs = (rows, rows, shard, shard, P("y"), shard, shard, shard, P("y"), shard, shard)
    out_specs = (rows, rows, P("y"), shard, shard, shard, P("y"), shard, shard)
    return jax.shard_map(body, mesh=fine, in_specs=in_specs, out_specs=out_specs, check_vma=False)
```

```python
import functools
import math

import jax
import jax.numpy as jnp
from jax import lax
from jax.experimental import pallas as pl
from jax.experimental.pallas import tpu as pltpu
from jax.sharding import Mesh
from jax.sharding import PartitionSpec as P

H = 12
HD = 128
FF = 4608
WINDOW = 1024
EPSILON = 1e-06
BF = jnp.bfloat16
F32 = jnp.float32
VMEM_LIMIT = 48 * 1024 * 1024


def tables(places, width):
    half_width = width // 2
    frequency = jnp.exp(
        jnp.arange(half_width, dtype=jnp.float32) * (-2.0 * math.log(10000.0) / width)
    )
    angles = places.astype(jnp.float32)[:, None] * frequency[None, :]
    return (jnp.cos(angles), jnp.sin(angles))


def rotate(values, cosine, sine):
    turned = jnp.concatenate([values[:, HD // 2 :], values[:, : HD // 2]], axis=1)
    return values * cosine + turned * sine


def rms_factor(values):
    return lax.rsqrt(jnp.mean(values * values, axis=-1, keepdims=True) + EPSILON)


def segment_info(places, seq_lengths):
    seq_ends = jnp.cumsum(seq_lengths)
    passed = places[:, None] >= seq_ends[None, :]
    segment = jnp.sum(passed.astype(jnp.int32), axis=1)
    seq_start = jnp.sum(jnp.where(passed, seq_lengths[None, :], 0), axis=1)
    return (segment, places - seq_start)


def dot(a, b):
    return jnp.dot(a, b, preferred_element_type=F32)


def dot_t(a, b):
    return lax.dot_general(a, b, (((1,), (1,)), ((), ())), preferred_element_type=F32)


def t_dot(a, b):
    return lax.dot_general(a, b, (((0,), (0,)), ((), ())), preferred_element_type=F32)


def after(value, *earlier):
    return lax.optimization_barrier((value,) + earlier)[0]


def shift(array, axis, mask):
    return lax.ppermute(array, axis, [(i, i ^ mask) for i in range(lax.axis_size(axis))])


def bit(axis, k=0):
    return (lax.axis_index(axis) >> k) & 1


def pick(array, index, dim):
    return lax.dynamic_index_in_dim(array, index, dim, keepdims=False)


def add(a, b):
    return (a.astype(F32) + b.astype(F32)).astype(BF)


def by_place(entries, axis_name):
    if len(entries) == 2:
        low, high = jnp.stack(entries), jnp.stack(entries[::-1])
        return jnp.where(lax.axis_index(axis_name) == 0, low, high)
    order = jnp.arange(len(entries), dtype=jnp.int32) ^ lax.axis_index(axis_name)
    return jnp.take(jnp.stack(entries), order, axis=0)


def kernel_call(function, **options):
    return pl.pallas_call(
        function,
        compiler_params=pltpu.CompilerParams(vmem_limit_bytes=VMEM_LIMIT),
        cost_estimate=pl.CostEstimate(flops=1000, bytes_accessed=1000, transcendentals=0),
        **options,
    )


def whole_spec(array):
    zeros = (0,) * array.ndim
    return pl.BlockSpec(array.shape, lambda *_: zeros)


ANY = pl.BlockSpec(memory_space=pl.ANY)


def load_rows(target, pieces, rows, sem):
    copies = []
    for n, piece in enumerate(pieces):
        start = pl.multiple_of(rows[n], 16)
        copies.append(
            pltpu.make_async_copy(piece, target.at[pl.ds(start, piece.shape[0])], sem.at[n])
        )
    for copy in copies:
        copy.start()
    return copies


def copy_kernel(blocks, spots, *refs):
    parts, out, sem = refs[:-2], refs[-2], refs[-1]
    copies = []
    for n, (part, rows, columns) in enumerate(blocks):
        at = [pl.multiple_of(spots[n, 0], 16), pl.multiple_of(spots[n, 1], 128)]
        to = [pl.multiple_of(spots[n, 2], 16), pl.multiple_of(spots[n, 3], 128)]
        copies.append(
            pltpu.make_async_copy(
                parts[part].at[pl.ds(at[0], rows), pl.ds(at[1], columns)],
                out.at[pl.ds(to[0], rows), pl.ds(to[1], columns)],
                sem.at[n],
            )
        )
    for copy in copies:
        copy.start()
    for copy in copies:
        copy.wait()


def lay_out(shape, parts, moves):
    aligned = all(size[0] % 16 == 0 and size[1] % 128 == 0 for _, size, _, _ in moves)
    if not aligned:
        out = jnp.zeros(shape, parts[0].dtype)
        for part, size, at, to in moves:
            out = lax.dynamic_update_slice(out, lax.dynamic_slice(parts[part], at, size), to)
        return out
    spots = jnp.stack(
        [jnp.stack([jnp.asarray(v, jnp.int32) for v in at + to]) for _, _, at, to in moves]
    )
    blocks = tuple((part,) + size for part, size, _, _ in moves)
    return kernel_call(
        functools.partial(copy_kernel, blocks),
        out_shape=jax.ShapeDtypeStruct(shape, parts[0].dtype),
        in_specs=[pl.BlockSpec(memory_space=pltpu.SMEM)] + [ANY] * len(parts),
        out_specs=pl.BlockSpec(memory_space=pltpu.VMEM),
        scratch_shapes=[pltpu.SemaphoreType.DMA((len(moves),))],
    )(spots, *parts)


def widen_kernel(count, maps, *refs):
    parts, out = refs[:count], refs[-1]
    source = pl.program_id(1) ^ maps[0]
    for n in range(count):

        @pl.when(source == n)
        def _(n=n):
            out[...] = parts[n][...].reshape(out.shape).astype(F32)


def widen(parts, beside, z_places, out_shape, spot, so_far=None):
    count = len(parts)
    z_count, rows, columns = parts[0].shape
    x_at, c_at, y_at = (lax.axis_index(name) for name in ("x", "c", "y"))
    if count == 2:
        flips = [c_at, x_at ^ (1 if beside else 0), y_at]
    else:
        flips = [c_at * 2 + x_at, x_at, y_at]
    if columns % 128 or rows % 16:
        out = jnp.zeros(out_shape, F32) if so_far is None else so_far
        ordered = jnp.stack(parts)
        for z in range(z_count):
            for k in range(count):
                block = ordered[k ^ flips[0], z_places[z]]
                at = spot(z, k, flips[1], y_at) if count == 2 else spot(z, k // 2, k % 2, y_at)
                out = lax.dynamic_update_slice(
                    out, block.astype(F32), (at[0] * rows, at[1] * columns)
                )
        return out
    maps = jnp.concatenate([jnp.stack(flips).astype(jnp.int32), z_places])

    def out_map(z, k, maps):
        if count == 2:
            return spot(z, k, maps[1], maps[2])
        return spot(z, k // 2, k % 2, maps[2])

    specs = [pl.BlockSpec((1, rows, columns), lambda z, k, maps: (maps[3 + z], 0, 0))] * count
    operands = list(parts)
    aliases = {}
    if so_far is not None:
        specs.append(ANY)
        operands.append(so_far)
        aliases = {count + 1: 0}
    return kernel_call(
        functools.partial(widen_kernel, count),
        grid_spec=pltpu.PrefetchScalarGridSpec(
            num_scalar_prefetch=1,
            grid=(z_count, count),
            in_specs=specs,
            out_specs=pl.BlockSpec((rows, columns), out_map),
        ),
        out_shape=jax.ShapeDtypeStruct(out_shape, F32),
        input_output_aliases=aliases,
    )(maps, *operands)


def once_kernel(function, n_in, maps, *refs):
    function(maps, refs[:n_in], refs[n_in:])


def once(function, shapes, *operands, maps=None):
    if maps is None:
        maps = jnp.zeros((1,), jnp.int32)
    return kernel_call(
        functools.partial(once_kernel, function, len(operands)),
        in_specs=[pl.BlockSpec(memory_space=pltpu.SMEM)]
        + [pl.BlockSpec(memory_space=pltpu.VMEM)] * len(operands),
        out_specs=[pl.BlockSpec(memory_space=pltpu.VMEM)] * len(shapes),
        out_shape=[jax.ShapeDtypeStruct(shape, kind) for shape, kind in shapes],
    )(maps, *operands)


def add_halves(kept, got):
    half = kept.shape[0] // 2
    if not half:

        def narrow(_, ins, outs):
            outs[0][...] = (ins[0][...].astype(F32) + ins[1][...].astype(F32)).astype(BF)

        return once(narrow, [(kept.shape, BF)], kept, got)

    def function(_, ins, outs):
        for n in range(2):
            part = pl.ds(n * half, half)
            outs[n][...] = (ins[0][part].astype(F32) + ins[1][part].astype(F32)).astype(BF)

    shape = ((half,) + kept.shape[1:], BF)
    return once(function, [shape, shape], kept, got)


def stack_two(held, got):
    count = held.shape[0]

    def function(_, ins, outs):
        outs[0][:count] = ins[0][...]
        outs[0][count:] = ins[1][...]

    return once(function, [((2 * count,) + held.shape[1:], BF)], held, got)[0]


def kv_kernel(rows, tokens, gain, cosine, sine, *refs):
    pieces = refs[:-4]
    normed, keyval, w_kv, sem = refs[-4:]
    copies = []
    for n, piece in enumerate(pieces):
        start = pl.multiple_of(rows[n], 16)
        copies.append(
            pltpu.make_async_copy(piece, w_kv.at[pl.ds(start, piece.shape[0])], sem.at[n])
        )
    for copy in copies:
        copy.start()
    inputs = tokens[...].astype(F32)
    normed[...] = (inputs * rms_factor(inputs) * gain[...]).astype(BF)
    for copy in copies:
        copy.wait()
    raw = dot(normed[...], w_kv[...])
    keyval[:, :HD] = rotate(raw[:, :HD], cosine[...], sine[...]).astype(BF)
    keyval[:, HD:] = raw[:, HD:].astype(BF)


def norm_back_rows(grad_normed, values, factor, gain):
    scaled = grad_normed * gain
    mean = jnp.mean(scaled * values, axis=-1, keepdims=True)
    return factor * scaled - values * (factor * factor * factor) * mean


def attend_kernel(n_q, n_o, spans, maps, *refs):
    normed, tokens, gain, bias, cosine, sine = refs[:6]
    blocks = refs[6 : 6 + spans]
    at = 6 + spans
    q_pieces, o_pieces = refs[at : at + n_q], refs[at + n_q : at + n_q + n_o]
    queries, attended, hidden, own_norm, factor = refs[at + n_q + n_o : at + n_q + n_o + 5]
    w_q, w_o, keys, values, total, q_sem, o_sem = refs[at + n_q + n_o + 5 :]
    step = pl.program_id(0)
    rows = normed.shape[0]

    @pl.when(step == 0)
    def _():
        first = load_rows(w_q, q_pieces, [maps[spans + n] for n in range(n_q)], q_sem)
        second = load_rows(w_o, o_pieces, [maps[spans + n_q + n] for n in range(n_o)], o_sem)
        for n in range(spans):
            keys[n * rows : (n + 1) * rows, :] = blocks[n][0, :, :HD]
            values[n * rows : (n + 1) * rows, :] = blocks[n][0, :, HD:]
        total[...] = tokens[...].astype(F32)
        for copy in first + second:
            copy.wait()

    columns = pl.ds(pl.multiple_of(step * 2 * HD, 2 * HD), 2 * HD)
    raw = dot(normed[...], w_q[:, columns])
    done = []
    for n in range(2):
        turned = rotate(raw[:, n * HD : (n + 1) * HD], cosine[...], sine[...])
        query = (turned * HD ** (-0.5)).astype(BF)
        queries[:, n * HD : (n + 1) * HD] = query
        scores = dot_t(query, keys[...]) + bias[...]
        weights = jnp.exp(scores - jnp.max(scores, axis=-1, keepdims=True))
        share = 1.0 / jnp.sum(weights, axis=-1, keepdims=True)
        done.append(dot((weights * share).astype(BF), values[...]).astype(BF))
    both = jnp.concatenate(done, axis=1)
    attended[...] = both
    total[...] += dot(both, w_o[columns, :])

    @pl.when(step == pl.num_programs(0) - 1)
    def _():
        out = total[...]
        hidden[...] = out
        scale = rms_factor(out)
        factor[...] = jnp.broadcast_to(scale, factor.shape)
        own_norm[...] = (out * scale * gain[...]).astype(BF)


def attend_back_kernel(n_o, spans, entry_count, maps, *refs):
    d_attn, queries, bias, cosine, sine = refs[:5]
    blocks = refs[5 : 5 + spans]
    pieces = refs[5 + spans : 5 + spans + n_o]
    d_raw, kept, sent = refs[5 + spans + n_o : 8 + spans + n_o]
    w_o, keys, values, d_keys, d_values, d_window, sem = refs[8 + spans + n_o :]
    step = pl.program_id(0)
    rows = d_attn.shape[0]

    @pl.when(step == 0)
    def _():
        base = spans + entry_count
        copies = load_rows(w_o, pieces, [maps[base + n] for n in range(n_o)], sem)
        for n in range(spans):
            keys[n * rows : (n + 1) * rows, :] = blocks[n][0, :, :HD]
            values[n * rows : (n + 1) * rows, :] = blocks[n][0, :, HD:]
        d_keys[...] = jnp.zeros_like(d_keys)
        d_values[...] = jnp.zeros_like(d_values)
        for copy in copies:
            copy.wait()

    w_rows = pl.ds(pl.multiple_of(step * 2 * HD, 2 * HD), 2 * HD)
    d_both = dot_t(d_attn[...], w_o[w_rows, :]).astype(BF)
    for n in range(2):
        query = queries[:, n * HD : (n + 1) * HD]
        d_out = d_both[:, n * HD : (n + 1) * HD]
        scores = dot_t(query, keys[...]) + bias[...]
        weights = jnp.exp(scores - jnp.max(scores, axis=-1, keepdims=True))
        soft = weights * (1.0 / jnp.sum(weights, axis=-1, keepdims=True))
        d_soft = dot_t(d_out, values[...])
        delta = jnp.sum(soft * d_soft, axis=-1, keepdims=True)
        d_scores = (soft * (d_soft - delta)).astype(BF)
        d_query = dot(d_scores, keys[...]) * HD ** (-0.5)
        d_raw[:, n * HD : (n + 1) * HD] = rotate(d_query, cosine[...], -sine[...]).astype(BF)
        d_keys[...] += t_dot(query, d_scores)
        d_values[...] += t_dot(d_out, soft.astype(BF))

    @pl.when(step == pl.num_programs(0) - 1)
    def _():
        d_window[: spans * rows, :HD] = d_keys[...].T.astype(BF)
        d_window[: spans * rows, HD:] = d_values[...].T.astype(BF)
        d_window[spans * rows :, :] = jnp.zeros((rows, 2 * HD), BF)
        for n in range(entry_count):
            out = kept if n < entry_count // 2 else sent
            start = pl.multiple_of(maps[spans + n] * rows, rows)
            out[n % (entry_count // 2)] = d_window[pl.ds(start, rows), :]


ROOT = math.sqrt(2.0 / math.pi)


def forward_kernel(n_tok, maps, *refs):
    pieces = refs[:n_tok]
    cot, w_gate, w_up, w_down = refs[n_tok : n_tok + 4]
    inner, inner_t, d_both, normed_t, normed, sem = refs[n_tok + 4 :]

    @pl.when(pl.program_id(0) == 0)
    def _():
        at = 0
        copies = []
        for n, piece in enumerate(pieces):
            copies.append(
                pltpu.make_async_copy(piece, normed.at[pl.ds(at, piece.shape[0])], sem.at[n])
            )
            at += piece.shape[0]
        for copy in copies:
            copy.start()
        for copy in copies:
            copy.wait()

    wide = normed_t.shape[0]
    columns = pl.ds(pl.multiple_of(pl.program_id(0) * wide, 128), wide)
    gate, up = dot(normed[...], w_gate[...]), dot(normed[...], w_up[...])
    d_inner = dot_t(cot[...], w_down[...])
    square = gate * gate
    bent = jnp.tanh(ROOT * (gate + 0.044715 * (square * gate)))
    half = 0.5 * (1.0 + bent)
    active = gate * half
    slope = half + 0.5 * gate * (1.0 - bent * bent) * (ROOT * (1.0 + 3 * 0.044715 * square))
    result = (active * up).astype(BF)
    inner[...] = result
    inner_t[...] = result.T
    d_both[0] = (d_inner * up * slope).astype(BF)
    d_both[1] = (d_inner * active).astype(BF)
    normed_t[...] = normed[:, columns].T


def cut_rows(result, picks, outs):
    for out, starts in zip(outs, picks, strict=True):
        rows = out.shape[1]
        for n, start in enumerate(starts):
            out[n] = result[start : start + rows].astype(BF)


def back_kernel(picks, d_both, w_gu, *outs):
    units = d_both.shape[2]
    result = dot_t(d_both[0], w_gu[:, :units]) + dot_t(d_both[1], w_gu[:, units:])
    cut_rows(result, picks, outs)


def down_kernel(picks, maps, inner, w_down, *outs):
    cut_rows(dot(inner[...], w_down[...]), picks, outs)


def grad_kernel(turned, groups, block_rows, added, maps, left, right, *refs):
    product = dot if turned else t_dot
    result = product(left[...], right[...].reshape(right.shape[-2:]))
    if added:
        result = result + refs[0][...].astype(F32)
    outs = refs[1:] if added else refs
    if groups is None:
        outs[0][...] = result.astype(BF)
        return
    total = outs[-1]
    total[...] = result
    place = 0
    for n, count in enumerate(groups):
        for k in range(count):
            start = pl.multiple_of(maps[2 + place] * block_rows, 16)
            outs[n][k] = total[pl.ds(start, block_rows), :].astype(BF)
            place += 1


def grad(
    left, left_block, left_columns, right, half, added=None, groups=None, order=None, turned=False
):
    tokens = left.shape[1 if turned else 0]
    if right.ndim == 3:
        columns = right.shape[2]
    else:
        columns = right.shape[1] // 2
    blocks = 0 if groups is None else sum(groups)
    block_rows = 0 if groups is None else left_columns // blocks
    if columns % 128 or left_columns % 128 or block_rows % 16:
        cut = lax.dynamic_slice_in_dim(
            left, left_block * left_columns, left_columns, 0 if turned else 1
        )
        if right.ndim == 3:
            other = pick(right, half, 0)
        else:
            other = lax.dynamic_slice_in_dim(right, half * columns, columns, 1)
        result = dot(cut, other) if turned else t_dot(cut, other)
        if added is not None:
            result = result + added.astype(F32)
        result = result.astype(BF)
        if groups is None:
            return result
        result = jnp.take(result.reshape(blocks, block_rows, columns), order, axis=0)
        outs, at = [], 0
        for count in groups:
            outs.append(result[at : at + count])
            at += count
        return outs
    wide = 384 if columns % 384 == 0 else (256 if columns % 256 == 0 else 128)
    steps = columns // wide
    maps = jnp.stack([jnp.asarray(left_block, jnp.int32), jnp.asarray(half, jnp.int32)])
    if groups is not None:
        maps = jnp.concatenate([maps, order.astype(jnp.int32)])
    if turned:
        in_specs = [pl.BlockSpec((left_columns, tokens), lambda i, maps: (maps[0], 0))]
    else:
        in_specs = [pl.BlockSpec((tokens, left_columns), lambda i, maps: (0, maps[0]))]
    if right.ndim == 3:
        in_specs.append(pl.BlockSpec((1, tokens, wide), lambda i, maps: (maps[1], 0, i)))
    else:
        in_specs.append(pl.BlockSpec((tokens, wide), lambda i, maps: (0, maps[1] * steps + i)))
    operands = [left, right]
    if added is not None:
        in_specs.append(pl.BlockSpec((left_columns, wide), lambda i, maps: (0, i)))
        operands.append(added)
    scratch = []
    if groups is None:
        shapes = [jax.ShapeDtypeStruct((left_columns, columns), BF)]
        out_specs = [pl.BlockSpec((left_columns, wide), lambda i, maps: (0, i))]
    else:
        shapes = [jax.ShapeDtypeStruct((count, block_rows, columns), BF) for count in groups]
        out_specs = [
            pl.BlockSpec((count, block_rows, wide), lambda i, maps: (0, 0, i)) for count in groups
        ]
        scratch = [pltpu.VMEM((left_columns, wide), F32)]
    outs = kernel_call(
        functools.partial(grad_kernel, turned, groups, block_rows, added is not None),
        grid_spec=pltpu.PrefetchScalarGridSpec(
            num_scalar_prefetch=1,
            grid=(steps,),
            in_specs=in_specs,
            out_specs=out_specs,
            scratch_shapes=scratch,
        ),
        out_shape=shapes,
    )(maps, *operands)
    return outs[0] if groups is None else outs


class Clock:
    def __init__(self):
        self.marks = ()

    def tie(self, value):
        return after(value, *self.marks) if self.marks else value

    def mark(self, *values):
        self.marks = values


PLAN = (
    "D",
    "W",
    "D",
    "back",
    "baW",
    "D",
    "down",
    "ae",
    "bO",
    "W",
    "a",
    "b",
    "hid",
    "D",
    "T",
    "att",
    "T",
    "QvOW",
    "Q",
    "D",
    "v",
    "T",
    "Oe",
    "v",
    "D",
    "Q",
    "T",
    "Wv",
    "T",
    "tok",
    "O",
    "eKT",
    "K",
    "WT",
    "DOK",
    "Tf",
    "KQ",
    "O",
    "KQ",
    "TQO",
    "fKW",
    "T",
    "K",
    "Q",
    "D",
    "K",
    "Q",
    "O",
    "W",
    "Q",
    "O",
    "Kf",
    "Q",
    "K",
)


def body(
    tokens,
    cotangent,
    lengths,
    block_of,
    gain_attn,
    w_query,
    w_keyval,
    w_out,
    gain_mlp,
    w_gateup,
    w_down,
):
    tok_rows, width = tokens.shape
    y_count, z_count = lax.axis_size("y"), lax.axis_size("z")
    ctx_count = 4 * z_count
    z_levels = z_count.bit_length() - 1
    x_at, c_at, y_at, z_at = (lax.axis_index(name) for name in ("x", "c", "y", "z"))
    own_index = (z_at * 2 + x_at) * 2 + c_at
    deep = w_query.shape[0]
    quarter = deep // 4
    units = FF // (2 * y_count)
    half_tok = tok_rows // 2
    group = 2 * y_count
    others = range(1, y_count)
    clock = Clock()
    tie, mark = clock.tie, clock.mark

    own_gains = jnp.zeros((16, deep), BF).at[0].set(gain_attn).at[1].set(gain_mlp)
    got_gains = [shift(own_gains, "y", r) for r in others]
    kv_weights = [w_keyval] + [shift(w_keyval, "y", r) for r in others]
    cot_x = shift(cotangent, "x", 1)
    place_cx = c_at * 2 + x_at
    place_cz = c_at * 2 + (z_at & 1)

    def rows_of(weight, place):
        return lax.dynamic_slice_in_dim(weight, place * quarter, quarter, 0)

    wq_piece = after(rows_of(w_query, place_cx), own_gains)
    wq_y = {r: shift(wq_piece, "y", r) for r in others}
    wo_piece = after(rows_of(w_out, place_cx), wq_piece)
    wo_y = {r: shift(wo_piece, "y", r) for r in others}
    gu_sent = {}
    for r in others:
        column = ((y_at ^ r) * 2 + x_at) * units
        moves = [
            (0, (quarter, units), (place_cz * quarter, part * FF + column), (0, part * units))
            for part in (0, 1)
        ]
        gu_sent[r] = lay_out((quarter, 2 * units), [after(w_gateup, wo_piece)], moves)

    def listed(shard, found, place):
        pieces, rows = [shard], [y_at * deep]
        for r, quarters in found.items():
            for s, piece in enumerate(quarters):
                pieces.append(piece)
                rows.append((y_at ^ r) * deep + (place ^ s) * quarter)
        return pieces, rows

    device_ids = jnp.arange(ctx_count, dtype=jnp.int32)
    block_row = block_of[0]
    own_block = jnp.sum(jnp.where(device_ids == own_index, block_row, 0))
    own_start = own_block * tok_rows
    owners = jnp.sum(
        jnp.where(block_row[None, :] == device_ids[:, None], device_ids[None, :], 0), axis=1
    )
    seq_lengths = lengths[0]
    query_places = own_start + jnp.arange(tok_rows, dtype=jnp.int32)
    key_places = own_start - WINDOW + jnp.arange(WINDOW + tok_rows, dtype=jnp.int32)
    query_segment, query_position = segment_info(query_places, seq_lengths)
    key_segment = segment_info(key_places, seq_lengths)[0]
    distance = query_places[:, None] - key_places[None, :]
    allowed = (
        (query_segment[:, None] == key_segment[None, :])
        & (key_places >= 0)[None, :]
        & (distance >= 0)
        & (distance < WINDOW)
    )
    bias = jnp.where(allowed, 0.0, -1e30).astype(F32)
    cosine, sine = tables(query_position, HD)
    cosine = jnp.concatenate([cosine, cosine], axis=1)
    sine = jnp.concatenate([-sine, sine], axis=1)
    spans = WINDOW // tok_rows + 1
    first_block = own_block - (spans - 1)

    def entry_of(ctx_index):
        differ = ctx_index ^ own_index
        return ((differ >> 1) & 1) | ((differ >> 2) << 1) | ((differ & 1) << (z_levels + 1))

    window = first_block + jnp.arange(spans, dtype=jnp.int32)
    window = entry_of(jnp.take(owners, jnp.clip(window, 0, ctx_count - 1)))
    entries = jnp.arange(ctx_count, dtype=jnp.int32)
    differ = ((entries >> 1) & (z_count - 1)) << 2
    differ = differ | ((entries & 1) << 1) | (entries >> (z_levels + 1))
    entry_block = jnp.take(block_row, differ ^ own_index) - first_block
    entry_block = jnp.where((entry_block >= 0) & (entry_block < spans), entry_block, spans)

    z_places = jnp.zeros((z_count,), jnp.int32)
    z_differ = jnp.arange(z_count, dtype=jnp.int32) ^ z_at
    for n, level in enumerate(reversed(range(z_levels))):
        z_places = z_places | (((z_differ >> level) & 1) << n)
    z_order = jnp.zeros((z_count,), jnp.int32)
    for level in range(z_levels):
        z_order = z_order | (
            ((jnp.arange(z_count, dtype=jnp.int32) >> (z_levels - 1 - level)) & 1) << level
        )
    z_order = z_order ^ z_at

    gains = by_place([own_gains[:2]] + [g[:2] for g in got_gains], "y")
    gains = jnp.swapaxes(gains, 0, 1).reshape(2, width).astype(F32)
    gain_one, gain_two = gains[:1], gains[1:]
    kv_rows = jnp.stack([(y_at ^ r) * deep for r in range(y_count)]).astype(jnp.int32)
    in_vmem = pl.BlockSpec(memory_space=pltpu.VMEM)
    normed, keyval = kernel_call(
        kv_kernel,
        in_specs=[pl.BlockSpec(memory_space=pltpu.SMEM)] + [in_vmem] * 4 + [ANY] * y_count,
        out_specs=[in_vmem, in_vmem],
        out_shape=[
            jax.ShapeDtypeStruct((tok_rows, width), BF),
            jax.ShapeDtypeStruct((tok_rows, 2 * HD), BF),
        ],
        scratch_shapes=[pltpu.VMEM((width, 2 * HD), BF), pltpu.SemaphoreType.DMA((y_count,))],
    )(kv_rows, tokens, gain_one, cosine, sine, *kv_weights)
    mark(keyval, bias, z_order, z_places, entry_block, window)
    held = stack_two(keyval[None], tie(shift(keyval, "x", 1)[None]))
    mark(held)
    over_z = [shift(held, "z", d) for d in range(1, z_count)]
    wq_y = {r: tie(piece) for r, piece in wq_y.items()}
    mark(*wq_y.values())
    wq_found = {r: [piece, shift(piece, "x", 1)] for r, piece in wq_y.items()}
    wo_y = {r: tie(piece) for r, piece in wo_y.items()}
    mark(*wo_y.values())
    cot_y = {r: shift(tie(cotangent), "y", r) for r in others}
    wq_found = {r: [pair[0], tie(pair[1])] for r, pair in wq_found.items()}
    mark(*[pair[1] for pair in wq_found.values()])
    wo_found = {r: [tie(piece), shift(tie(piece), "x", 1)] for r, piece in wo_y.items()}

    def stack_all(_, ins, outs):
        for n, part in enumerate(ins):
            outs[0][n * 2 : n * 2 + 2] = part[...]

    held = once(
        stack_all,
        [((2 * z_count, tok_rows, 2 * HD), BF)],
        held,
        *[tie(part) for part in over_z],
    )[0]
    mark(held)
    across = shift(held, "c", 1)
    wq_found = {r: pair + [shift(tie(p), "c", 1) for p in pair] for r, pair in wq_found.items()}
    cot_x = tie(cot_x)
    cot_corner_b = {r: shift(cot_x[half_tok:], "y", r) for r in others}
    gu_y = {r: shift(tie(piece), "y", r) for r, piece in gu_sent.items()}
    wo_found = {r: [pair[0], tie(pair[1])] for r, pair in wo_found.items()}
    mark(*[pair[1] for pair in wo_found.values()])
    wo_found = {r: pair + [shift(tie(p), "c", 1) for p in pair] for r, pair in wo_found.items()}
    cot_y = {r: tie(part) for r, part in cot_y.items()}
    cot_slices = {r: part[:half_tok] for r, part in cot_y.items()}
    mark(*cot_slices.values())
    cot_corner_a = {r: shift(part, "x", 1) for r, part in cot_slices.items()}

    all_kv = stack_two(held, tie(across))
    q_pieces, q_rows = listed(w_query, wq_found, place_cx)
    o_pieces, o_rows = listed(w_out, wo_found, place_cx)
    n_q, n_o = len(q_pieces), len(o_pieces)
    pairs = H // 2
    kv_specs = [
        pl.BlockSpec((1, tok_rows, 2 * HD), lambda i, maps, n=n: (maps[n], 0, 0))
        for n in range(spans)
    ]
    pair_spec = pl.BlockSpec((tok_rows, 2 * HD), lambda i, maps: (0, i))
    token_spec = pl.BlockSpec((tok_rows, width), lambda i, maps: (0, 0))
    maps = jnp.concatenate([window, jnp.stack(q_rows + o_rows).astype(jnp.int32)])
    small = [gain_two, bias, cosine, sine]
    queries, attended, hidden, own_norm, factor = kernel_call(
        functools.partial(attend_kernel, n_q, n_o, spans),
        grid_spec=pltpu.PrefetchScalarGridSpec(
            num_scalar_prefetch=1,
            grid=(pairs,),
            in_specs=[token_spec, token_spec]
            + [whole_spec(a) for a in small]
            + kv_specs
            + [ANY] * (n_q + n_o),
            out_specs=[
                pair_spec,
                pair_spec,
                token_spec,
                token_spec,
                pl.BlockSpec((tok_rows, HD), lambda i, maps: (0, 0)),
            ],
            scratch_shapes=[
                pltpu.VMEM((width, H * HD), BF),
                pltpu.VMEM((H * HD, width), BF),
                pltpu.VMEM((spans * tok_rows, HD), BF),
                pltpu.VMEM((spans * tok_rows, HD), BF),
                pltpu.VMEM((tok_rows, width), F32),
                pltpu.SemaphoreType.DMA((n_q,)),
                pltpu.SemaphoreType.DMA((n_o,)),
            ],
        ),
        out_shape=[
            jax.ShapeDtypeStruct((tok_rows, H * HD), BF),
            jax.ShapeDtypeStruct((tok_rows, H * HD), BF),
            jax.ShapeDtypeStruct((tok_rows, width), F32),
            jax.ShapeDtypeStruct((tok_rows, width), BF),
            jax.ShapeDtypeStruct((tok_rows, HD), F32),
        ],
    )(maps, normed, tokens, *small, *([all_kv] * spans), *q_pieces, *o_pieces)
    mark(own_norm)

    norm_y = {r: shift(own_norm, "y", r) for r in others}
    norm_x = shift(own_norm, "x", 1)
    gu_z = {r: shift(tie(piece), "z", 1) for r, piece in gu_y.items()}
    norm_slices = {r: tie(part)[:half_tok] for r, part in norm_y.items()}
    norm_slice = tie(norm_x)[half_tok:]
    mark(norm_slice, *norm_slices.values())
    norm_a = {r: shift(part, "x", 1) for r, part in norm_slices.items()}
    norm_b = {r: shift(norm_slice, "y", r) for r in others}
    cot_parts = [cotangent, *[cot_y[r] for r in others], cot_x]
    norm_parts = [own_norm, *[norm_y[r] for r in others], norm_x]
    for r in others:
        cot_parts += [cot_corner_a[r], cot_corner_b[r]]
        norm_parts += [norm_a[r], norm_b[r]]
    cot_all = jnp.concatenate([tie(part) for part in cot_parts], axis=0)
    gu_found = {r: [gu_y[r], tie(gu_z[r])] for r in others}
    gu_found = {r: pair + [shift(tie(p), "c", 1) for p in pair] for r, pair in gu_found.items()}
    gu_moves = [
        (0, (deep, units), (0, part * FF + (y_at * 2 + x_at) * units), (y_at * deep, part * units))
        for part in (0, 1)
    ]
    gu_pieces, gu_rows = listed(w_gateup, gu_found, place_cz)
    for n in range(1, len(gu_pieces)):
        gu_moves.append((n, (quarter, 2 * units), (0, 0), (gu_rows[n], 0)))
    w_gu = lay_out((width, 2 * units), gu_pieces, gu_moves)
    many = group * tok_rows
    fits = units % 128 == 0
    picks = [
        [r * tok_rows for r in range(y_count)],
        [(y_count + r) * tok_rows for r in range(y_count)],
        [half_tok, y_count * tok_rows + half_tok],
    ]
    picks += [[r * tok_rows + half_tok, (y_count + r) * tok_rows + half_tok] for r in others]
    cut_shapes = [jax.ShapeDtypeStruct((len(pick_), half_tok, width), BF) for pick_ in picks]
    x_maps = jnp.stack([x_at]).astype(jnp.int32)

    def cut(result):
        return [
            jnp.stack([result[start : start + half_tok].astype(BF) for start in starts])
            for starts in picks
        ]

    if fits:
        wide = 384 if units % 384 == 0 else 128
        steps = units // wide
        turn = width // steps
        block = 512
        cut_specs = [
            pl.BlockSpec((len(starts), half_tok, block), lambda i, *_: (0, 0, i))
            for starts in picks
        ]
        n_tok = len(norm_parts)
        inner_act, inner_t, d_both, normed_t = kernel_call(
            functools.partial(forward_kernel, n_tok),
            grid_spec=pltpu.PrefetchScalarGridSpec(
                num_scalar_prefetch=1,
                grid=(steps,),
                in_specs=[ANY] * n_tok
                + [
                    pl.BlockSpec((many, width), lambda i, maps: (0, 0)),
                    pl.BlockSpec((width, wide), lambda i, maps: (0, i)),
                    pl.BlockSpec((width, wide), lambda i, maps: (0, steps + i)),
                    pl.BlockSpec((wide, width), lambda i, maps: (maps[0] * steps + i, 0)),
                ],
                out_specs=[
                    pl.BlockSpec((many, wide), lambda i, maps: (0, i)),
                    pl.BlockSpec((wide, many), lambda i, maps: (i, 0)),
                    pl.BlockSpec((2, many, wide), lambda i, maps: (0, 0, i)),
                    pl.BlockSpec((turn, many), lambda i, maps: (i, 0)),
                ],
                scratch_shapes=[
                    pltpu.VMEM((many, width), BF),
                    pltpu.SemaphoreType.DMA((n_tok,)),
                ],
            ),
            out_shape=[
                jax.ShapeDtypeStruct((many, units), BF),
                jax.ShapeDtypeStruct((units, many), BF),
                jax.ShapeDtypeStruct((2, many, units), BF),
                jax.ShapeDtypeStruct((width, many), BF),
            ],
        )(x_maps, *norm_parts, cot_all, w_gu, w_gu, w_down)

        def back_cut():
            return kernel_call(
                functools.partial(back_kernel, picks),
                grid=(width // block,),
                in_specs=[
                    whole_spec(d_both),
                    pl.BlockSpec((block, 2 * units), lambda i: (i, 0)),
                ],
                out_specs=cut_specs,
                out_shape=cut_shapes,
            )(tie(d_both), w_gu)

        def down_cut():
            return kernel_call(
                functools.partial(down_kernel, picks),
                grid_spec=pltpu.PrefetchScalarGridSpec(
                    num_scalar_prefetch=1,
                    grid=(width // block,),
                    in_specs=[
                        pl.BlockSpec((many, units), lambda i, maps: (0, 0)),
                        pl.BlockSpec((units, block), lambda i, maps: (maps[0], i)),
                    ],
                    out_specs=cut_specs,
                ),
                out_shape=cut_shapes,
            )(x_maps, tie(inner_act), w_down)

    else:
        normed2 = jnp.concatenate(norm_parts, axis=0)
        w_dn = lax.dynamic_slice_in_dim(w_down, x_at * units, units, 0)
        d_inner = dot_t(cot_all, w_dn)
        both_parts = dot(normed2, w_gu)
        active, back = jax.vjp(
            lambda values: jax.nn.gelu(values, approximate=True), both_parts[:, :units]
        )
        up_part = both_parts[:, units:]
        inner_act = (active * up_part).astype(BF)
        d_both = jnp.stack([back(d_inner * up_part)[0], d_inner * active]).astype(BF)
        inner_t, normed_t = inner_act.T, normed2.T

        def back_cut():
            both = tie(d_both)
            return cut(dot_t(both[0], w_gu[:, :units]) + dot_t(both[1], w_gu[:, units:]))

        def down_cut():
            return cut(dot(tie(inner_act), w_dn))

    mark(d_both)

    def back_a(cuts_in, result):
        keep, send = cuts_in[0], cuts_in[1]
        got = yield [(send, "x", 1)]

        def function(_, ins, outs):
            for n in range(y_count):
                outs[n][...] = (ins[0][n].astype(F32) + ins[1][n].astype(F32)).astype(BF)

        left = once(function, [((half_tok, width), BF)] * y_count, keep, got[0])
        got = yield [(left[r], "y", r) for r in others]
        result.append([left[0]] + got)

    def back_b(cuts_in, result):
        keep, send = cuts_in[2], cuts_in[3:]
        got = yield [(part, "y", r) for r, part in zip(others, send, strict=True)]

        def function(_, ins, outs):
            for n in range(2):
                outs[n][...] = sum(ref[n].astype(F32) for ref in ins).astype(BF)

        left = once(function, [((half_tok, width), BF)] * 2, keep, *got)
        got = yield [(left[1], "x", 1)]
        result.append([left[0]] + got)

    def sum_rows(ins, n_first):
        first = sum(ref[...].astype(F32) for ref in ins[:n_first])
        second = sum(ref[...].astype(F32) for ref in ins[n_first : n_first + 2])
        return jnp.concatenate([first, second], axis=0)

    def scatter_z(kept, sent):
        for level in range(z_levels):
            got = yield [(sent, "z", 1 << level)]
            sums = add_halves(kept, got[0])
            kept, sent = sums[0], sums[-1]
        return kept

    def spread(piece, finish, split=True):
        held = piece
        for level in reversed(range(z_levels)):
            got = yield [(held, "z", 1 << level)]
            held = stack_two(held, got[0])
        beside, across = yield [(held, "x", 1), (held, "c", 1)]
        corner = yield [(beside, "c", 1)]
        if split:
            mark(finish([tie(held), across], False))
            mark(finish([tie(beside), corner[0]], True))
        else:
            mark(finish([tie(held), beside, across, corner[0]], False))

    z_groups = [z_count // 2, z_count // 2]

    found = {}

    def finish_down(parts, beside):
        found["down"] = widen(
            parts,
            beside,
            z_places,
            (w_down.shape[0], width),
            lambda z, c, x, y: (x * z_count + z, c),
            found.get("down"),
        )
        return found["down"]

    def finish_up(r):
        def finish(parts, beside):
            found["up"] = widen(
                parts,
                beside,
                z_places,
                (deep, 2 * FF),
                lambda z, c, x, y: (z, (c * y_count + (y ^ r)) * 2 + x),
                found.get("up"),
            )
            return found["up"]

        return finish

    def finish_attn(name, columns):
        def finish(parts, beside):
            found[name] = widen(
                parts, beside, z_places, (deep, columns), lambda z, c, x, y: (z * 2 + x, c)
            )
            return found[name]

        return finish

    def ffn_chain(job, finish, r):
        left, left_block, left_rows, right = job
        theirs = grad(tie(left), left_block, left_rows, right, 1 - c_at, turned=True)
        got = yield [(theirs, "c", 1)]
        kept, sent = grad(
            left, left_block, left_rows, right, c_at, got[0], z_groups, z_order, turned=True
        )
        piece = yield from scatter_z(kept, sent)
        if r:
            got = yield [(piece, "y", r)]
            piece = got[0]
        yield from spread(piece, finish)

    y_order = jnp.arange(y_count, dtype=jnp.int32) ^ y_at
    xz_maps = jnp.concatenate([z_order * 2 + x_at, z_order * 2 + (1 - x_at)])

    def attn_chain(left, right, finish, column=None):
        cols = right.shape[1] // 2
        theirs = grad(tie(left), 0, width, right, 1 - c_at)
        if column is not None:
            lane = jnp.arange(HD) == 0
            own = jnp.where(c_at == 0, column[0], column[1]).reshape(width, 1)
            other = jnp.where(c_at == 0, column[1], column[0]).reshape(width, 1)
            theirs = jnp.concatenate([theirs, jnp.where(lane, other, 0).astype(BF)], axis=1)
        got = yield [(theirs, "c", 1)]
        got = got[0]
        parts = grad(left, 0, width, right, c_at, got[:, :cols], [1] * y_count, y_order)
        parts = [part[0] for part in parts]
        if column is not None:
            extra = add(jnp.where(lane, own, 0), got[:, cols:]).reshape(y_count, deep, HD)
            parts = [
                jnp.concatenate([part, pick(extra, y_at ^ r, 0)], axis=1)
                for r, part in enumerate(parts)
            ]
        got = yield [(part, "y", r) for r, part in zip(others, parts[1:], strict=True)]
        cols = parts[0].shape[1]
        rows = deep // (2 * z_count)
        if rows % 16:
            total = sum(v.astype(F32) for v in [parts[0]] + got).astype(BF)
            blocks = jnp.take(total.reshape(2 * z_count, rows, cols), xz_maps, axis=0)
            kept, sent = blocks[:z_count], blocks[z_count:]
        else:

            def function(maps, ins, outs):
                for n in range(2 * z_count):
                    block = pl.ds(pl.multiple_of(maps[n] * rows, 16), rows)
                    total = sum(ref[block, :].astype(F32) for ref in ins)
                    outs[n // z_count][n % z_count] = total.astype(BF)

            kept, sent = once(
                function, [((z_count, rows, cols), BF)] * 2, parts[0], *got, maps=xz_maps
            )
        got = yield [(sent, "x", 1)]
        sums = add_halves(kept, got[0])
        piece = yield from scatter_z(sums[0], sums[1])
        yield from spread(piece, finish, split=False)

    chains, pending = {}, {}

    def advance(names):
        names = [name for name in names.split() if chains.get(name) is not None]
        waited = [part for name in names for part in pending.get(name, [])]
        if waited:
            waited = list(lax.optimization_barrier(tuple(waited) + clock.marks))[: len(waited)]
            mark(*waited)
        for name in names:
            count = len(pending.get(name, []))
            got, waited = waited[:count], waited[count:]
            try:
                if name in pending:
                    got = list(lax.optimization_barrier(tuple(got) + clock.marks))[: len(got)]
                    sends = chains[name].send(got)
                else:
                    sends = [(tie(part), axis, mask) for part, axis, mask in next(chains[name])]
            except StopIteration:
                chains[name] = None
                continue
            mark(*[part for part, _, _ in sends])
            pending[name] = [shift(*send) for send in sends]

    d_result, out_result = [], []
    jobs = [
        ffn_chain((normed_t, y_at ^ r, deep, d_both), finish_up(r), r) for r in list(others) + [0]
    ]
    ups = [f"U{r}" for r in others]
    for name, chain in zip(ups + ["W"], jobs, strict=True):
        chains[name] = chain
    first_up = " ".join(ups)
    chains["D"] = ffn_chain((inner_t, 0, units, cot_all), finish_down, 0)

    def do_back():
        d_cut = back_cut()
        mark(*d_cut)
        chains["a"], chains["b"] = back_a(d_cut, d_result), back_b(d_cut, d_result)

    def do_down():
        out_cut = down_cut()
        mark(*out_cut)
        chains["e"], chains["f"] = back_a(out_cut, out_result), back_b(out_cut, out_result)

    def hidden_back(_, ins, outs):
        grads = sum_rows(ins, y_count)
        values, scale, upstream, gain = (ref[...] for ref in ins[y_count + 2 :])
        scale = scale[:, :1]
        back = upstream.astype(F32) + norm_back_rows(grads, values, scale, gain)
        outs[0][...] = back
        outs[1][...] = back.astype(BF)
        outs[2][...] = jnp.sum(grads * values * scale, axis=0, keepdims=True)

    def do_hidden():
        found["d_hidden"], found["d_attn"], found["d_gain_mlp"] = once(
            hidden_back,
            [((tok_rows, width), F32), ((tok_rows, width), BF), ((1, width), F32)],
            *[tie(part) for found_part in d_result for part in found_part],
            hidden,
            factor,
            cotangent,
            gain_two,
        )
        mark(found["d_attn"], found["d_gain_mlp"])
        chains["T"] = attn_chain(attended, found["d_attn"], finish_attn("out", width))

    maps = jnp.concatenate([window, entry_block, jnp.stack(o_rows).astype(jnp.int32)])
    entry_spec = pl.BlockSpec((ctx_count // 2, tok_rows, 2 * HD), lambda i, maps: (0, 0, 0))
    entry_shape = jax.ShapeDtypeStruct((ctx_count // 2, tok_rows, 2 * HD), BF)
    small = [bias, cosine, sine]
    def do_attention():
        found["d_raw"], found["d_kept"], found["d_sent"] = kernel_call(
            functools.partial(attend_back_kernel, n_o, spans, ctx_count),
            grid_spec=pltpu.PrefetchScalarGridSpec(
                num_scalar_prefetch=1,
                grid=(pairs,),
                in_specs=[token_spec, pair_spec]
                + [whole_spec(a) for a in small]
                + kv_specs
                + [ANY] * n_o,
                out_specs=[pair_spec, entry_spec, entry_spec],
                scratch_shapes=[
                    pltpu.VMEM((H * HD, width), BF),
                    pltpu.VMEM((spans * tok_rows, HD), BF),
                    pltpu.VMEM((spans * tok_rows, HD), BF),
                    pltpu.VMEM((HD, spans * tok_rows), F32),
                    pltpu.VMEM((HD, spans * tok_rows), F32),
                    pltpu.VMEM(((spans + 1) * tok_rows, 2 * HD), BF),
                    pltpu.SemaphoreType.DMA((n_o,)),
                ],
            ),
            out_shape=[jax.ShapeDtypeStruct((tok_rows, H * HD), BF), entry_shape, entry_shape],
        )(maps, tie(found["d_attn"]), queries, *small, *([all_kv] * spans), *o_pieces)
        mark(found["d_sent"])
        chains["Q"] = attn_chain(normed, found["d_raw"], finish_attn("query", width))
        chains["v"] = kv_back(kv_result)

    def kv_back(result):
        got = yield [(found["d_sent"], "c", 1)]

        def first(_, ins, outs):
            for n in range(2 * z_count):
                outs[n % 2][n // 2] = (ins[0][n].astype(F32) + ins[1][n].astype(F32)).astype(BF)

        shape = ((z_count, tok_rows, 2 * HD), BF)
        kept, sent = once(first, [shape, shape], found["d_kept"], got[0])
        got = yield [(sent, "x", 1)]

        def second(_, ins, outs):
            for n in range(z_count):
                outs[n][...] = (ins[0][n].astype(F32) + ins[1][n].astype(F32)).astype(BF)

        left = once(second, [((tok_rows, 2 * HD), BF)] * z_count, kept, got[0])
        got = yield [(left[d], "z", d) for d in range(1, z_count)]
        result += [left[0]] + got

    kv_result = []
    def tokens_kernel(maps, *refs):
        n_kv = y_count
        d_raw, cosine_ref, sine_ref, tokens_ref, gain, back_hidden = refs[:6]
        parts = refs[6 : 6 + z_count]
        kv_pieces = refs[6 + z_count : 6 + z_count + n_kv]
        pieces = refs[6 + z_count + n_kv : 6 + z_count + n_kv + n_q]
        outs = refs[6 + z_count + n_kv + n_q :]
        d_kv, back, d_gain, whole_q, whole_kv, q_sem, kv_sem = outs
        copies = load_rows(whole_q, pieces, [maps[n] for n in range(n_q)], q_sem)
        copies += load_rows(whole_kv, kv_pieces, [maps[n_q + n] for n in range(n_kv)], kv_sem)
        total = sum(ref[...].astype(F32) for ref in parts)
        d_kv[:, :HD] = rotate(total[:, :HD], cosine_ref[...], -sine_ref[...]).astype(BF)
        d_kv[:, HD:] = total[:, HD:].astype(BF)
        inputs = tokens_ref[...].astype(F32)
        scale = rms_factor(inputs)
        for copy in copies:
            copy.wait()
        grads = dot_t(d_raw[...], whole_q[...]) + dot_t(d_kv[...], whole_kv[...])
        back[...] = back_hidden[...] + norm_back_rows(grads, inputs, scale, gain[...])
        d_gain[...] = jnp.sum(grads * inputs * scale, axis=0, keepdims=True)

    q_maps = jnp.concatenate([jnp.stack(q_rows).astype(jnp.int32), kv_rows])
    def do_tokens():
        d_kv_raw, found["tokens"], d_gain = kernel_call(
            tokens_kernel,
            in_specs=[pl.BlockSpec(memory_space=pltpu.SMEM)]
            + [in_vmem] * (6 + z_count)
            + [ANY] * (y_count + n_q),
            out_specs=[in_vmem] * 3,
            out_shape=[
                jax.ShapeDtypeStruct((tok_rows, 2 * HD), BF),
                jax.ShapeDtypeStruct((tok_rows, width), F32),
                jax.ShapeDtypeStruct((1, width), F32),
            ],
            scratch_shapes=[
                pltpu.VMEM((width, H * HD), BF),
                pltpu.VMEM((width, 2 * HD), BF),
                pltpu.SemaphoreType.DMA((n_q,)),
                pltpu.SemaphoreType.DMA((y_count,)),
            ],
        )(
            q_maps,
            found["d_raw"],
            cosine,
            sine,
            tokens,
            gain_one,
            found["d_hidden"],
            *[tie(part) for part in kv_result],
            *kv_weights,
            *q_pieces,
        )
        mark(d_kv_raw, d_gain, found["tokens"])
        chains["K"] = attn_chain(
            normed, d_kv_raw, finish_attn("keyval", 4 * HD), (d_gain, found["d_gain_mlp"])
        )

    works = {
        "back": do_back,
        "down": do_down,
        "hid": do_hidden,
        "att": do_attention,
        "tok": do_tokens,
    }
    for entry in PLAN:
        if entry in works:
            works[entry]()
        else:
            advance(" ".join(first_up if letter == "O" else letter for letter in entry))
    while any(chain is not None for chain in chains.values()):
        advance(" ".join(chains))

    def finish_output(_, ins, outs):
        outs[0][...] = (ins[-1][...] + sum_rows(ins, y_count)).astype(BF)

    block_output = once(
        finish_output, [((tok_rows, width), BF)], *[part for found_part in out_result for part in found_part], hidden
    )[0]
    last = found["keyval"]
    grad_keyval = jnp.concatenate([last[:, :HD], last[:, 2 * HD : 3 * HD]], axis=1)
    return (
        block_output,
        found["tokens"],
        last[:, HD],
        found["query"],
        grad_keyval,
        found["out"],
        last[:, 3 * HD],
        found["up"],
        found["down"],
    )


def solution(mesh):
    ctx_count, y_count = mesh.shape["ctx"], mesh.shape["fsdp"]
    fine = Mesh(mesh.devices.reshape(ctx_count // 4, 2, 2, y_count), ("z", "x", "c", "y"))
    rows, shard = P(("z", "x", "c", "y"), None), P("y", None)
    in_specs = (rows, rows, shard, shard, P("y"), shard, shard, shard, P("y"), shard, shard)
    out_specs = (rows, rows, P("y"), shard, shard, shard, P("y"), shard, shard)
    return jax.shard_map(body, mesh=fine, in_specs=in_specs, out_specs=out_specs, check_vma=False)
```

```python
import functools
import math

import jax
import jax.numpy as jnp
from jax import lax
from jax.experimental import pallas as pl
from jax.experimental.pallas import tpu as pltpu
from jax.sharding import Mesh
from jax.sharding import PartitionSpec as P

H = 12
HD = 128
FF = 4608
WINDOW = 1024
EPSILON = 1e-06
BF = jnp.bfloat16
F32 = jnp.float32
VMEM_LIMIT = 48 * 1024 * 1024


def tables(places, width):
    half_width = width // 2
    frequency = jnp.exp(
        jnp.arange(half_width, dtype=jnp.float32) * (-2.0 * math.log(10000.0) / width)
    )
    angles = places.astype(jnp.float32)[:, None] * frequency[None, :]
    return (jnp.cos(angles), jnp.sin(angles))


def rotate(values, cosine, sine):
    turned = jnp.concatenate([values[:, HD // 2 :], values[:, : HD // 2]], axis=1)
    return values * cosine + turned * sine


def rms_factor(values):
    return lax.rsqrt(jnp.mean(values * values, axis=-1, keepdims=True) + EPSILON)


def segment_info(places, seq_lengths):
    seq_ends = jnp.cumsum(seq_lengths)
    passed = places[:, None] >= seq_ends[None, :]
    segment = jnp.sum(passed.astype(jnp.int32), axis=1)
    seq_start = jnp.sum(jnp.where(passed, seq_lengths[None, :], 0), axis=1)
    return (segment, places - seq_start)


def dot(a, b):
    return jnp.dot(a, b, preferred_element_type=F32)


def dot_t(a, b):
    return lax.dot_general(a, b, (((1,), (1,)), ((), ())), preferred_element_type=F32)


def t_dot(a, b):
    return lax.dot_general(a, b, (((0,), (0,)), ((), ())), preferred_element_type=F32)


def after(value, *earlier):
    return lax.optimization_barrier((value,) + earlier)[0]


def shift(array, axis, mask):
    return lax.ppermute(array, axis, [(i, i ^ mask) for i in range(lax.axis_size(axis))])


def bit(axis, k=0):
    return (lax.axis_index(axis) >> k) & 1


def pick(array, index, dim):
    return lax.dynamic_index_in_dim(array, index, dim, keepdims=False)


def add(a, b):
    return (a.astype(F32) + b.astype(F32)).astype(BF)


def by_place(entries, axis_name):
    if len(entries) == 2:
        low, high = jnp.stack(entries), jnp.stack(entries[::-1])
        return jnp.where(lax.axis_index(axis_name) == 0, low, high)
    order = jnp.arange(len(entries), dtype=jnp.int32) ^ lax.axis_index(axis_name)
    return jnp.take(jnp.stack(entries), order, axis=0)


def kernel_call(function, **options):
    return pl.pallas_call(
        function,
        compiler_params=pltpu.CompilerParams(vmem_limit_bytes=VMEM_LIMIT),
        cost_estimate=pl.CostEstimate(flops=1000, bytes_accessed=1000, transcendentals=0),
        **options,
    )


def whole_spec(array):
    zeros = (0,) * array.ndim
    return pl.BlockSpec(array.shape, lambda *_: zeros)


ANY = pl.BlockSpec(memory_space=pl.ANY)


def load_rows(target, pieces, rows, sem):
    copies = []
    for n, piece in enumerate(pieces):
        start = pl.multiple_of(rows[n], 16)
        copies.append(
            pltpu.make_async_copy(piece, target.at[pl.ds(start, piece.shape[0])], sem.at[n])
        )
    for copy in copies:
        copy.start()
    return copies


def copy_kernel(blocks, spots, *refs):
    parts, out, sem = refs[:-2], refs[-2], refs[-1]
    copies = []
    for n, (part, rows, columns) in enumerate(blocks):
        at = [pl.multiple_of(spots[n, 0], 16), pl.multiple_of(spots[n, 1], 128)]
        to = [pl.multiple_of(spots[n, 2], 16), pl.multiple_of(spots[n, 3], 128)]
        copies.append(
            pltpu.make_async_copy(
                parts[part].at[pl.ds(at[0], rows), pl.ds(at[1], columns)],
                out.at[pl.ds(to[0], rows), pl.ds(to[1], columns)],
                sem.at[n],
            )
        )
    for copy in copies:
        copy.start()
    for copy in copies:
        copy.wait()


def lay_out(shape, parts, moves):
    aligned = all(size[0] % 16 == 0 and size[1] % 128 == 0 for _, size, _, _ in moves)
    if not aligned:
        out = jnp.zeros(shape, parts[0].dtype)
        for part, size, at, to in moves:
            out = lax.dynamic_update_slice(out, lax.dynamic_slice(parts[part], at, size), to)
        return out
    spots = jnp.stack(
        [jnp.stack([jnp.asarray(v, jnp.int32) for v in at + to]) for _, _, at, to in moves]
    )
    blocks = tuple((part,) + size for part, size, _, _ in moves)
    return kernel_call(
        functools.partial(copy_kernel, blocks),
        out_shape=jax.ShapeDtypeStruct(shape, parts[0].dtype),
        in_specs=[pl.BlockSpec(memory_space=pltpu.SMEM)] + [ANY] * len(parts),
        out_specs=pl.BlockSpec(memory_space=pltpu.VMEM),
        scratch_shapes=[pltpu.SemaphoreType.DMA((len(moves),))],
    )(spots, *parts)


def widen_kernel(count, maps, *refs):
    parts, out = refs[:count], refs[-1]
    source = pl.program_id(0) ^ maps[0]
    z_count, rows, columns = parts[0].shape
    lead = out.shape[0] == 1
    for n in range(count):

        @pl.when(source == n)
        def _(n=n):
            for z in range(z_count):
                block = parts[n][maps[3 + z]].astype(F32)
                if lead:
                    out[0, z] = block
                else:
                    out[z, 0] = block


def widen(parts, beside, z_places, out_shape, spot, so_far=None, column=0, columns=None):
    count = len(parts)
    z_count, rows = parts[0].shape[:2]
    columns = columns or parts[0].shape[2]
    x_at, c_at, y_at = (lax.axis_index(name) for name in ("x", "c", "y"))
    if count == 2:
        flips = [c_at, x_at ^ (1 if beside else 0), y_at]
    else:
        flips = [c_at * 2 + x_at, x_at, y_at]
    z_first = spot(0, 0, 0)[0] is None
    size = (z_count, 1) if z_first else (1, z_count)
    flat = (out_shape[0] * out_shape[1] * out_shape[2], out_shape[3])
    if columns % 128 or rows % 16:
        out = jnp.zeros(out_shape, F32) if so_far is None else so_far.reshape(out_shape)
        ordered = jnp.stack(parts)[..., column * columns : (column + 1) * columns]
        for k in range(count):
            block = jnp.take(ordered[k ^ flips[0]], z_places, axis=0)
            c, x = (k, flips[1]) if count == 2 else (k // 2, k % 2)
            at = [0 if v is None else v for v in spot(c, x, y_at)]
            block = block.reshape(size + (rows, columns)).astype(F32)
            out = lax.dynamic_update_slice(out, block, (at[0], at[1], 0, at[2] * columns))
        return out.reshape(flat)
    maps = jnp.concatenate([jnp.stack(flips).astype(jnp.int32), z_places])

    def out_map(k, maps):
        at = spot(k, maps[1], maps[2]) if count == 2 else spot(k // 2, k % 2, maps[2])
        at = [0 if v is None else v for v in at]
        return (at[0], at[1], 0, at[2])

    specs = [pl.BlockSpec((z_count, rows, columns), lambda k, maps: (0, 0, column))] * count
    operands = list(parts)
    aliases = {}
    if so_far is not None:
        specs.append(ANY)
        operands.append(so_far.reshape(out_shape))
        aliases = {count + 1: 0}
    return kernel_call(
        functools.partial(widen_kernel, count),
        grid_spec=pltpu.PrefetchScalarGridSpec(
            num_scalar_prefetch=1,
            grid=(count,),
            in_specs=specs,
            out_specs=pl.BlockSpec(size + (rows, columns), out_map),
        ),
        out_shape=jax.ShapeDtypeStruct(out_shape, F32),
        input_output_aliases=aliases,
    )(maps, *operands).reshape(flat)


def once_kernel(function, n_in, maps, *refs):
    function(maps, refs[:n_in], refs[n_in:])


def once(function, shapes, *operands, maps=None):
    if maps is None:
        maps = jnp.zeros((1,), jnp.int32)
    return kernel_call(
        functools.partial(once_kernel, function, len(operands)),
        in_specs=[pl.BlockSpec(memory_space=pltpu.SMEM)]
        + [pl.BlockSpec(memory_space=pltpu.VMEM)] * len(operands),
        out_specs=[pl.BlockSpec(memory_space=pltpu.VMEM)] * len(shapes),
        out_shape=[jax.ShapeDtypeStruct(shape, kind) for shape, kind in shapes],
    )(maps, *operands)


def add_halves(kept, got):
    half = kept.shape[0] // 2
    if not half:

        def narrow(_, ins, outs):
            outs[0][...] = (ins[0][...].astype(F32) + ins[1][...].astype(F32)).astype(BF)

        return once(narrow, [(kept.shape, BF)], kept, got)

    def function(_, ins, outs):
        for n in range(2):
            part = pl.ds(n * half, half)
            outs[n][...] = (ins[0][part].astype(F32) + ins[1][part].astype(F32)).astype(BF)

    shape = ((half,) + kept.shape[1:], BF)
    return once(function, [shape, shape], kept, got)


def stack_two(held, got):
    count = held.shape[0]

    def function(_, ins, outs):
        outs[0][:count] = ins[0][...]
        outs[0][count:] = ins[1][...]

    return once(function, [((2 * count,) + held.shape[1:], BF)], held, got)[0]


def kv_kernel(rows, tokens, gain, cosine, sine, *refs):
    pieces = refs[:-4]
    normed, keyval, w_kv, sem = refs[-4:]
    copies = []
    for n, piece in enumerate(pieces):
        start = pl.multiple_of(rows[n], 16)
        copies.append(
            pltpu.make_async_copy(piece, w_kv.at[pl.ds(start, piece.shape[0])], sem.at[n])
        )
    for copy in copies:
        copy.start()
    inputs = tokens[...].astype(F32)
    normed[...] = (inputs * rms_factor(inputs) * gain[...]).astype(BF)
    for copy in copies:
        copy.wait()
    raw = dot(normed[...], w_kv[...])
    keyval[:, :HD] = rotate(raw[:, :HD], cosine[...], sine[...]).astype(BF)
    keyval[:, HD:] = raw[:, HD:].astype(BF)


def norm_back_rows(grad_normed, values, factor, gain):
    scaled = grad_normed * gain
    mean = jnp.mean(scaled * values, axis=-1, keepdims=True)
    return factor * scaled - values * (factor * factor * factor) * mean


def attend_kernel(n_q, spans, maps, *refs):
    normed, bias, cosine, sine = refs[:4]
    blocks = refs[4 : 4 + spans]
    pieces = refs[4 + spans : 4 + spans + n_q]
    queries, attended, softs, w_q, keys, values, sem = refs[4 + spans + n_q :]
    step = pl.program_id(0)
    rows = normed.shape[0]

    @pl.when(step == 0)
    def _():
        copies = load_rows(w_q, pieces, [maps[spans + n] for n in range(n_q)], sem)
        for n in range(spans):
            keys[n * rows : (n + 1) * rows, :] = blocks[n][0, :, :HD]
            values[n * rows : (n + 1) * rows, :] = blocks[n][0, :, HD:]
        for copy in copies:
            copy.wait()

    columns = pl.ds(pl.multiple_of(step * 2 * HD, 2 * HD), 2 * HD)
    raw = dot(normed[...], w_q[:, columns])
    for n in range(2):
        turned = rotate(raw[:, n * HD : (n + 1) * HD], cosine[...], sine[...])
        query = (turned * HD ** (-0.5)).astype(BF)
        queries[:, n * HD : (n + 1) * HD] = query
        scores = dot_t(query, keys[...]) + bias[...]
        weights = jnp.exp(scores - jnp.max(scores, axis=-1, keepdims=True))
        soft = (weights * (1.0 / jnp.sum(weights, axis=-1, keepdims=True))).astype(BF)
        softs[n] = soft
        attended[:, n * HD : (n + 1) * HD] = dot(soft, values[...]).astype(BF)


def project_kernel(n_o, rows, *refs):
    attended, tokens, gain = refs[:3]
    pieces = refs[3 : 3 + n_o]
    hidden, own_norm, factor, w_o, sem = refs[3 + n_o :]
    for copy in load_rows(w_o, pieces, [rows[n] for n in range(n_o)], sem):
        copy.wait()
    out = tokens[...].astype(F32) + dot(attended[...], w_o[...])
    hidden[...] = out
    scale = rms_factor(out)
    factor[...] = jnp.broadcast_to(scale, factor.shape)
    own_norm[...] = (out * scale * gain[...]).astype(BF)


def attend_back_kernel(n_o, spans, entry_count, maps, *refs):
    d_attn, queries, softs, cosine, sine = refs[:5]
    blocks = refs[5 : 5 + spans]
    pieces = refs[5 + spans : 5 + spans + n_o]
    d_raw, kept, sent = refs[5 + spans + n_o : 8 + spans + n_o]
    w_o, keys, values, d_keys, d_values, d_window, sem = refs[8 + spans + n_o :]
    step = pl.program_id(0)
    rows = d_attn.shape[0]

    @pl.when(step == 0)
    def _():
        base = spans + entry_count
        copies = load_rows(w_o, pieces, [maps[base + n] for n in range(n_o)], sem)
        for n in range(spans):
            keys[n * rows : (n + 1) * rows, :] = blocks[n][0, :, :HD]
            values[n * rows : (n + 1) * rows, :] = blocks[n][0, :, HD:]
        d_keys[...] = jnp.zeros_like(d_keys)
        d_values[...] = jnp.zeros_like(d_values)
        for copy in copies:
            copy.wait()

    w_rows = pl.ds(pl.multiple_of(step * 2 * HD, 2 * HD), 2 * HD)
    d_both = dot_t(d_attn[...], w_o[w_rows, :]).astype(BF)
    for n in range(2):
        query = queries[:, n * HD : (n + 1) * HD]
        d_out = d_both[:, n * HD : (n + 1) * HD]
        soft = softs[n]
        d_soft = dot_t(d_out, values[...])
        wide_soft = soft.astype(F32)
        delta = jnp.sum(wide_soft * d_soft, axis=-1, keepdims=True)
        d_scores = (wide_soft * (d_soft - delta)).astype(BF)
        d_query = dot(d_scores, keys[...]) * HD ** (-0.5)
        d_raw[:, n * HD : (n + 1) * HD] = rotate(d_query, cosine[...], -sine[...]).astype(BF)
        d_keys[...] += t_dot(query, d_scores)
        d_values[...] += t_dot(d_out, soft)

    @pl.when(step == pl.num_programs(0) - 1)
    def _():
        d_window[: spans * rows, :HD] = d_keys[...].T.astype(BF)
        d_window[: spans * rows, HD:] = d_values[...].T.astype(BF)
        d_window[spans * rows :, :] = jnp.zeros((rows, 2 * HD), BF)
        for n in range(entry_count):
            out = kept if n < entry_count // 2 else sent
            start = pl.multiple_of(maps[spans + n] * rows, rows)
            out[n % (entry_count // 2)] = d_window[pl.ds(start, rows), :]


ROOT = math.sqrt(2.0 / math.pi)


def forward_kernel(n_tok, maps, *refs):
    pieces = refs[:n_tok]
    cot, w_gate, w_up, w_down = refs[n_tok : n_tok + 4]
    inner, inner_t, d_both, normed_t, normed, sem = refs[n_tok + 4 :]

    @pl.when(pl.program_id(0) == 0)
    def _():
        at = 0
        copies = []
        for n, piece in enumerate(pieces):
            copies.append(
                pltpu.make_async_copy(piece, normed.at[pl.ds(at, piece.shape[0])], sem.at[n])
            )
            at += piece.shape[0]
        for copy in copies:
            copy.start()
        for copy in copies:
            copy.wait()

    wide = normed_t.shape[0]
    columns = pl.ds(pl.multiple_of(pl.program_id(0) * wide, 128), wide)
    gate, up = dot(normed[...], w_gate[...]), dot(normed[...], w_up[...])
    d_inner = dot_t(cot[...], w_down[...])
    square = gate * gate
    bent = jnp.tanh(ROOT * (gate + 0.044715 * (square * gate)))
    half = 0.5 * (1.0 + bent)
    active = gate * half
    slope = half + 0.5 * gate * (1.0 - bent * bent) * (ROOT * (1.0 + 3 * 0.044715 * square))
    result = (active * up).astype(BF)
    inner[...] = result
    inner_t[...] = result.T
    d_both[0] = (d_inner * up * slope).astype(BF)
    d_both[1] = (d_inner * active).astype(BF)
    normed_t[...] = normed[:, columns].T


def cut_rows(results, picks, outs):
    for out, starts in zip(outs, picks, strict=True):
        rows = out.shape[1]
        for n, start in enumerate(starts):
            for result in results:
                if start < result.shape[0]:
                    out[n] = result[start : start + rows].astype(BF)
                    break
                start -= result.shape[0]


def back_kernel(picks, n_parts, *refs):
    w_gu, outs = refs[n_parts], refs[n_parts + 1 :]
    units = refs[0].shape[2]
    results = [
        dot_t(part[0], w_gu[:, :units]) + dot_t(part[1], w_gu[:, units:]) for part in refs[:n_parts]
    ]
    cut_rows(results, picks, outs)


def down_kernel(picks, n_parts, maps, *refs):
    w_down, outs = refs[n_parts], refs[n_parts + 1 :]
    cut_rows([dot(part[...], w_down[...]) for part in refs[:n_parts]], picks, outs)


def grad_kernel(turned, n_parts, groups, block_rows, added, maps, *refs):
    product = dot if turned else t_dot
    lefts, rights = refs[:n_parts], refs[n_parts : 2 * n_parts]
    refs = refs[2 * n_parts :]
    result = sum(
        product(left[...], right[...].reshape(right.shape[-2:]))
        for left, right in zip(lefts, rights, strict=True)
    )
    if added:
        result = result + refs[0][...].astype(F32)
    outs = refs[1:] if added else refs
    if groups is None:
        outs[0][...] = result.astype(BF)
        return
    total = outs[-1]
    total[...] = result
    place = 0
    for n, count in enumerate(groups):
        for k in range(count):
            start = pl.multiple_of(maps[2 + place] * block_rows, 16)
            outs[n][k] = total[pl.ds(start, block_rows), :].astype(BF)
            place += 1


def grad(
    lefts, left_block, left_columns, rights, half, added=None, groups=None, order=None, turned=False
):
    right = rights[0]
    if right.ndim == 3:
        columns = right.shape[2]
    else:
        columns = right.shape[1] // 2
    blocks = 0 if groups is None else sum(groups)
    block_rows = 0 if groups is None else left_columns // blocks
    if columns % 128 or left_columns % 128 or block_rows % 16:
        result = 0
        for left, right in zip(lefts, rights, strict=True):
            cut = lax.dynamic_slice_in_dim(
                left, left_block * left_columns, left_columns, 0 if turned else 1
            )
            if right.ndim == 3:
                other = pick(right, half, 0)
            else:
                other = lax.dynamic_slice_in_dim(right, half * columns, columns, 1)
            result = result + (dot(cut, other) if turned else t_dot(cut, other))
        if added is not None:
            result = result + added.astype(F32)
        result = result.astype(BF)
        if groups is None:
            return result
        result = jnp.take(result.reshape(blocks, block_rows, columns), order, axis=0)
        outs, at = [], 0
        for count in groups:
            outs.append(result[at : at + count])
            at += count
        return outs
    wide = 384 if columns % 384 == 0 else (256 if columns % 256 == 0 else 128)
    steps = columns // wide
    maps = jnp.stack([jnp.asarray(left_block, jnp.int32), jnp.asarray(half, jnp.int32)])
    if groups is not None:
        maps = jnp.concatenate([maps, order.astype(jnp.int32)])
    in_specs = []
    for left in lefts:
        if turned:
            shape = (left_columns, left.shape[1])
            in_specs.append(pl.BlockSpec(shape, lambda i, maps: (maps[0], 0)))
        else:
            shape = (left.shape[0], left_columns)
            in_specs.append(pl.BlockSpec(shape, lambda i, maps: (0, maps[0])))
    for right in rights:
        if right.ndim == 3:
            shape = (1, right.shape[1], wide)
            in_specs.append(pl.BlockSpec(shape, lambda i, maps: (maps[1], 0, i)))
        else:
            shape = (right.shape[0], wide)
            in_specs.append(pl.BlockSpec(shape, lambda i, maps: (0, maps[1] * steps + i)))
    operands = list(lefts) + list(rights)
    if added is not None:
        in_specs.append(pl.BlockSpec((left_columns, wide), lambda i, maps: (0, i)))
        operands.append(added)
    scratch = []
    if groups is None:
        shapes = [jax.ShapeDtypeStruct((left_columns, columns), BF)]
        out_specs = [pl.BlockSpec((left_columns, wide), lambda i, maps: (0, i))]
    else:
        shapes = [jax.ShapeDtypeStruct((count, block_rows, columns), BF) for count in groups]
        out_specs = [
            pl.BlockSpec((count, block_rows, wide), lambda i, maps: (0, 0, i)) for count in groups
        ]
        scratch = [pltpu.VMEM((left_columns, wide), F32)]
    outs = kernel_call(
        functools.partial(grad_kernel, turned, len(lefts), groups, block_rows, added is not None),
        grid_spec=pltpu.PrefetchScalarGridSpec(
            num_scalar_prefetch=1,
            grid=(steps,),
            in_specs=in_specs,
            out_specs=out_specs,
            scratch_shapes=scratch,
        ),
        out_shape=shapes,
    )(maps, *operands)
    return outs[0] if groups is None else outs


class Clock:
    def __init__(self):
        self.marks = ()

    def tie(self, value):
        return after(value, *self.marks) if self.marks else value

    def mark(self, *values):
        self.marks = values


PLAN = (
    "D",
    "O",
    "W",
    "D",
    "back",
    "abO",
    "WD",
    "b",
    "a",
    "down",
    "O",
    "ba",
    "hid",
    "D",
    "e",
    "att",
    "O",
    "T",
    "W",
    "QD",
    "ve",
    "T",
    "Q",
    "v",
    "W",
    "eDv",
    "TWvQ",
    "O",
    "tok",
    "W",
    "K",
    "OD",
    "Q",
    "K",
    "Q",
    "K",
    "O",
    "WQK",
    "W",
    "K",
    "Q",
    "D",
    "Q",
    "OK",
    "KO",
    "K",
    "Q",
    "K",
    "Q",
    "K",
)


def body(
    tokens,
    cotangent,
    lengths,
    block_of,
    gain_attn,
    w_query,
    w_keyval,
    w_out,
    gain_mlp,
    w_gateup,
    w_down,
):
    tok_rows, width = tokens.shape
    y_count, z_count = lax.axis_size("y"), lax.axis_size("z")
    ctx_count = 4 * z_count
    z_levels = z_count.bit_length() - 1
    x_at, c_at, y_at, z_at = (lax.axis_index(name) for name in ("x", "c", "y", "z"))
    own_index = (z_at * 2 + x_at) * 2 + c_at
    deep = w_query.shape[0]
    quarter = deep // 4
    units = FF // (2 * y_count)
    half_tok = tok_rows // 2
    group = 2 * y_count
    others = range(1, y_count)
    clock = Clock()
    tie, mark = clock.tie, clock.mark

    def together(*values):
        return lax.optimization_barrier(values + clock.marks)[: len(values)]


    own_gains = jnp.zeros((16, deep), BF).at[0].set(gain_attn).at[1].set(gain_mlp)
    got_gains = [shift(own_gains, "y", r) for r in others]
    kv_weights = [w_keyval] + [shift(w_keyval, "y", r) for r in others]
    place_cx = c_at * 2 + x_at
    place_cz = c_at * 2 + (z_at & 1)

    def rows_of(weight, place):
        return lax.dynamic_slice_in_dim(weight, place * quarter, quarter, 0)

    wq_piece = after(rows_of(w_query, place_cx), own_gains)
    wq_y = {r: shift(wq_piece, "y", r) for r in others}
    wo_piece = after(rows_of(w_out, place_cx), wq_piece)
    wo_y = {r: shift(wo_piece, "y", r) for r in others}
    cot_x = shift(after(cotangent, wo_piece), "x", 1)
    gu_sent = {}
    for r in others:
        column = ((y_at ^ r) * 2 + x_at) * units
        moves = [
            (0, (quarter, units), (place_cz * quarter, part * FF + column), (0, part * units))
            for part in (0, 1)
        ]
        gu_sent[r] = lay_out((quarter, 2 * units), [after(w_gateup, wo_piece)], moves)

    def listed(shard, found, place):
        pieces, rows = [shard], [y_at * deep]
        for r, quarters in found.items():
            for s, piece in enumerate(quarters):
                pieces.append(piece)
                rows.append((y_at ^ r) * deep + (place ^ s) * piece.shape[0])
        return pieces, rows

    device_ids = jnp.arange(ctx_count, dtype=jnp.int32)
    block_row = block_of[0]
    own_block = jnp.sum(jnp.where(device_ids == own_index, block_row, 0))
    own_start = own_block * tok_rows
    owners = jnp.sum(
        jnp.where(block_row[None, :] == device_ids[:, None], device_ids[None, :], 0), axis=1
    )
    seq_lengths = lengths[0]
    query_places = own_start + jnp.arange(tok_rows, dtype=jnp.int32)
    key_places = own_start - WINDOW + jnp.arange(WINDOW + tok_rows, dtype=jnp.int32)
    query_segment, query_position = segment_info(query_places, seq_lengths)
    key_segment = segment_info(key_places, seq_lengths)[0]
    distance = query_places[:, None] - key_places[None, :]
    allowed = (
        (query_segment[:, None] == key_segment[None, :])
        & (key_places >= 0)[None, :]
        & (distance >= 0)
        & (distance < WINDOW)
    )
    bias = jnp.where(allowed, 0.0, -1e30).astype(F32)
    cosine, sine = tables(query_position, HD)
    cosine = jnp.concatenate([cosine, cosine], axis=1)
    sine = jnp.concatenate([-sine, sine], axis=1)
    spans = WINDOW // tok_rows + 1
    first_block = own_block - (spans - 1)

    def entry_of(ctx_index):
        differ = ctx_index ^ own_index
        return ((differ >> 1) & 1) | ((differ >> 2) << 1) | ((differ & 1) << (z_levels + 1))

    window = first_block + jnp.arange(spans, dtype=jnp.int32)
    window = entry_of(jnp.take(owners, jnp.clip(window, 0, ctx_count - 1)))
    entries = jnp.arange(ctx_count, dtype=jnp.int32)
    differ = ((entries >> 1) & (z_count - 1)) << 2
    differ = differ | ((entries & 1) << 1) | (entries >> (z_levels + 1))
    entry_block = jnp.take(block_row, differ ^ own_index) - first_block
    entry_block = jnp.where((entry_block >= 0) & (entry_block < spans), entry_block, spans)

    z_places = jnp.zeros((z_count,), jnp.int32)
    z_differ = jnp.arange(z_count, dtype=jnp.int32) ^ z_at
    for n, level in enumerate(reversed(range(z_levels))):
        z_places = z_places | (((z_differ >> level) & 1) << n)
    z_order = jnp.zeros((z_count,), jnp.int32)
    for level in range(z_levels):
        z_order = z_order | (
            ((jnp.arange(z_count, dtype=jnp.int32) >> (z_levels - 1 - level)) & 1) << level
        )
    z_order = z_order ^ z_at

    gains = by_place([own_gains[:2]] + [g[:2] for g in got_gains], "y")
    gains = jnp.swapaxes(gains, 0, 1).reshape(2, width).astype(F32)
    gain_one, gain_two = gains[:1], gains[1:]
    kv_rows = jnp.stack([(y_at ^ r) * deep for r in range(y_count)]).astype(jnp.int32)
    in_vmem = pl.BlockSpec(memory_space=pltpu.VMEM)
    normed, keyval = kernel_call(
        kv_kernel,
        in_specs=[pl.BlockSpec(memory_space=pltpu.SMEM)] + [in_vmem] * 4 + [ANY] * y_count,
        out_specs=[in_vmem, in_vmem],
        out_shape=[
            jax.ShapeDtypeStruct((tok_rows, width), BF),
            jax.ShapeDtypeStruct((tok_rows, 2 * HD), BF),
        ],
        scratch_shapes=[pltpu.VMEM((width, 2 * HD), BF), pltpu.SemaphoreType.DMA((y_count,))],
    )(kv_rows, tokens, gain_one, cosine, sine, *kv_weights)
    mark(keyval, bias, z_order, z_places, entry_block, window)
    held = stack_two(keyval[None], tie(shift(keyval, "x", 1)[None]))
    mark(held)
    over_z = [shift(held, "z", d) for d in range(1, z_count)]
    wq_y = {r: tie(piece) for r, piece in wq_y.items()}
    mark(*wq_y.values())
    wq_found = {r: [piece, shift(piece, "x", 1)] for r, piece in wq_y.items()}

    def stack_all(_, ins, outs):
        for n, part in enumerate(ins):
            outs[0][n * 2 : n * 2 + 2] = part[...]

    held = once(
        stack_all,
        [((2 * z_count, tok_rows, 2 * HD), BF)],
        held,
        *[tie(part) for part in over_z],
    )[0]
    mark(held)
    across = shift(held, "c", 1)
    count = y_count - 1
    gu_y = {r: shift(piece, "y", r) for r, piece in gu_sent.items()}
    joint = [wq_found[r][1] for r in others] + [wo_y[r] for r in others]
    joint = together(cot_x, *joint, *[gu_y[r] for r in others])
    cot_x, joint = joint[0], joint[1:]
    mark(cot_x, *joint)
    wq_found = {r: [wq_found[r][0], joint[n]] for n, r in enumerate(others)}
    wo_y = {r: joint[count + n] for n, r in enumerate(others)}
    gu_y = {r: joint[2 * count + n] for n, r in enumerate(others)}
    wq_found = {r: pair + [shift(p, "c", 1) for p in pair] for r, pair in wq_found.items()}
    wo_found = {r: [piece, shift(piece, "x", 1)] for r, piece in wo_y.items()}
    gu_z = {r: shift(piece, "z", 1) for r, piece in gu_y.items()}
    cot_y = {r: shift(tie(cotangent), "y", r) for r in others}

    all_kv = stack_two(held, tie(across))
    mark(all_kv)
    q_pieces, q_rows = listed(w_query, wq_found, place_cx)
    q_pieces = [tie(piece) for piece in q_pieces]
    n_q = len(q_pieces)
    pairs = H // 2
    kv_specs = [
        pl.BlockSpec((1, tok_rows, 2 * HD), lambda i, maps, n=n: (maps[n], 0, 0))
        for n in range(spans)
    ]
    pair_spec = pl.BlockSpec((tok_rows, 2 * HD), lambda i, maps: (0, i))
    token_spec = pl.BlockSpec((tok_rows, width), lambda i, maps: (0, 0))
    maps = jnp.concatenate([window, jnp.stack(q_rows).astype(jnp.int32)])
    small = [bias, cosine, sine]
    soft_spec = pl.BlockSpec((2, tok_rows, spans * tok_rows), lambda i, maps: (i, 0, 0))
    queries, attended, softs = kernel_call(
        functools.partial(attend_kernel, n_q, spans),
        grid_spec=pltpu.PrefetchScalarGridSpec(
            num_scalar_prefetch=1,
            grid=(pairs,),
            in_specs=[token_spec] + [whole_spec(a) for a in small] + kv_specs + [ANY] * n_q,
            out_specs=[pair_spec, pair_spec, soft_spec],
            scratch_shapes=[
                pltpu.VMEM((width, H * HD), BF),
                pltpu.VMEM((spans * tok_rows, HD), BF),
                pltpu.VMEM((spans * tok_rows, HD), BF),
                pltpu.SemaphoreType.DMA((n_q,)),
            ],
        ),
        out_shape=[
            jax.ShapeDtypeStruct((tok_rows, H * HD), BF),
            jax.ShapeDtypeStruct((tok_rows, H * HD), BF),
            jax.ShapeDtypeStruct((H, tok_rows, spans * tok_rows), BF),
        ],
    )(maps, tie(normed), *small, *([all_kv] * spans), *q_pieces)
    joint = [wo_found[r][1] for r in others] + [gu_z[r] for r in others]
    joint = together(attended, *joint, *[cot_y[r] for r in others])
    attended, joint = joint[0], joint[1:]
    mark(attended, *joint)
    wo_found = {r: [wo_found[r][0], joint[n]] for n, r in enumerate(others)}
    gu_found = {r: [gu_y[r], joint[count + n]] for n, r in enumerate(others)}
    cot_y = {r: joint[2 * count + n] for n, r in enumerate(others)}
    wo_found = {r: pair + [shift(p, "c", 1) for p in pair] for r, pair in wo_found.items()}
    gu_found = {r: pair + [shift(p, "c", 1) for p in pair] for r, pair in gu_found.items()}
    o_pieces, o_rows = listed(w_out, wo_found, place_cx)
    n_o = len(o_pieces)
    hidden, own_norm, factor = kernel_call(
        functools.partial(project_kernel, n_o),
        in_specs=[pl.BlockSpec(memory_space=pltpu.SMEM)] + [in_vmem] * 3 + [ANY] * n_o,
        out_specs=[in_vmem] * 3,
        out_shape=[
            jax.ShapeDtypeStruct((tok_rows, width), F32),
            jax.ShapeDtypeStruct((tok_rows, width), BF),
            jax.ShapeDtypeStruct((tok_rows, HD), F32),
        ],
        scratch_shapes=[pltpu.VMEM((H * HD, width), BF), pltpu.SemaphoreType.DMA((n_o,))],
    )(jnp.stack(o_rows).astype(jnp.int32), attended, tokens, gain_two, *o_pieces)
    mark(own_norm)

    norm_y = {r: shift(own_norm, "y", r) for r in others}
    norm_x = shift(own_norm, "x", 1)
    cot_a = {r: shift(part[:half_tok], "x", 1) for r, part in cot_y.items()}
    cot_b = {r: shift(cot_x[half_tok:], "y", r) for r in others}
    cot_near = jnp.concatenate([cotangent, *[cot_y[r] for r in others], cot_x], axis=0)
    gu_moves = [
        (0, (deep, units), (0, part * FF + (y_at * 2 + x_at) * units), (y_at * deep, part * units))
        for part in (0, 1)
    ]
    gu_pieces, gu_rows = listed(w_gateup, gu_found, place_cz)
    for n in range(1, len(gu_pieces)):
        gu_moves.append((n, (quarter, 2 * units), (0, 0), (gu_rows[n], 0)))
    w_gu = lay_out((width, 2 * units), gu_pieces, gu_moves)
    mark(w_gu, cot_near)
    norm_slices = {r: tie(part)[:half_tok] for r, part in norm_y.items()}
    norm_slice = tie(norm_x)[half_tok:]
    mark(norm_slice, *norm_slices.values())
    norm_a = {r: shift(part, "x", 1) for r, part in norm_slices.items()}
    norm_b = {r: shift(norm_slice, "y", r) for r in others}
    near = [tie(own_norm), *[norm_y[r] for r in others], norm_x]
    far, cot_far = [], []
    for r in others:
        far += [norm_a[r], norm_b[r]]
        cot_far += [cot_a[r], cot_b[r]]
    many = group * tok_rows
    fits = units % 128 == 0
    picks = [
        [r * tok_rows for r in range(y_count)],
        [(y_count + r) * tok_rows for r in range(y_count)],
        [half_tok, y_count * tok_rows + half_tok],
    ]
    picks += [[r * tok_rows + half_tok, (y_count + r) * tok_rows + half_tok] for r in others]
    cut_shapes = [jax.ShapeDtypeStruct((len(pick_), half_tok, width), BF) for pick_ in picks]
    x_maps = jnp.stack([x_at]).astype(jnp.int32)

    out_picks = [[r * tok_rows, (y_count + r) * tok_rows] for r in range(y_count)]
    out_shapes = [jax.ShapeDtypeStruct((2, tok_rows, width), BF)] * y_count

    def cut(result, places, rows):
        return [
            jnp.stack([result[start : start + rows].astype(BF) for start in starts])
            for starts in places
        ]

    if fits:
        wide = 384 if units % 384 == 0 else 128
        steps = units // wide
        turn = width // steps
        block = 512
        cut_specs = [
            pl.BlockSpec((len(starts), half_tok, block), lambda i, *_: (0, 0, i))
            for starts in picks
        ]

        def forward(pieces, cot):
            n_tok, rows = len(pieces), cot.shape[0]
            return kernel_call(
                functools.partial(forward_kernel, n_tok),
                grid_spec=pltpu.PrefetchScalarGridSpec(
                    num_scalar_prefetch=1,
                    grid=(steps,),
                    in_specs=[ANY] * n_tok
                    + [
                        pl.BlockSpec((rows, width), lambda i, maps: (0, 0)),
                        pl.BlockSpec((width, wide), lambda i, maps: (0, i)),
                        pl.BlockSpec((width, wide), lambda i, maps: (0, steps + i)),
                        pl.BlockSpec((wide, width), lambda i, maps: (maps[0] * steps + i, 0)),
                    ],
                    out_specs=[
                        pl.BlockSpec((rows, wide), lambda i, maps: (0, i)),
                        pl.BlockSpec((wide, rows), lambda i, maps: (i, 0)),
                        pl.BlockSpec((2, rows, wide), lambda i, maps: (0, 0, i)),
                        pl.BlockSpec((turn, rows), lambda i, maps: (i, 0)),
                    ],
                    scratch_shapes=[
                        pltpu.VMEM((rows, width), BF),
                        pltpu.SemaphoreType.DMA((n_tok,)),
                    ],
                ),
                out_shape=[
                    jax.ShapeDtypeStruct((rows, units), BF),
                    jax.ShapeDtypeStruct((units, rows), BF),
                    jax.ShapeDtypeStruct((2, rows, units), BF),
                    jax.ShapeDtypeStruct((width, rows), BF),
                ],
            )(x_maps, *pieces, cot, w_gu, w_gu, w_down)

        results = forward(near, cot_near)
        mark(*results)
        joint = together(*far, *cot_far)
        far, cot_far = joint[: len(far)], jnp.concatenate(joint[len(far) :], axis=0)
        results = list(zip(results, forward(far, cot_far), strict=True))
        inner_act, inner_t, d_both, normed_t = results
        cots = (cot_near, cot_far)

        def back_cut():
            return kernel_call(
                functools.partial(back_kernel, picks, len(d_both)),
                grid=(width // block,),
                in_specs=[whole_spec(part) for part in d_both]
                + [pl.BlockSpec((block, 2 * units), lambda i: (i, 0))],
                out_specs=cut_specs,
                out_shape=cut_shapes,
            )(tie(d_both[0]), *d_both[1:], w_gu)

        def down_cut():
            return kernel_call(
                functools.partial(down_kernel, out_picks, len(inner_act)),
                grid_spec=pltpu.PrefetchScalarGridSpec(
                    num_scalar_prefetch=1,
                    grid=(width // block,),
                    in_specs=[whole_spec(part) for part in inner_act]
                    + [pl.BlockSpec((units, block), lambda i, maps: (maps[0], i))],
                    out_specs=[pl.BlockSpec((2, tok_rows, block), lambda i, *_: (0, 0, i))]
                    * y_count,
                ),
                out_shape=out_shapes,
            )(x_maps, tie(inner_act[0]), *inner_act[1:], w_down)

    else:
        normed2 = jnp.concatenate(near + far, axis=0)
        cot_all = jnp.concatenate([cot_near, *cot_far], axis=0)
        w_dn = lax.dynamic_slice_in_dim(w_down, x_at * units, units, 0)
        d_inner = dot_t(cot_all, w_dn)
        both_parts = dot(normed2, w_gu)
        active, back = jax.vjp(
            lambda values: jax.nn.gelu(values, approximate=True), both_parts[:, :units]
        )
        up_part = both_parts[:, units:]
        inner_act = (active * up_part).astype(BF)
        d_both = [jnp.stack([back(d_inner * up_part)[0], d_inner * active]).astype(BF)]
        inner_t, normed_t, cots = [inner_act.T], [normed2.T], [cot_all]

        def back_cut():
            both = tie(d_both[0])
            result = dot_t(both[0], w_gu[:, :units]) + dot_t(both[1], w_gu[:, units:])
            return cut(result, picks, half_tok)

        def down_cut():
            return cut(dot(tie(inner_act), w_dn), out_picks, tok_rows)

    mark(*d_both)

    def back_a(cuts_in, result):
        keep, send = cuts_in[0], cuts_in[1]
        got = yield [(send, "x", 1)]

        def function(_, ins, outs):
            for n in range(y_count):
                outs[n][...] = (ins[0][n].astype(F32) + ins[1][n].astype(F32)).astype(BF)

        left = once(function, [((half_tok, width), BF)] * y_count, keep, got[0])
        got = yield [(left[r], "y", r) for r in others]
        result["a"] = [left[0]] + got

    def back_b(cuts_in, result):
        keep, send = cuts_in[2], cuts_in[3:]
        got = yield [(part, "y", r) for r, part in zip(others, send, strict=True)]

        def function(_, ins, outs):
            for n in range(2):
                outs[n][...] = sum(ref[n].astype(F32) for ref in ins).astype(BF)

        left = once(function, [((half_tok, width), BF)] * 2, keep, *got)
        got = yield [(left[1], "x", 1)]
        result["b"] = [left[0]] + got

    def sum_rows(ins, n_first):
        first = sum(ref[...].astype(F32) for ref in ins[:n_first])
        second = sum(ref[...].astype(F32) for ref in ins[n_first : n_first + 2])
        return jnp.concatenate([first, second], axis=0)

    def back_whole(keep, sent, result):
        got = yield [(part, "y", r) for r, part in zip(others, sent, strict=True)]

        def function(_, ins, outs):
            for n in range(2):
                outs[n][...] = sum(ref[n].astype(F32) for ref in ins).astype(BF)

        left = once(function, [((tok_rows, width), BF)] * 2, keep, *got)
        got = yield [(left[1], "x", 1)]
        result += [left[0]] + got

    def scatter_z(kept, sent):
        for level in range(z_levels):
            got = yield [(sent, "z", 1 << level)]
            sums = add_halves(kept, got[0])
            kept, sent = sums[0], sums[-1]
        return kept

    def spread(piece, finish, split=True):
        held = piece
        for level in reversed(range(z_levels)):
            got = yield [(held, "z", 1 << level)]
            held = stack_two(held, got[0])
        beside, across = yield [(held, "x", 1), (held, "c", 1)]
        corner = yield [(beside, "c", 1)]
        if split:
            mark(finish([tie(held), across], False))
            mark(finish([tie(beside), corner[0]], True))
        else:
            mark(finish([tie(held), beside, across, corner[0]], False))

    z_groups = [z_count // 2, z_count // 2]

    found = {}

    def finish_down(parts, beside):
        found["down"] = widen(
            parts,
            beside,
            z_places,
            (2, z_count, w_down.shape[0] // (2 * z_count), width),
            lambda c, x, y: (x, None, c),
            found.get("down"),
        )
        return found["down"]

    def finish_up(r):
        def finish(parts, beside):
            found["up"] = widen(
                parts,
                beside,
                z_places,
                (1, z_count, deep // z_count, 2 * FF),
                lambda c, x, y: (0, None, (c * y_count + (y ^ r)) * 2 + x),
                found.get("up"),
            )
            return found["up"]

        return finish

    def finish_attn(names, cols):
        def finish(parts, _):
            rows = deep // (2 * z_count)
            for n, name in enumerate(names):
                found[name] = widen(
                    parts,
                    False,
                    z_places,
                    (z_count, 2, rows, 2 * cols),
                    lambda c, x, y: (None, x, c),
                    None,
                    n,
                    cols,
                )
                mark(found[name])
            return found[names[-1]]

        return finish

    def ffn_chain(job, finish, r):
        left, left_block, left_rows, right = job
        left = [tie(left[0])] + list(left[1:])
        theirs = grad(left, left_block, left_rows, right, 1 - c_at, turned=True)
        got = yield [(theirs, "c", 1)]
        kept, sent = grad(
            left, left_block, left_rows, right, c_at, got[0], z_groups, z_order, turned=True
        )
        piece = yield from scatter_z(kept, sent)
        if r:
            got = yield [(piece, "y", r)]
            piece = got[0]
        yield from spread(piece, finish)

    y_order = jnp.arange(y_count, dtype=jnp.int32) ^ y_at
    xz_maps = jnp.concatenate([z_order * 2 + x_at, z_order * 2 + (1 - x_at)])

    cut_rows_x = deep // (2 * z_count)

    def cut_x(*parts_of):
        widths = [parts[0].shape[1] for parts in parts_of]
        flat = [part for parts in parts_of for part in parts]
        total_width = sum(widths)
        if cut_rows_x % 16:
            total = jnp.concatenate([sum(v.astype(F32) for v in parts) for parts in parts_of], axis=1)
            blocks = total.astype(BF).reshape(2 * z_count, cut_rows_x, total_width)
            blocks = jnp.take(blocks, xz_maps, axis=0)
            return blocks[:z_count], blocks[z_count:]

        def function(maps, ins, outs):
            for n in range(2 * z_count):
                block = pl.ds(pl.multiple_of(maps[n] * cut_rows_x, 16), cut_rows_x)
                at, ref_at = 0, 0
                for parts, wide_ in zip(parts_of, widths, strict=True):
                    refs = ins[ref_at : ref_at + len(parts)]
                    total = sum(ref[block, :].astype(F32) for ref in refs)
                    outs[n // z_count][n % z_count, :, at : at + wide_] = total.astype(BF)
                    at, ref_at = at + wide_, ref_at + len(parts)

        return once(function, [((z_count, cut_rows_x, total_width), BF)] * 2, *flat, maps=xz_maps)

    def core_then_y(left, right, column=None):
        cols = right.shape[1] // 2
        theirs = grad([tie(left)], 0, width, [right], 1 - c_at)
        if column is not None:
            lane = jnp.arange(HD) == 0
            own = jnp.where(c_at == 0, column[0], column[1]).reshape(width, 1)
            other = jnp.where(c_at == 0, column[1], column[0]).reshape(width, 1)
            theirs = jnp.concatenate([theirs, jnp.where(lane, other, 0).astype(BF)], axis=1)
        got = yield [(theirs, "c", 1)]
        got = got[0]
        parts = grad([left], 0, width, [right], c_at, got[:, :cols], [1] * y_count, y_order)
        parts = [part[0] for part in parts]
        if column is not None:
            extra = add(jnp.where(lane, own, 0), got[:, cols:]).reshape(y_count, deep, HD)
            parts = [
                jnp.concatenate([part, pick(extra, y_at ^ r, 0)], axis=1)
                for r, part in enumerate(parts)
            ]
        got = yield [(part, "y", r) for r, part in zip(others, parts[1:], strict=True)]
        return [parts[0]] + got

    def x_then_z(kept, sent):
        got = yield [(sent, "x", 1)]
        sums = add_halves(kept, got[0])
        return (yield from scatter_z(sums[0], sums[1]))

    def chain_t():
        found["t_parts"] = yield from core_then_y(attended, found["d_attn"])

    def chain_q():
        parts = yield from core_then_y(normed, found["d_raw"])
        piece = yield from x_then_z(*cut_x([tie(part) for part in found["t_parts"]], parts))
        yield from spread(piece, finish_attn(("out", "query"), width // 2), split=False)

    def chain_k(d_kv_raw, d_gain):
        parts = yield from core_then_y(normed, d_kv_raw, (d_gain, found["d_gain_mlp"]))
        piece = yield from x_then_z(*cut_x(parts))

        yield from spread(piece, finish_attn(("keyval",), 2 * HD), split=False)

    chains, pending = {}, {}

    def advance(names):
        names = [name for name in names.split() if chains.get(name) is not None]
        waited = [part for name in names for part in pending.get(name, [])]
        if waited:
            waited = list(together(*waited))
            mark(*waited)
        for name in names:
            count = len(pending.get(name, []))
            got, waited = waited[:count], waited[count:]
            try:
                if name in pending:
                    got = list(together(*got)) if got else []
                    sends = chains[name].send(got)
                else:
                    sends = [(tie(part), axis, mask) for part, axis, mask in next(chains[name])]
            except StopIteration:
                chains[name] = None
                continue
            mark(*[part for part, _, _ in sends])
            pending[name] = [shift(*send) for send in sends]

    d_result, out_result = {}, []
    jobs = [
        ffn_chain((normed_t, y_at ^ r, deep, d_both), finish_up(r), r) for r in list(others) + [0]
    ]
    ups = [f"U{r}" for r in others]
    for name, chain in zip(ups + ["W"], jobs, strict=True):
        chains[name] = chain
    first_up = " ".join(ups)
    chains["D"] = ffn_chain((inner_t, 0, units, cots), finish_down, 0)

    def do_back():
        d_cut = back_cut()
        mark(*d_cut)
        chains["a"], chains["b"] = back_a(d_cut, d_result), back_b(d_cut, d_result)

    def do_down():
        out_cut = down_cut()
        mark(*out_cut)
        chains["e"] = back_whole(out_cut[0], out_cut[1:], out_result)

    def hidden_back(_, ins, outs):
        grads = sum_rows(ins, y_count)
        values, scale, upstream, gain = (ref[...] for ref in ins[y_count + 2 :])
        scale = scale[:, :1]
        back = upstream.astype(F32) + norm_back_rows(grads, values, scale, gain)
        outs[0][...] = back
        outs[1][...] = back.astype(BF)
        outs[2][...] = jnp.sum(grads * values * scale, axis=0, keepdims=True)

    def do_hidden():
        found["d_hidden"], found["d_attn"], found["d_gain_mlp"] = once(
            hidden_back,
            [((tok_rows, width), F32), ((tok_rows, width), BF), ((1, width), F32)],
            *[tie(part) for part in d_result["a"] + d_result["b"]],
            hidden,
            factor,
            cotangent,
            gain_two,
        )
        mark(found["d_attn"], found["d_gain_mlp"])
        chains["T"] = chain_t()

    maps = jnp.concatenate([window, entry_block, jnp.stack(o_rows).astype(jnp.int32)])
    entry_spec = pl.BlockSpec((ctx_count // 2, tok_rows, 2 * HD), lambda i, maps: (0, 0, 0))
    entry_shape = jax.ShapeDtypeStruct((ctx_count // 2, tok_rows, 2 * HD), BF)
    small = [cosine, sine]

    def do_attention():
        found["d_raw"], found["d_kept"], found["d_sent"] = kernel_call(
            functools.partial(attend_back_kernel, n_o, spans, ctx_count),
            grid_spec=pltpu.PrefetchScalarGridSpec(
                num_scalar_prefetch=1,
                grid=(pairs,),
                in_specs=[token_spec, pair_spec, soft_spec]
                + [whole_spec(a) for a in small]
                + kv_specs
                + [ANY] * n_o,
                out_specs=[pair_spec, entry_spec, entry_spec],
                scratch_shapes=[
                    pltpu.VMEM((H * HD, width), BF),
                    pltpu.VMEM((spans * tok_rows, HD), BF),
                    pltpu.VMEM((spans * tok_rows, HD), BF),
                    pltpu.VMEM((HD, spans * tok_rows), F32),
                    pltpu.VMEM((HD, spans * tok_rows), F32),
                    pltpu.VMEM(((spans + 1) * tok_rows, 2 * HD), BF),
                    pltpu.SemaphoreType.DMA((n_o,)),
                ],
            ),
            out_shape=[jax.ShapeDtypeStruct((tok_rows, H * HD), BF), entry_shape, entry_shape],
        )(maps, tie(found["d_attn"]), queries, softs, *small, *([all_kv] * spans), *o_pieces)
        mark(found["d_sent"])
        chains["Q"] = chain_q()
        chains["v"] = kv_back(kv_result)

    def kv_back(result):
        got = yield [(found["d_sent"], "c", 1)]

        def first(_, ins, outs):
            for n in range(2 * z_count):
                outs[n % 2][n // 2] = (ins[0][n].astype(F32) + ins[1][n].astype(F32)).astype(BF)

        shape = ((z_count, tok_rows, 2 * HD), BF)
        kept, sent = once(first, [shape, shape], found["d_kept"], got[0])
        got = yield [(sent, "x", 1)]

        def second(_, ins, outs):
            for n in range(z_count):
                outs[n][...] = (ins[0][n].astype(F32) + ins[1][n].astype(F32)).astype(BF)

        left = once(second, [((tok_rows, 2 * HD), BF)] * z_count, kept, got[0])
        got = yield [(left[d], "z", d) for d in range(1, z_count)]
        result += [left[0]] + got

    kv_result = []

    def tokens_kernel(maps, *refs):
        n_kv = y_count
        d_raw, cosine_ref, sine_ref, tokens_ref, gain, back_hidden = refs[:6]
        parts = refs[6 : 6 + z_count]
        kv_pieces = refs[6 + z_count : 6 + z_count + n_kv]
        pieces = refs[6 + z_count + n_kv : 6 + z_count + n_kv + n_q]
        outs = refs[6 + z_count + n_kv + n_q :]
        d_kv, back, d_gain, whole_q, whole_kv, q_sem, kv_sem = outs
        copies = load_rows(whole_q, pieces, [maps[n] for n in range(n_q)], q_sem)
        copies += load_rows(whole_kv, kv_pieces, [maps[n_q + n] for n in range(n_kv)], kv_sem)
        total = sum(ref[...].astype(F32) for ref in parts)
        d_kv[:, :HD] = rotate(total[:, :HD], cosine_ref[...], -sine_ref[...]).astype(BF)
        d_kv[:, HD:] = total[:, HD:].astype(BF)
        inputs = tokens_ref[...].astype(F32)
        scale = rms_factor(inputs)
        for copy in copies:
            copy.wait()
        grads = dot_t(d_raw[...], whole_q[...]) + dot_t(d_kv[...], whole_kv[...])
        back[...] = back_hidden[...] + norm_back_rows(grads, inputs, scale, gain[...])
        d_gain[...] = jnp.sum(grads * inputs * scale, axis=0, keepdims=True)

    q_maps = jnp.concatenate([jnp.stack(q_rows).astype(jnp.int32), kv_rows])
    def do_tokens():
        d_kv_raw, found["tokens"], d_gain = kernel_call(
            tokens_kernel,
            in_specs=[pl.BlockSpec(memory_space=pltpu.SMEM)]
            + [in_vmem] * (6 + z_count)
            + [ANY] * (y_count + n_q),
            out_specs=[in_vmem] * 3,
            out_shape=[
                jax.ShapeDtypeStruct((tok_rows, 2 * HD), BF),
                jax.ShapeDtypeStruct((tok_rows, width), F32),
                jax.ShapeDtypeStruct((1, width), F32),
            ],
            scratch_shapes=[
                pltpu.VMEM((width, H * HD), BF),
                pltpu.VMEM((width, 2 * HD), BF),
                pltpu.SemaphoreType.DMA((n_q,)),
                pltpu.SemaphoreType.DMA((y_count,)),
            ],
        )(
            q_maps,
            found["d_raw"],
            cosine,
            sine,
            tokens,
            gain_one,
            found["d_hidden"],
            *[tie(part) for part in kv_result],
            *kv_weights,
            *q_pieces,
        )
        mark(d_kv_raw, d_gain, found["tokens"])
        chains["K"] = chain_k(d_kv_raw, d_gain)

    works = {
        "back": do_back,
        "down": do_down,
        "hid": do_hidden,
        "att": do_attention,
        "tok": do_tokens,
    }
    for entry in PLAN:
        if entry in works:
            works[entry]()
        else:
            advance(" ".join(first_up if letter == "O" else letter for letter in entry))
    while any(chain is not None for chain in chains.values()):
        advance(" ".join(chains))

    def finish_output(_, ins, outs):
        outs[0][...] = (ins[-1][...] + sum(ref[...].astype(F32) for ref in ins[:-1])).astype(BF)

    block_output = once(finish_output, [((tok_rows, width), BF)], *out_result, hidden)[0]
    last = found["keyval"]
    grad_keyval = jnp.concatenate([last[:, :HD], last[:, 2 * HD : 3 * HD]], axis=1)
    return (
        block_output,
        found["tokens"],
        last[:, HD],
        found["query"],
        grad_keyval,
        found["out"],
        last[:, 3 * HD],
        found["up"],
        found["down"],
    )


def solution(mesh):
    ctx_count, y_count = mesh.shape["ctx"], mesh.shape["fsdp"]
    fine = Mesh(mesh.devices.reshape(ctx_count // 4, 2, 2, y_count), ("z", "x", "c", "y"))
    rows, shard = P(("z", "x", "c", "y"), None), P("y", None)
    in_specs = (rows, rows, shard, shard, P("y"), shard, shard, shard, P("y"), shard, shard)
    out_specs = (rows, rows, P("y"), shard, shard, shard, P("y"), shard, shard)
    return jax.shard_map(body, mesh=fine, in_specs=in_specs, out_specs=out_specs, check_vma=False)
```

```python
import functools
import math

import jax
import jax.numpy as jnp
from jax import lax
from jax.experimental import pallas as pl
from jax.experimental.pallas import tpu as pltpu
from jax.sharding import Mesh
from jax.sharding import PartitionSpec as P

H = 12
HD = 128
FF = 4608
WINDOW = 1024
EPSILON = 1e-06
BF = jnp.bfloat16
F32 = jnp.float32
VMEM_LIMIT = 48 * 1024 * 1024


def tables(places, width):
    half_width = width // 2
    frequency = jnp.exp(
        jnp.arange(half_width, dtype=jnp.float32) * (-2.0 * math.log(10000.0) / width)
    )
    angles = places.astype(jnp.float32)[:, None] * frequency[None, :]
    return (jnp.cos(angles), jnp.sin(angles))


def rotate(values, cosine, sine):
    turned = jnp.concatenate([values[:, HD // 2 :], values[:, : HD // 2]], axis=1)
    return values * cosine + turned * sine


def rms_factor(values):
    return lax.rsqrt(jnp.mean(values * values, axis=-1, keepdims=True) + EPSILON)


def segment_info(places, seq_lengths):
    seq_ends = jnp.cumsum(seq_lengths)
    passed = places[:, None] >= seq_ends[None, :]
    segment = jnp.sum(passed.astype(jnp.int32), axis=1)
    seq_start = jnp.sum(jnp.where(passed, seq_lengths[None, :], 0), axis=1)
    return (segment, places - seq_start)


def dot(a, b):
    return jnp.dot(a, b, preferred_element_type=F32)


def dot_t(a, b):
    return lax.dot_general(a, b, (((1,), (1,)), ((), ())), preferred_element_type=F32)


def t_dot(a, b):
    return lax.dot_general(a, b, (((0,), (0,)), ((), ())), preferred_element_type=F32)


def after(value, *earlier):
    return lax.optimization_barrier((value,) + earlier)[0]


def shift(array, axis, mask):
    return lax.ppermute(array, axis, [(i, i ^ mask) for i in range(lax.axis_size(axis))])


def bit(axis, k=0):
    return (lax.axis_index(axis) >> k) & 1


def pick(array, index, dim):
    return lax.dynamic_index_in_dim(array, index, dim, keepdims=False)


def add(a, b):
    return (a.astype(F32) + b.astype(F32)).astype(BF)


def by_place(entries, axis_name):
    if len(entries) == 2:
        low, high = jnp.stack(entries), jnp.stack(entries[::-1])
        return jnp.where(lax.axis_index(axis_name) == 0, low, high)
    order = jnp.arange(len(entries), dtype=jnp.int32) ^ lax.axis_index(axis_name)
    return jnp.take(jnp.stack(entries), order, axis=0)


def kernel_call(function, **options):
    return pl.pallas_call(
        function,
        compiler_params=pltpu.CompilerParams(vmem_limit_bytes=VMEM_LIMIT),
        cost_estimate=pl.CostEstimate(flops=1000, bytes_accessed=1000, transcendentals=0),
        **options,
    )


def whole_spec(array):
    zeros = (0,) * array.ndim
    return pl.BlockSpec(array.shape, lambda *_: zeros)


ANY = pl.BlockSpec(memory_space=pl.ANY)


def load_rows(target, pieces, rows, sem):
    copies = []
    for n, piece in enumerate(pieces):
        start = pl.multiple_of(rows[n], 16)
        copies.append(
            pltpu.make_async_copy(piece, target.at[pl.ds(start, piece.shape[0])], sem.at[n])
        )
    for copy in copies:
        copy.start()
    return copies


def copy_kernel(blocks, spots, *refs):
    parts, out, sem = refs[:-2], refs[-2], refs[-1]
    copies = []
    for n, (part, rows, columns) in enumerate(blocks):
        at = [pl.multiple_of(spots[n, 0], 16), pl.multiple_of(spots[n, 1], 128)]
        to = [pl.multiple_of(spots[n, 2], 16), pl.multiple_of(spots[n, 3], 128)]
        copies.append(
            pltpu.make_async_copy(
                parts[part].at[pl.ds(at[0], rows), pl.ds(at[1], columns)],
                out.at[pl.ds(to[0], rows), pl.ds(to[1], columns)],
                sem.at[n],
            )
        )
    for copy in copies:
        copy.start()
    for copy in copies:
        copy.wait()


def lay_out(shape, parts, moves):
    aligned = all(size[0] % 16 == 0 and size[1] % 128 == 0 for _, size, _, _ in moves)
    if not aligned:
        out = jnp.zeros(shape, parts[0].dtype)
        for part, size, at, to in moves:
            out = lax.dynamic_update_slice(out, lax.dynamic_slice(parts[part], at, size), to)
        return out
    spots = jnp.stack(
        [jnp.stack([jnp.asarray(v, jnp.int32) for v in at + to]) for _, _, at, to in moves]
    )
    blocks = tuple((part,) + size for part, size, _, _ in moves)
    return kernel_call(
        functools.partial(copy_kernel, blocks),
        out_shape=jax.ShapeDtypeStruct(shape, parts[0].dtype),
        in_specs=[pl.BlockSpec(memory_space=pltpu.SMEM)] + [ANY] * len(parts),
        out_specs=pl.BlockSpec(memory_space=pltpu.VMEM),
        scratch_shapes=[pltpu.SemaphoreType.DMA((len(moves),))],
    )(spots, *parts)


def widen_kernel(count, maps, *refs):
    parts, out = refs[:count], refs[-1]
    source = pl.program_id(0) ^ maps[0]
    z_count, rows, columns = parts[0].shape
    lead = out.shape[0] == 1
    for n in range(count):

        @pl.when(source == n)
        def _(n=n):
            for z in range(z_count):
                block = parts[n][maps[3 + z]].astype(F32)
                if lead:
                    out[0, z] = block
                else:
                    out[z, 0] = block


def widen(parts, beside, z_places, out_shape, spot, so_far=None, column=0, columns=None):
    count = len(parts)
    z_count, rows = parts[0].shape[:2]
    columns = columns or parts[0].shape[2]
    x_at, c_at, y_at = (lax.axis_index(name) for name in ("x", "c", "y"))
    if count == 2:
        flips = [c_at, x_at ^ (1 if beside else 0), y_at]
    else:
        flips = [c_at * 2 + x_at, x_at, y_at]
    z_first = spot(0, 0, 0)[0] is None
    size = (z_count, 1) if z_first else (1, z_count)
    flat = (out_shape[0] * out_shape[1] * out_shape[2], out_shape[3])
    if columns % 128 or rows % 16:
        out = jnp.zeros(out_shape, F32) if so_far is None else so_far.reshape(out_shape)
        ordered = jnp.stack(parts)[..., column * columns : (column + 1) * columns]
        for k in range(count):
            block = jnp.take(ordered[k ^ flips[0]], z_places, axis=0)
            c, x = (k, flips[1]) if count == 2 else (k // 2, k % 2)
            at = [0 if v is None else v for v in spot(c, x, y_at)]
            block = block.reshape(size + (rows, columns)).astype(F32)
            out = lax.dynamic_update_slice(out, block, (at[0], at[1], 0, at[2] * columns))
        return out.reshape(flat)
    maps = jnp.concatenate([jnp.stack(flips).astype(jnp.int32), z_places])

    def out_map(k, maps):
        at = spot(k, maps[1], maps[2]) if count == 2 else spot(k // 2, k % 2, maps[2])
        at = [0 if v is None else v for v in at]
        return (at[0], at[1], 0, at[2])

    specs = [pl.BlockSpec((z_count, rows, columns), lambda k, maps: (0, 0, column))] * count
    operands = list(parts)
    aliases = {}
    if so_far is not None:
        specs.append(ANY)
        operands.append(so_far.reshape(out_shape))
        aliases = {count + 1: 0}
    return kernel_call(
        functools.partial(widen_kernel, count),
        grid_spec=pltpu.PrefetchScalarGridSpec(
            num_scalar_prefetch=1,
            grid=(count,),
            in_specs=specs,
            out_specs=pl.BlockSpec(size + (rows, columns), out_map),
        ),
        out_shape=jax.ShapeDtypeStruct(out_shape, F32),
        input_output_aliases=aliases,
    )(maps, *operands).reshape(flat)


def once_kernel(function, n_in, maps, *refs):
    function(maps, refs[:n_in], refs[n_in:])


def once(function, shapes, *operands, maps=None):
    if maps is None:
        maps = jnp.zeros((1,), jnp.int32)
    return kernel_call(
        functools.partial(once_kernel, function, len(operands)),
        in_specs=[pl.BlockSpec(memory_space=pltpu.SMEM)]
        + [pl.BlockSpec(memory_space=pltpu.VMEM)] * len(operands),
        out_specs=[pl.BlockSpec(memory_space=pltpu.VMEM)] * len(shapes),
        out_shape=[jax.ShapeDtypeStruct(shape, kind) for shape, kind in shapes],
    )(maps, *operands)


def add_halves(kept, got):
    half = kept.shape[0] // 2
    if not half:

        def narrow(_, ins, outs):
            outs[0][...] = (ins[0][...].astype(F32) + ins[1][...].astype(F32)).astype(BF)

        return once(narrow, [(kept.shape, BF)], kept, got)

    def function(_, ins, outs):
        for n in range(2):
            part = pl.ds(n * half, half)
            outs[n][...] = (ins[0][part].astype(F32) + ins[1][part].astype(F32)).astype(BF)

    shape = ((half,) + kept.shape[1:], BF)
    return once(function, [shape, shape], kept, got)


def stack_two(held, got):
    count = held.shape[0]

    def function(_, ins, outs):
        outs[0][:count] = ins[0][...]
        outs[0][count:] = ins[1][...]

    return once(function, [((2 * count,) + held.shape[1:], BF)], held, got)[0]


def kv_kernel(rows, tokens, gain, cosine, sine, *refs):
    pieces = refs[:-4]
    normed, keyval, w_kv, sem = refs[-4:]
    copies = []
    for n, piece in enumerate(pieces):
        start = pl.multiple_of(rows[n], 16)
        copies.append(
            pltpu.make_async_copy(piece, w_kv.at[pl.ds(start, piece.shape[0])], sem.at[n])
        )
    for copy in copies:
        copy.start()
    inputs = tokens[...].astype(F32)
    normed[...] = (inputs * rms_factor(inputs) * gain[...]).astype(BF)
    for copy in copies:
        copy.wait()
    raw = dot(normed[...], w_kv[...])
    keyval[:, :HD] = rotate(raw[:, :HD], cosine[...], sine[...]).astype(BF)
    keyval[:, HD:] = raw[:, HD:].astype(BF)


def norm_back_rows(grad_normed, values, factor, gain):
    scaled = grad_normed * gain
    mean = jnp.mean(scaled * values, axis=-1, keepdims=True)
    return factor * scaled - values * (factor * factor * factor) * mean


def attend_kernel(n_q, spans, maps, *refs):
    normed, bias, cosine, sine = refs[:4]
    blocks = refs[4 : 4 + spans]
    pieces = refs[4 + spans : 4 + spans + n_q]
    queries, attended, softs, w_q, keys, values, sem = refs[4 + spans + n_q :]
    step = pl.program_id(0)
    rows = normed.shape[0]

    @pl.when(step == 0)
    def _():
        copies = load_rows(w_q, pieces, [maps[spans + n] for n in range(n_q)], sem)
        for n in range(spans):
            keys[n * rows : (n + 1) * rows, :] = blocks[n][0, :, :HD]
            values[n * rows : (n + 1) * rows, :] = blocks[n][0, :, HD:]
        for copy in copies:
            copy.wait()

    wide = queries.shape[1]
    heads = wide // HD
    columns = pl.ds(pl.multiple_of(step * wide, HD), wide)
    raw = dot(normed[...], w_q[:, columns])
    stacked = []
    for n in range(heads):
        turned = rotate(raw[:, n * HD : (n + 1) * HD], cosine[...], sine[...])
        query = (turned * HD ** (-0.5)).astype(BF)
        queries[:, n * HD : (n + 1) * HD] = query
        stacked.append(query)
    scores = dot_t(jnp.concatenate(stacked, axis=0), keys[...])
    scores = scores.reshape(heads, rows, scores.shape[1]) + bias[...][None]
    weights = jnp.exp(scores - jnp.max(scores, axis=-1, keepdims=True))
    soft = (weights * (1.0 / jnp.sum(weights, axis=-1, keepdims=True))).astype(BF)
    softs[...] = soft
    result = dot(soft.reshape(heads * rows, soft.shape[2]), values[...]).astype(BF)
    for n in range(heads):
        attended[:, n * HD : (n + 1) * HD] = result[n * rows : (n + 1) * rows]


def project_kernel(n_o, rows, *refs):
    attended, tokens, gain = refs[:3]
    pieces = refs[3 : 3 + n_o]
    hidden, own_norm, factor, w_o, sem = refs[3 + n_o :]
    for copy in load_rows(w_o, pieces, [rows[n] for n in range(n_o)], sem):
        copy.wait()
    out = tokens[...].astype(F32) + dot(attended[...], w_o[...])
    hidden[...] = out
    scale = rms_factor(out)
    factor[...] = jnp.broadcast_to(scale, factor.shape)
    own_norm[...] = (out * scale * gain[...]).astype(BF)


def attend_back_kernel(n_o, spans, entry_count, maps, *refs):
    d_attn, queries, softs, cosine, sine = refs[:5]
    blocks = refs[5 : 5 + spans]
    pieces = refs[5 + spans : 5 + spans + n_o]
    d_raw, kept, sent = refs[5 + spans + n_o : 8 + spans + n_o]
    w_o, keys, values, d_keys, d_values, d_window, sem = refs[8 + spans + n_o :]
    step = pl.program_id(0)
    rows = d_attn.shape[0]

    @pl.when(step == 0)
    def _():
        base = spans + entry_count
        copies = load_rows(w_o, pieces, [maps[base + n] for n in range(n_o)], sem)
        for n in range(spans):
            keys[n * rows : (n + 1) * rows, :] = blocks[n][0, :, :HD]
            values[n * rows : (n + 1) * rows, :] = blocks[n][0, :, HD:]
        d_keys[...] = jnp.zeros_like(d_keys)
        d_values[...] = jnp.zeros_like(d_values)
        for copy in copies:
            copy.wait()

    wide = queries.shape[1]
    heads = wide // HD
    w_rows = pl.ds(pl.multiple_of(step * wide, HD), wide)
    d_both = dot_t(d_attn[...], w_o[w_rows, :]).astype(BF)
    query = jnp.concatenate([queries[:, n * HD : (n + 1) * HD] for n in range(heads)], axis=0)
    d_out = jnp.concatenate([d_both[:, n * HD : (n + 1) * HD] for n in range(heads)], axis=0)
    flat_soft = softs[...].reshape(heads * rows, softs.shape[2])
    d_soft = dot_t(d_out, values[...])
    wide_soft = flat_soft.astype(F32)
    delta = jnp.sum(wide_soft * d_soft, axis=-1, keepdims=True)
    d_scores = (wide_soft * (d_soft - delta)).astype(BF)
    d_query = dot(d_scores, keys[...]) * HD ** (-0.5)
    for n in range(heads):
        back = rotate(d_query[n * rows : (n + 1) * rows], cosine[...], -sine[...])
        d_raw[:, n * HD : (n + 1) * HD] = back.astype(BF)
    d_keys[...] += t_dot(query, d_scores)
    d_values[...] += t_dot(d_out, flat_soft)

    @pl.when(step == pl.num_programs(0) - 1)
    def _():
        d_window[: spans * rows, :HD] = d_keys[...].T.astype(BF)
        d_window[: spans * rows, HD:] = d_values[...].T.astype(BF)
        d_window[spans * rows :, :] = jnp.zeros((rows, 2 * HD), BF)
        for n in range(entry_count):
            out = kept if n < entry_count // 2 else sent
            start = pl.multiple_of(maps[spans + n] * rows, rows)
            out[n % (entry_count // 2)] = d_window[pl.ds(start, rows), :]


ROOT = math.sqrt(2.0 / math.pi)


def forward_kernel(n_tok, maps, *refs):
    pieces = refs[:n_tok]
    cot, w_gate, w_up, w_down = refs[n_tok : n_tok + 4]
    inner, inner_t, d_both, normed_t, normed, sem = refs[n_tok + 4 :]

    @pl.when(pl.program_id(0) == 0)
    def _():
        at = 0
        copies = []
        for n, piece in enumerate(pieces):
            copies.append(
                pltpu.make_async_copy(piece, normed.at[pl.ds(at, piece.shape[0])], sem.at[n])
            )
            at += piece.shape[0]
        for copy in copies:
            copy.start()
        for copy in copies:
            copy.wait()

    wide = normed_t.shape[0]
    columns = pl.ds(pl.multiple_of(pl.program_id(0) * wide, 128), wide)
    gate, up = dot(normed[...], w_gate[...]), dot(normed[...], w_up[...])
    d_inner = dot_t(cot[...], w_down[...])
    square = gate * gate
    bent = jnp.tanh(ROOT * (gate + 0.044715 * (square * gate)))
    half = 0.5 * (1.0 + bent)
    active = gate * half
    slope = half + 0.5 * gate * (1.0 - bent * bent) * (ROOT * (1.0 + 3 * 0.044715 * square))
    result = (active * up).astype(BF)
    inner[...] = result
    inner_t[...] = result.T
    d_both[0] = (d_inner * up * slope).astype(BF)
    d_both[1] = (d_inner * active).astype(BF)
    normed_t[...] = normed[:, columns].T


def cut_rows(results, picks, outs):
    for out, starts in zip(outs, picks, strict=True):
        rows = out.shape[1]
        for n, start in enumerate(starts):
            for result in results:
                if start < result.shape[0]:
                    out[n] = result[start : start + rows].astype(BF)
                    break
                start -= result.shape[0]


def back_kernel(picks, n_parts, *refs):
    w_gu, outs = refs[n_parts], refs[n_parts + 1 :]
    units = refs[0].shape[2]
    results = [
        dot_t(part[0], w_gu[:, :units]) + dot_t(part[1], w_gu[:, units:]) for part in refs[:n_parts]
    ]
    cut_rows(results, picks, outs)


def down_kernel(picks, n_parts, maps, *refs):
    w_down, outs = refs[n_parts], refs[n_parts + 1 :]
    cut_rows([dot(part[...], w_down[...]) for part in refs[:n_parts]], picks, outs)


def grad_kernel(turned, n_parts, groups, block_rows, added, maps, *refs):
    product = dot if turned else t_dot
    lefts, rights = refs[:n_parts], refs[n_parts : 2 * n_parts]
    refs = refs[2 * n_parts :]
    result = sum(
        product(left[...], right[...].reshape(right.shape[-2:]))
        for left, right in zip(lefts, rights, strict=True)
    )
    if added:
        result = result + refs[0][...].astype(F32)
    outs = refs[1:] if added else refs
    if groups is None:
        outs[0][...] = result.astype(BF)
        return
    total = outs[-1]
    total[...] = result
    place = 0
    for n, count in enumerate(groups):
        for k in range(count):
            start = pl.multiple_of(maps[2 + place] * block_rows, 16)
            outs[n][k] = total[pl.ds(start, block_rows), :].astype(BF)
            place += 1


def grad(
    lefts, left_block, left_columns, rights, half, added=None, groups=None, order=None, turned=False
):
    right = rights[0]
    if right.ndim == 3:
        columns = right.shape[2]
    else:
        columns = right.shape[1] // 2
    blocks = 0 if groups is None else sum(groups)
    block_rows = 0 if groups is None else left_columns // blocks
    if columns % 128 or left_columns % 128 or block_rows % 16:
        result = 0
        for left, right in zip(lefts, rights, strict=True):
            cut = lax.dynamic_slice_in_dim(
                left, left_block * left_columns, left_columns, 0 if turned else 1
            )
            if right.ndim == 3:
                other = pick(right, half, 0)
            else:
                other = lax.dynamic_slice_in_dim(right, half * columns, columns, 1)
            result = result + (dot(cut, other) if turned else t_dot(cut, other))
        if added is not None:
            result = result + added.astype(F32)
        result = result.astype(BF)
        if groups is None:
            return result
        result = jnp.take(result.reshape(blocks, block_rows, columns), order, axis=0)
        outs, at = [], 0
        for count in groups:
            outs.append(result[at : at + count])
            at += count
        return outs
    wide = 384 if columns % 384 == 0 else (256 if columns % 256 == 0 else 128)
    steps = columns // wide
    maps = jnp.stack([jnp.asarray(left_block, jnp.int32), jnp.asarray(half, jnp.int32)])
    if groups is not None:
        maps = jnp.concatenate([maps, order.astype(jnp.int32)])
    in_specs = []
    for left in lefts:
        if turned:
            shape = (left_columns, left.shape[1])
            in_specs.append(pl.BlockSpec(shape, lambda i, maps: (maps[0], 0)))
        else:
            shape = (left.shape[0], left_columns)
            in_specs.append(pl.BlockSpec(shape, lambda i, maps: (0, maps[0])))
    for right in rights:
        if right.ndim == 3:
            shape = (1, right.shape[1], wide)
            in_specs.append(pl.BlockSpec(shape, lambda i, maps: (maps[1], 0, i)))
        else:
            shape = (right.shape[0], wide)
            in_specs.append(pl.BlockSpec(shape, lambda i, maps: (0, maps[1] * steps + i)))
    operands = list(lefts) + list(rights)
    if added is not None:
        in_specs.append(pl.BlockSpec((left_columns, wide), lambda i, maps: (0, i)))
        operands.append(added)
    scratch = []
    if groups is None:
        shapes = [jax.ShapeDtypeStruct((left_columns, columns), BF)]
        out_specs = [pl.BlockSpec((left_columns, wide), lambda i, maps: (0, i))]
    else:
        shapes = [jax.ShapeDtypeStruct((count, block_rows, columns), BF) for count in groups]
        out_specs = [
            pl.BlockSpec((count, block_rows, wide), lambda i, maps: (0, 0, i)) for count in groups
        ]
        scratch = [pltpu.VMEM((left_columns, wide), F32)]
    outs = kernel_call(
        functools.partial(grad_kernel, turned, len(lefts), groups, block_rows, added is not None),
        grid_spec=pltpu.PrefetchScalarGridSpec(
            num_scalar_prefetch=1,
            grid=(steps,),
            in_specs=in_specs,
            out_specs=out_specs,
            scratch_shapes=scratch,
        ),
        out_shape=shapes,
    )(maps, *operands)
    return outs[0] if groups is None else outs


class Clock:
    def __init__(self):
        self.marks = ()

    def tie(self, value):
        return after(value, *self.marks) if self.marks else value

    def mark(self, *values):
        self.marks = values


PLAN = (
    "D",
    "WO",
    "D",
    "back",
    "ba",
    "O",
    "D",
    "W",
    "a",
    "b",
    "down",
    "e",
    "O",
    "Dab",
    "hid",
    "att",
    "TO",
    "W",
    "QD",
    "ve",
    "T",
    "v",
    "Q",
    "W",
    "e",
    "Dv",
    "TWvQ",
    "O",
    "tok",
    "KW",
    "O",
    "D",
    "Q",
    "K",
    "Q",
    "K",
    "O",
    "WQK",
    "W",
    "QK",
    "D",
    "Q",
    "OK",
    "KO",
    "K",
    "Q",
    "K",
    "Q",
    "K",
)


def body(
    tokens,
    cotangent,
    lengths,
    block_of,
    gain_attn,
    w_query,
    w_keyval,
    w_out,
    gain_mlp,
    w_gateup,
    w_down,
):
    tok_rows, width = tokens.shape
    y_count, z_count = lax.axis_size("y"), lax.axis_size("z")
    ctx_count = 4 * z_count
    z_levels = z_count.bit_length() - 1
    x_at, c_at, y_at, z_at = (lax.axis_index(name) for name in ("x", "c", "y", "z"))
    own_index = (z_at * 2 + x_at) * 2 + c_at
    deep = w_query.shape[0]
    quarter = deep // 4
    units = FF // (2 * y_count)
    half_tok = tok_rows // 2
    group = 2 * y_count
    others = range(1, y_count)
    clock = Clock()
    tie, mark = clock.tie, clock.mark

    def together(*values):
        return lax.optimization_barrier(values + clock.marks)[: len(values)]


    own_gains = jnp.zeros((16, deep), BF).at[0].set(gain_attn).at[1].set(gain_mlp)
    got_gains = [shift(own_gains, "y", r) for r in others]
    kv_weights = [w_keyval] + [shift(w_keyval, "y", r) for r in others]
    place_cx = c_at * 2 + x_at
    place_cz = c_at * 2 + (z_at & 1)

    def rows_of(weight, place):
        return lax.dynamic_slice_in_dim(weight, place * quarter, quarter, 0)

    wq_piece = after(rows_of(w_query, place_cx), own_gains)
    wq_y = {r: shift(wq_piece, "y", r) for r in others}
    wo_piece = after(rows_of(w_out, place_cx), wq_piece)
    wo_y = {r: shift(wo_piece, "y", r) for r in others}
    cot_x = shift(after(cotangent, wo_piece), "x", 1)
    gu_sent = {}
    for r in others:
        column = ((y_at ^ r) * 2 + x_at) * units
        moves = [
            (0, (quarter, units), (place_cz * quarter, part * FF + column), (0, part * units))
            for part in (0, 1)
        ]
        gu_sent[r] = lay_out((quarter, 2 * units), [after(w_gateup, wo_piece)], moves)

    def listed(shard, found, place):
        pieces, rows = [shard], [y_at * deep]
        for r, quarters in found.items():
            for s, piece in enumerate(quarters):
                pieces.append(piece)
                rows.append((y_at ^ r) * deep + (place ^ s) * piece.shape[0])
        return pieces, rows

    device_ids = jnp.arange(ctx_count, dtype=jnp.int32)
    block_row = block_of[0]
    own_block = jnp.sum(jnp.where(device_ids == own_index, block_row, 0))
    own_start = own_block * tok_rows
    owners = jnp.sum(
        jnp.where(block_row[None, :] == device_ids[:, None], device_ids[None, :], 0), axis=1
    )
    seq_lengths = lengths[0]
    query_places = own_start + jnp.arange(tok_rows, dtype=jnp.int32)
    key_places = own_start - WINDOW + jnp.arange(WINDOW + tok_rows, dtype=jnp.int32)
    query_segment, query_position = segment_info(query_places, seq_lengths)
    key_segment = segment_info(key_places, seq_lengths)[0]
    distance = query_places[:, None] - key_places[None, :]
    allowed = (
        (query_segment[:, None] == key_segment[None, :])
        & (key_places >= 0)[None, :]
        & (distance >= 0)
        & (distance < WINDOW)
    )
    bias = jnp.where(allowed, 0.0, -1e30).astype(F32)
    cosine, sine = tables(query_position, HD)
    cosine = jnp.concatenate([cosine, cosine], axis=1)
    sine = jnp.concatenate([-sine, sine], axis=1)
    spans = WINDOW // tok_rows + 1
    first_block = own_block - (spans - 1)

    def entry_of(ctx_index):
        differ = ctx_index ^ own_index
        return ((differ >> 1) & 1) | ((differ >> 2) << 1) | ((differ & 1) << (z_levels + 1))

    window = first_block + jnp.arange(spans, dtype=jnp.int32)
    window = entry_of(jnp.take(owners, jnp.clip(window, 0, ctx_count - 1)))
    entries = jnp.arange(ctx_count, dtype=jnp.int32)
    differ = ((entries >> 1) & (z_count - 1)) << 2
    differ = differ | ((entries & 1) << 1) | (entries >> (z_levels + 1))
    entry_block = jnp.take(block_row, differ ^ own_index) - first_block
    entry_block = jnp.where((entry_block >= 0) & (entry_block < spans), entry_block, spans)

    z_places = jnp.zeros((z_count,), jnp.int32)
    z_differ = jnp.arange(z_count, dtype=jnp.int32) ^ z_at
    for n, level in enumerate(reversed(range(z_levels))):
        z_places = z_places | (((z_differ >> level) & 1) << n)
    z_order = jnp.zeros((z_count,), jnp.int32)
    for level in range(z_levels):
        z_order = z_order | (
            ((jnp.arange(z_count, dtype=jnp.int32) >> (z_levels - 1 - level)) & 1) << level
        )
    z_order = z_order ^ z_at

    gains = by_place([own_gains[:2]] + [g[:2] for g in got_gains], "y")
    gains = jnp.swapaxes(gains, 0, 1).reshape(2, width).astype(F32)
    gain_one, gain_two = gains[:1], gains[1:]
    kv_rows = jnp.stack([(y_at ^ r) * deep for r in range(y_count)]).astype(jnp.int32)
    in_vmem = pl.BlockSpec(memory_space=pltpu.VMEM)
    normed, keyval = kernel_call(
        kv_kernel,
        in_specs=[pl.BlockSpec(memory_space=pltpu.SMEM)] + [in_vmem] * 4 + [ANY] * y_count,
        out_specs=[in_vmem, in_vmem],
        out_shape=[
            jax.ShapeDtypeStruct((tok_rows, width), BF),
            jax.ShapeDtypeStruct((tok_rows, 2 * HD), BF),
        ],
        scratch_shapes=[pltpu.VMEM((width, 2 * HD), BF), pltpu.SemaphoreType.DMA((y_count,))],
    )(kv_rows, tokens, gain_one, cosine, sine, *kv_weights)
    mark(keyval, bias, z_order, z_places, entry_block, window)
    held = stack_two(keyval[None], tie(shift(keyval, "x", 1)[None]))
    mark(held)
    over_z = [shift(held, "z", d) for d in range(1, z_count)]
    wq_y = {r: tie(piece) for r, piece in wq_y.items()}
    mark(*wq_y.values())
    wq_found = {r: [piece, shift(piece, "x", 1)] for r, piece in wq_y.items()}

    def stack_all(_, ins, outs):
        for n, part in enumerate(ins):
            outs[0][n * 2 : n * 2 + 2] = part[...]

    held = once(
        stack_all,
        [((2 * z_count, tok_rows, 2 * HD), BF)],
        held,
        *[tie(part) for part in over_z],
    )[0]
    mark(held)
    across = shift(held, "c", 1)
    count = y_count - 1
    gu_y = {r: shift(piece, "y", r) for r, piece in gu_sent.items()}
    joint = [wq_found[r][1] for r in others] + [wo_y[r] for r in others]
    joint = together(cot_x, *joint, *[gu_y[r] for r in others])
    cot_x, joint = joint[0], joint[1:]
    mark(cot_x, *joint)
    wq_found = {r: [wq_found[r][0], joint[n]] for n, r in enumerate(others)}
    wo_y = {r: joint[count + n] for n, r in enumerate(others)}
    gu_y = {r: joint[2 * count + n] for n, r in enumerate(others)}
    wq_found = {r: pair + [shift(p, "c", 1) for p in pair] for r, pair in wq_found.items()}
    wo_found = {r: [piece, shift(piece, "x", 1)] for r, piece in wo_y.items()}
    gu_z = {r: shift(piece, "z", 1) for r, piece in gu_y.items()}
    cot_y = {r: shift(tie(cotangent), "y", r) for r in others}

    all_kv = stack_two(held, tie(across))
    mark(all_kv)
    q_pieces, q_rows = listed(w_query, wq_found, place_cx)
    q_pieces = [tie(piece) for piece in q_pieces]
    n_q = len(q_pieces)
    heads = 4
    pairs = H // heads
    kv_specs = [
        pl.BlockSpec((1, tok_rows, 2 * HD), lambda i, maps, n=n: (maps[n], 0, 0))
        for n in range(spans)
    ]
    pair_spec = pl.BlockSpec((tok_rows, heads * HD), lambda i, maps: (0, i))
    token_spec = pl.BlockSpec((tok_rows, width), lambda i, maps: (0, 0))
    maps = jnp.concatenate([window, jnp.stack(q_rows).astype(jnp.int32)])
    small = [bias, cosine, sine]
    soft_spec = pl.BlockSpec((heads, tok_rows, spans * tok_rows), lambda i, maps: (i, 0, 0))
    queries, attended, softs = kernel_call(
        functools.partial(attend_kernel, n_q, spans),
        grid_spec=pltpu.PrefetchScalarGridSpec(
            num_scalar_prefetch=1,
            grid=(pairs,),
            in_specs=[token_spec] + [whole_spec(a) for a in small] + kv_specs + [ANY] * n_q,
            out_specs=[pair_spec, pair_spec, soft_spec],
            scratch_shapes=[
                pltpu.VMEM((width, H * HD), BF),
                pltpu.VMEM((spans * tok_rows, HD), BF),
                pltpu.VMEM((spans * tok_rows, HD), BF),
                pltpu.SemaphoreType.DMA((n_q,)),
            ],
        ),
        out_shape=[
            jax.ShapeDtypeStruct((tok_rows, H * HD), BF),
            jax.ShapeDtypeStruct((tok_rows, H * HD), BF),
            jax.ShapeDtypeStruct((H, tok_rows, spans * tok_rows), BF),
        ],
    )(maps, tie(normed), *small, *([all_kv] * spans), *q_pieces)
    joint = [wo_found[r][1] for r in others] + [gu_z[r] for r in others]
    joint = together(attended, *joint, *[cot_y[r] for r in others])
    attended, joint = joint[0], joint[1:]
    mark(attended, *joint)
    wo_found = {r: [wo_found[r][0], joint[n]] for n, r in enumerate(others)}
    gu_found = {r: [gu_y[r], joint[count + n]] for n, r in enumerate(others)}
    cot_y = {r: joint[2 * count + n] for n, r in enumerate(others)}
    wo_found = {r: pair + [shift(p, "c", 1) for p in pair] for r, pair in wo_found.items()}
    gu_found = {r: pair + [shift(p, "c", 1) for p in pair] for r, pair in gu_found.items()}
    o_pieces, o_rows = listed(w_out, wo_found, place_cx)
    n_o = len(o_pieces)
    hidden, own_norm, factor = kernel_call(
        functools.partial(project_kernel, n_o),
        in_specs=[pl.BlockSpec(memory_space=pltpu.SMEM)] + [in_vmem] * 3 + [ANY] * n_o,
        out_specs=[in_vmem] * 3,
        out_shape=[
            jax.ShapeDtypeStruct((tok_rows, width), F32),
            jax.ShapeDtypeStruct((tok_rows, width), BF),
            jax.ShapeDtypeStruct((tok_rows, HD), F32),
        ],
        scratch_shapes=[pltpu.VMEM((H * HD, width), BF), pltpu.SemaphoreType.DMA((n_o,))],
    )(jnp.stack(o_rows).astype(jnp.int32), attended, tokens, gain_two, *o_pieces)
    mark(own_norm)

    norm_y = {r: shift(own_norm, "y", r) for r in others}
    norm_x = shift(own_norm, "x", 1)
    cot_a = {r: shift(part[:half_tok], "x", 1) for r, part in cot_y.items()}
    cot_b = {r: shift(cot_x[half_tok:], "y", r) for r in others}
    cot_near = jnp.concatenate([cotangent, *[cot_y[r] for r in others], cot_x], axis=0)
    gu_moves = [
        (0, (deep, units), (0, part * FF + (y_at * 2 + x_at) * units), (y_at * deep, part * units))
        for part in (0, 1)
    ]
    gu_pieces, gu_rows = listed(w_gateup, gu_found, place_cz)
    for n in range(1, len(gu_pieces)):
        gu_moves.append((n, (quarter, 2 * units), (0, 0), (gu_rows[n], 0)))
    w_gu = lay_out((width, 2 * units), gu_pieces, gu_moves)
    mark(w_gu, cot_near)
    norm_slices = {r: tie(part)[:half_tok] for r, part in norm_y.items()}
    norm_slice = tie(norm_x)[half_tok:]
    mark(norm_slice, *norm_slices.values())
    norm_a = {r: shift(part, "x", 1) for r, part in norm_slices.items()}
    norm_b = {r: shift(norm_slice, "y", r) for r in others}
    near = [tie(own_norm), *[norm_y[r] for r in others], norm_x]
    far, cot_far = [], []
    for r in others:
        far += [norm_a[r], norm_b[r]]
        cot_far += [cot_a[r], cot_b[r]]
    many = group * tok_rows
    fits = units % 128 == 0
    picks = [
        [r * tok_rows for r in range(y_count)],
        [(y_count + r) * tok_rows for r in range(y_count)],
        [half_tok, y_count * tok_rows + half_tok],
    ]
    picks += [[r * tok_rows + half_tok, (y_count + r) * tok_rows + half_tok] for r in others]
    cut_shapes = [jax.ShapeDtypeStruct((len(pick_), half_tok, width), BF) for pick_ in picks]
    x_maps = jnp.stack([x_at]).astype(jnp.int32)

    out_picks = [[r * tok_rows, (y_count + r) * tok_rows] for r in range(y_count)]
    out_shapes = [jax.ShapeDtypeStruct((2, tok_rows, width), BF)] * y_count

    def cut(result, places, rows):
        return [
            jnp.stack([result[start : start + rows].astype(BF) for start in starts])
            for starts in places
        ]

    if fits:
        wide = 384 if units % 384 == 0 else 128
        steps = units // wide
        turn = width // steps
        block = 512
        cut_specs = [
            pl.BlockSpec((len(starts), half_tok, block), lambda i, *_: (0, 0, i))
            for starts in picks
        ]

        def forward(pieces, cot):
            n_tok, rows = len(pieces), cot.shape[0]
            return kernel_call(
                functools.partial(forward_kernel, n_tok),
                grid_spec=pltpu.PrefetchScalarGridSpec(
                    num_scalar_prefetch=1,
                    grid=(steps,),
                    in_specs=[ANY] * n_tok
                    + [
                        pl.BlockSpec((rows, width), lambda i, maps: (0, 0)),
                        pl.BlockSpec((width, wide), lambda i, maps: (0, i)),
                        pl.BlockSpec((width, wide), lambda i, maps: (0, steps + i)),
                        pl.BlockSpec((wide, width), lambda i, maps: (maps[0] * steps + i, 0)),
                    ],
                    out_specs=[
                        pl.BlockSpec((rows, wide), lambda i, maps: (0, i)),
                        pl.BlockSpec((wide, rows), lambda i, maps: (i, 0)),
                        pl.BlockSpec((2, rows, wide), lambda i, maps: (0, 0, i)),
                        pl.BlockSpec((turn, rows), lambda i, maps: (i, 0)),
                    ],
                    scratch_shapes=[
                        pltpu.VMEM((rows, width), BF),
                        pltpu.SemaphoreType.DMA((n_tok,)),
                    ],
                ),
                out_shape=[
                    jax.ShapeDtypeStruct((rows, units), BF),
                    jax.ShapeDtypeStruct((units, rows), BF),
                    jax.ShapeDtypeStruct((2, rows, units), BF),
                    jax.ShapeDtypeStruct((width, rows), BF),
                ],
            )(x_maps, *pieces, cot, w_gu, w_gu, w_down)

        results = forward(near, cot_near)
        mark(*results)
        joint = together(*far, *cot_far)
        far, cot_far = joint[: len(far)], jnp.concatenate(joint[len(far) :], axis=0)
        results = list(zip(results, forward(far, cot_far), strict=True))
        inner_act, inner_t, d_both, normed_t = results
        cots = (cot_near, cot_far)

        def back_cut():
            return kernel_call(
                functools.partial(back_kernel, picks, len(d_both)),
                grid=(width // block,),
                in_specs=[whole_spec(part) for part in d_both]
                + [pl.BlockSpec((block, 2 * units), lambda i: (i, 0))],
                out_specs=cut_specs,
                out_shape=cut_shapes,
            )(tie(d_both[0]), *d_both[1:], w_gu)

        def down_cut():
            return kernel_call(
                functools.partial(down_kernel, out_picks, len(inner_act)),
                grid_spec=pltpu.PrefetchScalarGridSpec(
                    num_scalar_prefetch=1,
                    grid=(width // block,),
                    in_specs=[whole_spec(part) for part in inner_act]
                    + [pl.BlockSpec((units, block), lambda i, maps: (maps[0], i))],
                    out_specs=[pl.BlockSpec((2, tok_rows, block), lambda i, *_: (0, 0, i))]
                    * y_count,
                ),
                out_shape=out_shapes,
            )(x_maps, tie(inner_act[0]), *inner_act[1:], w_down)

    else:
        normed2 = jnp.concatenate(near + far, axis=0)
        cot_all = jnp.concatenate([cot_near, *cot_far], axis=0)
        w_dn = lax.dynamic_slice_in_dim(w_down, x_at * units, units, 0)
        d_inner = dot_t(cot_all, w_dn)
        both_parts = dot(normed2, w_gu)
        active, back = jax.vjp(
            lambda values: jax.nn.gelu(values, approximate=True), both_parts[:, :units]
        )
        up_part = both_parts[:, units:]
        inner_act = (active * up_part).astype(BF)
        d_both = [jnp.stack([back(d_inner * up_part)[0], d_inner * active]).astype(BF)]
        inner_t, normed_t, cots = [inner_act.T], [normed2.T], [cot_all]

        def back_cut():
            both = tie(d_both[0])
            result = dot_t(both[0], w_gu[:, :units]) + dot_t(both[1], w_gu[:, units:])
            return cut(result, picks, half_tok)

        def down_cut():
            return cut(dot(tie(inner_act), w_dn), out_picks, tok_rows)

    mark(*d_both)

    def back_a(cuts_in, result):
        keep, send = cuts_in[0], cuts_in[1]
        got = yield [(send, "x", 1)]

        def function(_, ins, outs):
            for n in range(y_count):
                outs[n][...] = (ins[0][n].astype(F32) + ins[1][n].astype(F32)).astype(BF)

        left = once(function, [((half_tok, width), BF)] * y_count, keep, got[0])
        got = yield [(left[r], "y", r) for r in others]
        result["a"] = [left[0]] + got

    def back_b(cuts_in, result):
        keep, send = cuts_in[2], cuts_in[3:]
        got = yield [(part, "y", r) for r, part in zip(others, send, strict=True)]

        def function(_, ins, outs):
            for n in range(2):
                outs[n][...] = sum(ref[n].astype(F32) for ref in ins).astype(BF)

        left = once(function, [((half_tok, width), BF)] * 2, keep, *got)
        got = yield [(left[1], "x", 1)]
        result["b"] = [left[0]] + got

    def sum_rows(ins, n_first):
        first = sum(ref[...].astype(F32) for ref in ins[:n_first])
        second = sum(ref[...].astype(F32) for ref in ins[n_first : n_first + 2])
        return jnp.concatenate([first, second], axis=0)

    def back_whole(keep, sent, result):
        got = yield [(part, "y", r) for r, part in zip(others, sent, strict=True)]

        def function(_, ins, outs):
            for n in range(2):
                outs[n][...] = sum(ref[n].astype(F32) for ref in ins).astype(BF)

        left = once(function, [((tok_rows, width), BF)] * 2, keep, *got)
        got = yield [(left[1], "x", 1)]
        result += [left[0]] + got

    def scatter_z(kept, sent):
        for level in range(z_levels):
            got = yield [(sent, "z", 1 << level)]
            sums = add_halves(kept, got[0])
            kept, sent = sums[0], sums[-1]
        return kept

    def spread(piece, finish, split=True):
        held = piece
        for level in reversed(range(z_levels)):
            got = yield [(held, "z", 1 << level)]
            held = stack_two(held, got[0])
        beside, across = yield [(held, "x", 1), (held, "c", 1)]
        corner = yield [(beside, "c", 1)]
        if split:
            mark(finish([tie(held), across], False))
            mark(finish([tie(beside), corner[0]], True))
        else:
            mark(finish([tie(held), beside, across, corner[0]], False))

    z_groups = [z_count // 2, z_count // 2]

    found = {}

    def finish_down(parts, beside):
        found["down"] = widen(
            parts,
            beside,
            z_places,
            (2, z_count, w_down.shape[0] // (2 * z_count), width),
            lambda c, x, y: (x, None, c),
            found.get("down"),
        )
        return found["down"]

    def finish_up(r):
        def finish(parts, beside):
            found["up"] = widen(
                parts,
                beside,
                z_places,
                (1, z_count, deep // z_count, 2 * FF),
                lambda c, x, y: (0, None, (c * y_count + (y ^ r)) * 2 + x),
                found.get("up"),
            )
            return found["up"]

        return finish

    def finish_attn(names, cols):
        def finish(parts, _):
            rows = deep // (2 * z_count)
            for n, name in enumerate(names):
                found[name] = widen(
                    parts,
                    False,
                    z_places,
                    (z_count, 2, rows, 2 * cols),
                    lambda c, x, y: (None, x, c),
                    None,
                    n,
                    cols,
                )
                mark(found[name])
            return found[names[-1]]

        return finish

    def ffn_chain(job, finish, r):
        left, left_block, left_rows, right = job
        left = [tie(left[0])] + list(left[1:])
        theirs = grad(left, left_block, left_rows, right, 1 - c_at, turned=True)
        got = yield [(theirs, "c", 1)]
        kept, sent = grad(
            left, left_block, left_rows, right, c_at, got[0], z_groups, z_order, turned=True
        )
        piece = yield from scatter_z(kept, sent)
        if r:
            got = yield [(piece, "y", r)]
            piece = got[0]
        yield from spread(piece, finish)

    y_order = jnp.arange(y_count, dtype=jnp.int32) ^ y_at
    xz_maps = jnp.concatenate([z_order * 2 + x_at, z_order * 2 + (1 - x_at)])

    cut_rows_x = deep // (2 * z_count)

    def cut_x(*parts_of):
        widths = [parts[0].shape[1] for parts in parts_of]
        flat = [part for parts in parts_of for part in parts]
        total_width = sum(widths)
        if cut_rows_x % 16:
            total = jnp.concatenate([sum(v.astype(F32) for v in parts) for parts in parts_of], axis=1)
            blocks = total.astype(BF).reshape(2 * z_count, cut_rows_x, total_width)
            blocks = jnp.take(blocks, xz_maps, axis=0)
            return blocks[:z_count], blocks[z_count:]

        def function(maps, ins, outs):
            for n in range(2 * z_count):
                block = pl.ds(pl.multiple_of(maps[n] * cut_rows_x, 16), cut_rows_x)
                at, ref_at = 0, 0
                for parts, wide_ in zip(parts_of, widths, strict=True):
                    refs = ins[ref_at : ref_at + len(parts)]
                    total = sum(ref[block, :].astype(F32) for ref in refs)
                    outs[n // z_count][n % z_count, :, at : at + wide_] = total.astype(BF)
                    at, ref_at = at + wide_, ref_at + len(parts)

        return once(function, [((z_count, cut_rows_x, total_width), BF)] * 2, *flat, maps=xz_maps)

    def core_then_y(left, right, column=None):
        cols = right.shape[1] // 2
        theirs = grad([tie(left)], 0, width, [right], 1 - c_at)
        if column is not None:
            lane = jnp.arange(HD) == 0
            own = jnp.where(c_at == 0, column[0], column[1]).reshape(width, 1)
            other = jnp.where(c_at == 0, column[1], column[0]).reshape(width, 1)
            theirs = jnp.concatenate([theirs, jnp.where(lane, other, 0).astype(BF)], axis=1)
        got = yield [(theirs, "c", 1)]
        got = got[0]
        parts = grad([left], 0, width, [right], c_at, got[:, :cols], [1] * y_count, y_order)
        parts = [part[0] for part in parts]
        if column is not None:
            extra = add(jnp.where(lane, own, 0), got[:, cols:]).reshape(y_count, deep, HD)
            parts = [
                jnp.concatenate([part, pick(extra, y_at ^ r, 0)], axis=1)
                for r, part in enumerate(parts)
            ]
        got = yield [(part, "y", r) for r, part in zip(others, parts[1:], strict=True)]
        return [parts[0]] + got

    def x_then_z(kept, sent):
        got = yield [(sent, "x", 1)]
        sums = add_halves(kept, got[0])
        return (yield from scatter_z(sums[0], sums[1]))

    def chain_t():
        found["t_parts"] = yield from core_then_y(attended, found["d_attn"])

    def chain_q():
        parts = yield from core_then_y(normed, found["d_raw"])
        piece = yield from x_then_z(*cut_x([tie(part) for part in found["t_parts"]], parts))
        yield from spread(piece, finish_attn(("out", "query"), width // 2), split=False)

    def chain_k(d_kv_raw, d_gain):
        parts = yield from core_then_y(normed, d_kv_raw, (d_gain, found["d_gain_mlp"]))
        piece = yield from x_then_z(*cut_x(parts))

        yield from spread(piece, finish_attn(("keyval",), 2 * HD), split=False)

    chains, pending = {}, {}

    def advance(names):
        names = [name for name in names.split() if chains.get(name) is not None]
        waited = [part for name in names for part in pending.get(name, [])]
        if waited:
            waited = list(together(*waited))
            mark(*waited)
        for name in names:
            count = len(pending.get(name, []))
            got, waited = waited[:count], waited[count:]
            try:
                if name in pending:
                    got = list(together(*got)) if got else []
                    sends = chains[name].send(got)
                else:
                    sends = [(tie(part), axis, mask) for part, axis, mask in next(chains[name])]
            except StopIteration:
                chains[name] = None
                continue
            mark(*[part for part, _, _ in sends])
            pending[name] = [shift(*send) for send in sends]

    d_result, out_result = {}, []
    jobs = [
        ffn_chain((normed_t, y_at ^ r, deep, d_both), finish_up(r), r) for r in list(others) + [0]
    ]
    ups = [f"U{r}" for r in others]
    for name, chain in zip(ups + ["W"], jobs, strict=True):
        chains[name] = chain
    first_up = " ".join(ups)
    chains["D"] = ffn_chain((inner_t, 0, units, cots), finish_down, 0)

    def do_back():
        d_cut = back_cut()
        mark(*d_cut)
        chains["a"], chains["b"] = back_a(d_cut, d_result), back_b(d_cut, d_result)

    def do_down():
        out_cut = down_cut()
        mark(*out_cut)
        chains["e"] = back_whole(out_cut[0], out_cut[1:], out_result)

    def hidden_back(_, ins, outs):
        grads = sum_rows(ins, y_count)
        values, scale, upstream, gain = (ref[...] for ref in ins[y_count + 2 :])
        scale = scale[:, :1]
        back = upstream.astype(F32) + norm_back_rows(grads, values, scale, gain)
        outs[0][...] = back
        outs[1][...] = back.astype(BF)
        outs[2][...] = jnp.sum(grads * values * scale, axis=0, keepdims=True)

    def do_hidden():
        found["d_hidden"], found["d_attn"], found["d_gain_mlp"] = once(
            hidden_back,
            [((tok_rows, width), F32), ((tok_rows, width), BF), ((1, width), F32)],
            *[tie(part) for part in d_result["a"] + d_result["b"]],
            hidden,
            factor,
            cotangent,
            gain_two,
        )
        mark(found["d_attn"], found["d_gain_mlp"])
        chains["T"] = chain_t()

    maps = jnp.concatenate([window, entry_block, jnp.stack(o_rows).astype(jnp.int32)])
    entry_spec = pl.BlockSpec((ctx_count // 2, tok_rows, 2 * HD), lambda i, maps: (0, 0, 0))
    entry_shape = jax.ShapeDtypeStruct((ctx_count // 2, tok_rows, 2 * HD), BF)
    small = [cosine, sine]

    def do_attention():
        found["d_raw"], found["d_kept"], found["d_sent"] = kernel_call(
            functools.partial(attend_back_kernel, n_o, spans, ctx_count),
            grid_spec=pltpu.PrefetchScalarGridSpec(
                num_scalar_prefetch=1,
                grid=(pairs,),
                in_specs=[token_spec, pair_spec, soft_spec]
                + [whole_spec(a) for a in small]
                + kv_specs
                + [ANY] * n_o,
                out_specs=[pair_spec, entry_spec, entry_spec],
                scratch_shapes=[
                    pltpu.VMEM((H * HD, width), BF),
                    pltpu.VMEM((spans * tok_rows, HD), BF),
                    pltpu.VMEM((spans * tok_rows, HD), BF),
                    pltpu.VMEM((HD, spans * tok_rows), F32),
                    pltpu.VMEM((HD, spans * tok_rows), F32),
                    pltpu.VMEM(((spans + 1) * tok_rows, 2 * HD), BF),
                    pltpu.SemaphoreType.DMA((n_o,)),
                ],
            ),
            out_shape=[jax.ShapeDtypeStruct((tok_rows, H * HD), BF), entry_shape, entry_shape],
        )(maps, tie(found["d_attn"]), queries, softs, *small, *([all_kv] * spans), *o_pieces)
        mark(found["d_sent"])
        chains["Q"] = chain_q()
        chains["v"] = kv_back(kv_result)

    def kv_back(result):
        got = yield [(found["d_sent"], "c", 1)]

        def first(_, ins, outs):
            for n in range(2 * z_count):
                outs[n % 2][n // 2] = (ins[0][n].astype(F32) + ins[1][n].astype(F32)).astype(BF)

        shape = ((z_count, tok_rows, 2 * HD), BF)
        kept, sent = once(first, [shape, shape], found["d_kept"], got[0])
        got = yield [(sent, "x", 1)]

        def second(_, ins, outs):
            for n in range(z_count):
                outs[n][...] = (ins[0][n].astype(F32) + ins[1][n].astype(F32)).astype(BF)

        left = once(second, [((tok_rows, 2 * HD), BF)] * z_count, kept, got[0])
        got = yield [(left[d], "z", d) for d in range(1, z_count)]
        result += [left[0]] + got

    kv_result = []

    def tokens_kernel(maps, *refs):
        n_kv = y_count
        d_raw, cosine_ref, sine_ref, tokens_ref, gain, back_hidden = refs[:6]
        parts = refs[6 : 6 + z_count]
        kv_pieces = refs[6 + z_count : 6 + z_count + n_kv]
        pieces = refs[6 + z_count + n_kv : 6 + z_count + n_kv + n_q]
        outs = refs[6 + z_count + n_kv + n_q :]
        d_kv, back, d_gain, whole_q, whole_kv, q_sem, kv_sem = outs
        copies = load_rows(whole_q, pieces, [maps[n] for n in range(n_q)], q_sem)
        copies += load_rows(whole_kv, kv_pieces, [maps[n_q + n] for n in range(n_kv)], kv_sem)
        total = sum(ref[...].astype(F32) for ref in parts)
        d_kv[:, :HD] = rotate(total[:, :HD], cosine_ref[...], -sine_ref[...]).astype(BF)
        d_kv[:, HD:] = total[:, HD:].astype(BF)
        inputs = tokens_ref[...].astype(F32)
        scale = rms_factor(inputs)
        for copy in copies:
            copy.wait()
        grads = dot_t(d_raw[...], whole_q[...]) + dot_t(d_kv[...], whole_kv[...])
        back[...] = back_hidden[...] + norm_back_rows(grads, inputs, scale, gain[...])
        d_gain[...] = jnp.sum(grads * inputs * scale, axis=0, keepdims=True)

    q_maps = jnp.concatenate([jnp.stack(q_rows).astype(jnp.int32), kv_rows])
    def do_tokens():
        d_kv_raw, found["tokens"], d_gain = kernel_call(
            tokens_kernel,
            in_specs=[pl.BlockSpec(memory_space=pltpu.SMEM)]
            + [in_vmem] * (6 + z_count)
            + [ANY] * (y_count + n_q),
            out_specs=[in_vmem] * 3,
            out_shape=[
                jax.ShapeDtypeStruct((tok_rows, 2 * HD), BF),
                jax.ShapeDtypeStruct((tok_rows, width), F32),
                jax.ShapeDtypeStruct((1, width), F32),
            ],
            scratch_shapes=[
                pltpu.VMEM((width, H * HD), BF),
                pltpu.VMEM((width, 2 * HD), BF),
                pltpu.SemaphoreType.DMA((n_q,)),
                pltpu.SemaphoreType.DMA((y_count,)),
            ],
        )(
            q_maps,
            found["d_raw"],
            cosine,
            sine,
            tokens,
            gain_one,
            found["d_hidden"],
            *[tie(part) for part in kv_result],
            *kv_weights,
            *q_pieces,
        )
        mark(d_kv_raw, d_gain, found["tokens"])
        chains["K"] = chain_k(d_kv_raw, d_gain)

    works = {
        "back": do_back,
        "down": do_down,
        "hid": do_hidden,
        "att": do_attention,
        "tok": do_tokens,
    }
    for entry in PLAN:
        if entry in works:
            works[entry]()
        else:
            advance(" ".join(first_up if letter == "O" else letter for letter in entry))
    while any(chain is not None for chain in chains.values()):
        advance(" ".join(chains))

    def finish_output(_, ins, outs):
        outs[0][...] = (ins[-1][...] + sum(ref[...].astype(F32) for ref in ins[:-1])).astype(BF)

    block_output = once(finish_output, [((tok_rows, width), BF)], *out_result, hidden)[0]
    last = found["keyval"]
    grad_keyval = jnp.concatenate([last[:, :HD], last[:, 2 * HD : 3 * HD]], axis=1)
    return (
        block_output,
        found["tokens"],
        last[:, HD],
        found["query"],
        grad_keyval,
        found["out"],
        last[:, 3 * HD],
        found["up"],
        found["down"],
    )


def solution(mesh):
    ctx_count, y_count = mesh.shape["ctx"], mesh.shape["fsdp"]
    fine = Mesh(mesh.devices.reshape(ctx_count // 4, 2, 2, y_count), ("z", "x", "c", "y"))
    rows, shard = P(("z", "x", "c", "y"), None), P("y", None)
    in_specs = (rows, rows, shard, shard, P("y"), shard, shard, shard, P("y"), shard, shard)
    out_specs = (rows, rows, P("y"), shard, shard, shard, P("y"), shard, shard)
    return jax.shard_map(body, mesh=fine, in_specs=in_specs, out_specs=out_specs, check_vma=False)
```
